128 devices in a mesh: aa: 16 (over x_hi, z, core), ba: 8 (over y, x_lo).
Axes of the slice: x: 4 (x_hi: 2, x_lo: 2; x = x_hi * 2 + x_lo), y: 4, z: 4, core: 2. Of those that a mesh axis runs over, the one named last changes fastest.
Arguments:
- field: bfloat16 [1024, 1024, 1024], P(None, 'aa', 'ba'), may hold values from -8 to 8
- mode_one: bfloat16 [1024, 256], replicated, may hold values from -0.1875 to 0.1875
- mode_two: bfloat16 [1024, 256], P('aa'), may hold values from -0.1875 to 0.1875
Outputs:
- gram: float32 [1024, 1024], P('ba')
The draws below stay inside these ranges and needn't reach their ends.
All inputs are finite; a program needn't handle non-finite values.
Results may differ from the reference program's by a relative error of at most 0.00077.
Values may be sent and summed in bfloat16 or wider, within the bound.
A program may use at most 192 MiB of HBM per device.

```python
import jax
import jax.numpy as jnp
from jax import lax

I1 = 1024
RANK = 256
K_DEV = 128
I2 = 1024
I3 = 1024


def draw_field(key, part):
    key = jax.random.fold_in(key, 1)
    first_key, second_key, third_key, fourth_key = jax.random.split(key, 4)
    noise = jax.random.normal(first_key, (I1, I2, I3), jnp.float32)
    spread = jax.random.uniform(fourth_key, (I3,), jnp.float32, 0.5, 1.5)
    base = jax.random.normal(second_key, (I1, I2), jnp.float32)
    mixing = jax.random.normal(third_key, (I2, I3), jnp.float32)
    values = noise * spread[None, None, :] + 1.5 * base[:, :, None] * mixing[None, :, :]
    return jnp.clip(values, -8.0, 8.0).astype(jnp.bfloat16)


def shard_levels(key, dims, cuts, least, largest):
    gain, own = 1.0, jax.random.fold_in(key, 6)
    for axis_at, shards_of in cuts:
        steps = jnp.exp(jax.random.uniform(jax.random.fold_in(own, axis_at), (shards_of,), jnp.float32, least / len(cuts), largest / len(cuts)))
        gain = gain * jnp.repeat(steps, dims[axis_at] // shards_of).reshape([-1 if axis == axis_at else 1 for axis in range(len(dims))])
    return gain


def centred(stream_key, dims, scale, most, shards=(), held_as=jnp.bfloat16):
    array = scale * jax.random.normal(stream_key, dims, jnp.float32)
    if shards:
        array = array * shard_levels(stream_key, dims, shards, -0.22, 0.18)
    return jnp.clip(array, -most, most).astype(held_as)


def setup_inputs(seed: int = 0) -> dict:
    arg_keys = jax.random.split(jax.random.key(seed), 4)
    field = draw_field(jax.random.fold_in(arg_keys[3], 71), 0)
    mode_one = centred(arg_keys[1], (I1, RANK), I1 ** -0.5, 0.1875)
    mode_two = centred(arg_keys[2], (I2, RANK), I2 ** -0.5, 0.1875, ((0, 16),))
    return dict(field=field, mode_one=mode_one, mode_two=mode_two)


def reference(field, mode_one, mode_two):
    blocks = I3 // K_DEV
    one = mode_one.astype(jnp.float32)
    two = mode_two.astype(jnp.float32)

    def core_block(index):
        start = (index * K_DEV).astype(jnp.int32)
        piece = lax.dynamic_slice_in_dim(field, start, K_DEV, 2).astype(jnp.float32)
        first = jnp.einsum('ijk,ir->kjr', piece, one).astype(jnp.bfloat16)
        return jnp.einsum('kjr,js->skr', first.astype(jnp.float32), two).astype(jnp.bfloat16)

    pieces = lax.map(core_block, jnp.arange(blocks, dtype=jnp.int32))
    core = jnp.transpose(pieces, (1, 0, 2, 3)).reshape(RANK, I3, RANK).astype(jnp.float32)
    gram = jnp.einsum('skr,snr->kn', core, core)
    return gram / (RANK * RANK)
```

```python
import functools

import jax
import jax.numpy as jnp
from jax import lax
from jax.experimental import pallas as pl
from jax.experimental.pallas import tpu as pltpu
from jax.sharding import PartitionSpec as P

BF, F32 = jnp.bfloat16, jnp.float32
MESH = pl.DeviceIdType.MESH
JT = 16
ND = 5


def where_am_i():
    aa, ba = lax.axis_index("aa"), lax.axis_index("ba")
    core, z = lax.rem(aa, 2), lax.rem(lax.div(aa, 2), 4)
    x = 2 * lax.div(aa, 8) + lax.rem(ba, 2)
    y = lax.div(ba, 2)
    return aa, ba, x, y, z, core


def place(x, y, z, core):
    aa = 8 * lax.div(x, 2) + 2 * z + core
    ba = 2 * y + lax.rem(x, 2)
    return aa, ba


def offset(step):
    one, two, three = lax.rem(step, 4), lax.rem(lax.div(step, 4), 4), lax.rem(lax.div(step, 16), 4)
    four = lax.div(step, 64)
    return lax.rem(one + two + three, 4), lax.rem(one + two, 4), one, lax.rem(one + four, 2)


def total_wait(ref, sem):
    pltpu.make_async_copy(ref, ref, sem).wait()


def kernel(
    field, m1, m2, out,
    fbuf, tbuf, obuf, sbuf, rbuf, m1t, m2buf, m2t, cc, gs, gr, acc, fr, tr, pmat,
    fsem, send, recv, m2send, m2recv, csend, crecv, gsend, grecv, osend, frecv, trecv,
):
    aa, ba, x, y, z, core = where_am_i()
    tiles = fbuf.shape[0]

    def load(tile):
        return pltpu.make_async_copy(field.at[:, pl.ds(JT * tile, JT), :], fbuf.at[tile], fsem.at[tile])

    load(0).start()

    def partner(step):
        dx, dy, dz, dc = offset(step)
        return place(lax.rem(x + dx, 4), lax.rem(y + dy, 4), lax.rem(z + dz, 4), lax.rem(core + dc, 2))

    barrier = pltpu.get_barrier_semaphore()

    @pl.loop(1, 128)
    def _(step):
        to_aa, to_ba = partner(step)
        pl.semaphore_signal(barrier, inc=1, device_id={"aa": to_aa, "ba": to_ba}, device_id_type=MESH)

    for tile in range(1, tiles):
        load(tile).start()

    row = lax.broadcasted_iota(jnp.int32, (256, 256), 0)
    col = lax.broadcasted_iota(jnp.int32, (256, 256), 1)
    swap = ((row & 15) * 16 + (row >> 4)) == col
    pmat[...] = jnp.where(swap, 1.0, 0.0).astype(BF)
    m1t[...] = m1[...].T

    def send_rows(first_row, rows):
        def block(to_aa, to_ba):
            mine = sbuf.at[pl.ds(2 * (8 * to_aa + to_ba), 2), pl.ds(first_row, rows), :]
            there = rbuf.at[:, ba, pl.ds(pl.multiple_of(64 * aa + first_row, JT), rows), :]
            return mine, there

        @pl.loop(1, 128)
        def _(step):
            to_aa, to_ba = partner(step)
            mine, there = block(to_aa, to_ba)
            pltpu.make_async_remote_copy(
                mine, there, send, recv, device_id={"aa": to_aa, "ba": to_ba}, device_id_type=MESH
            ).start()

        mine, there = block(aa, ba)
        pltpu.make_async_copy(mine, there, recv).start()

    @pl.loop(0, tiles)
    def _(tile):
        load(tile).wait()

        @pl.loop(0, 32, unroll=4)
        def _(group):
            at = 32 * group
            left = fbuf[tile, pl.ds(at, 16)].reshape(256, 128)
            right = fbuf[tile, pl.ds(at + 16, 16)].reshape(256, 128)
            both = jnp.concatenate([left, right], axis=1)
            turned = jnp.dot(pmat[...], both, preferred_element_type=F32).astype(BF)
            here = pl.multiple_of(at, 32)
            tbuf[:, pl.ds(here, 16), :] = turned[:, :128].reshape(16, 16, 128)
            tbuf[:, pl.ds(pl.multiple_of(here + 16, 16), 16), :] = turned[:, 128:].reshape(16, 16, 128)

        @pl.loop(0, JT // 2)
        def _(pair):
            both = jnp.concatenate([tbuf[2 * pair], tbuf[2 * pair + 1]], axis=1)
            got = jnp.dot(m1t[...], both, preferred_element_type=F32).astype(BF)
            obuf[2 * pair] = got[:, :128]
            obuf[2 * pair + 1] = got[:, 128:]

        @pl.loop(0, 8, unroll=2)
        def _(group):
            at = pl.multiple_of(32 * group, 32)
            left = obuf[:, pl.ds(at, 16), :].reshape(256, 128)
            right = obuf[:, pl.ds(pl.multiple_of(at + 16, 16), 16), :].reshape(256, 128)
            both = jnp.concatenate([left, right], axis=1)
            turned = jnp.dot(pmat[...], both, preferred_element_type=F32).astype(BF)
            rows = pl.ds(pl.multiple_of(JT * tile, JT), JT)
            sbuf[pl.ds(at, 16), rows, :] = turned[:, :128].reshape(16, 16, 128)
            sbuf[pl.ds(at + 16, 16), rows, :] = turned[:, 128:].reshape(16, 16, 128)

        @pl.when(tile == 0)
        def _():
            pl.semaphore_wait(barrier, 127)
            mine = m2buf.at[pl.ds(pl.multiple_of(64 * aa, 64), 64), :]

            @pl.loop(1, 16)
            def _(step):
                pltpu.make_async_remote_copy(
                    m2, mine, m2send, m2recv,
                    device_id={"aa": lax.rem(aa + step, 16), "ba": ba}, device_id_type=MESH,
                ).start()

            pltpu.make_async_copy(m2, mine, m2recv).start()

        @pl.when(tile < 2)
        def _():
            send_rows(pl.multiple_of(JT * tile, JT), JT)

        @pl.when(tile == 3)
        def _():
            send_rows(2 * JT, 2 * JT)

    total_wait(m2buf, m2recv)
    total_wait(m2buf.at[pl.ds(0, 960), :], m2send)
    m2t[...] = m2buf[...].T
    total_wait(rbuf, recv)

    def share(half):
        return pltpu.make_async_remote_copy(
            cc.at[:, pl.ds(256 * half, 256), :], cc.at[:, pl.ds(512 + 256 * half, 256), :],
            csend.at[half], crecv.at[half],
            device_id={"aa": aa + 1 - 2 * core, "ba": ba}, device_id_type=MESH,
        )

    for half in range(2):
        @pl.loop(0, 4)
        def _(pair):
            both = jnp.concatenate([rbuf[half, 2 * pair], rbuf[half, 2 * pair + 1]], axis=1)
            got = jnp.dot(m2t[...], both, preferred_element_type=F32).astype(BF)
            cc[2 * pair, pl.ds(256 * half, 256), :] = got[:, :128]
            cc[2 * pair + 1, pl.ds(256 * half, 256), :] = got[:, 128:]

        share(half).start()
    for half in range(2):
        share(half).wait()

    chip = 16 * x + 4 * y + z

    @pl.loop(0, 4)
    def _(local):
        block_row = 4 * core + local
        right = jnp.concatenate([cc[lax.rem(block_row + d, 8)] for d in range(ND)], axis=1)
        got = lax.dot_general(cc[block_row], right, (((0,), (0,)), ((), ())), preferred_element_type=F32)
        for d in range(ND):
            gs[local, d] = got[:, 128 * d : 128 * d + 128]

        @pl.loop(0, 16)
        def _(step):
            to_aa = lax.rem(aa + step, 16)
            mine = gs.at[local, :, pl.ds(pl.multiple_of(8 * to_aa, 8), 8), :]
            self = jnp.logical_and(block_row == ba, step == 0)

            @pl.when(self)
            def _():
                pltpu.make_async_copy(mine, gr.at[chip], grecv).start()

            @pl.when(jnp.logical_not(self))
            def _():
                pltpu.make_async_remote_copy(
                    mine, gr.at[chip], gsend, grecv,
                    device_id={"aa": to_aa, "ba": block_row}, device_id_type=MESH,
                ).start()

    total_wait(gr, grecv)
    got = jnp.sum(gr[...], axis=0) * (1.0 / 65536.0)
    acc[...] = got
    own = pl.ds(pl.multiple_of(8 * aa, 8), 8)
    fr[:, own, :] = got

    @pl.loop(1, 16)
    def _(step):
        pltpu.make_async_remote_copy(
            acc, fr.at[:, own, :], osend, frecv,
            device_id={"aa": lax.rem(aa + step, 16), "ba": ba}, device_id_type=MESH,
        ).start()

    for d in range(1, 4):
        @pl.loop(0, 16)
        def _(step):
            pltpu.make_async_remote_copy(
                acc.at[d], tr.at[d - 1, own, :], osend, trecv,
                device_id={"aa": lax.rem(aa + step, 16), "ba": lax.rem(ba + d, 8)}, device_id_type=MESH,
            ).start()

    total_wait(fr.at[:, pl.ds(0, 120), :], frecv)
    for d in range(ND):
        out[:, pl.ds(pl.multiple_of(128 * lax.rem(ba + d, 8), 128), 128)] = fr[d]
    total_wait(tr, trecv)
    for d in range(1, 4):
        out[:, pl.ds(pl.multiple_of(128 * lax.rem(ba + 8 - d, 8), 128), 128)] = tr[d - 1].T

    total_wait(sbuf.at[pl.ds(0, 254)], send)
    inside = lax.div(ba, 4) == core

    @pl.when(inside)
    def _():
        total_wait(gr.at[pl.ds(0, 63)], gsend)

    @pl.when(jnp.logical_not(inside))
    def _():
        total_wait(gr, gsend)

    total_wait(fr.at[:, pl.ds(0, 120), :], osend)
    total_wait(tr, osend)


def shards(field, mode_one, mode_two):
    dma = pltpu.SemaphoreType.DMA
    return pl.pallas_call(
        kernel,
        out_shape=jax.ShapeDtypeStruct((128, 1024), F32),
        in_specs=[
            pl.BlockSpec(memory_space=pl.ANY),
            pl.BlockSpec(memory_space=pltpu.VMEM),
            pl.BlockSpec(memory_space=pltpu.VMEM),
        ],
        out_specs=pl.BlockSpec(memory_space=pltpu.VMEM),
        scratch_shapes=[
            pltpu.VMEM((4, 1024, JT, 128), BF),
            pltpu.VMEM((JT, 1024, 128), BF),
            pltpu.VMEM((JT, 256, 128), BF),
            pltpu.VMEM((256, 64, 128), BF),
            pltpu.VMEM((2, 8, 1024, 128), BF),
            pltpu.VMEM((256, 1024), BF),
            pltpu.VMEM((1024, 256), BF),
            pltpu.VMEM((256, 1024), BF),
            pltpu.VMEM((8, 1024, 128), BF),
            pltpu.VMEM((4, ND, 128, 128), F32),
            pltpu.VMEM((64, ND, 8, 128), F32),
            pltpu.VMEM((ND, 8, 128), F32),
            pltpu.VMEM((ND, 128, 128), F32),
            pltpu.VMEM((3, 128, 128), F32),
            pltpu.VMEM((256, 256), BF),
            dma((4,)),
            dma, dma, dma, dma,
            dma((2,)), dma((2,)),
            dma, dma, dma, dma, dma,
        ],
        compiler_params=pltpu.CompilerParams(
            collective_id=0, has_side_effects=True, vmem_limit_bytes=56 * 1024 * 1024
        ),
        cost_estimate=pl.CostEstimate(flops=13_000_000_000, bytes_accessed=18_000_000, transcendentals=0),
    )(field, mode_one, mode_two)


def solution(mesh):
    in_specs = (P(None, "aa", "ba"), P(), P("aa", None))
    return jax.shard_map(shards, mesh=mesh, in_specs=in_specs, out_specs=P("ba", None), check_vma=False)
```

```python
import functools

import jax
import jax.numpy as jnp
from jax import lax
from jax.experimental import pallas as pl
from jax.experimental.pallas import tpu as pltpu
from jax.sharding import PartitionSpec as P

BF, F32 = jnp.bfloat16, jnp.float32
MESH = pl.DeviceIdType.MESH
JT = 16
ND = 5


def where_am_i():
    aa, ba = lax.axis_index("aa"), lax.axis_index("ba")
    core, z = lax.rem(aa, 2), lax.rem(lax.div(aa, 2), 4)
    x = 2 * lax.div(aa, 8) + lax.rem(ba, 2)
    y = lax.div(ba, 2)
    return aa, ba, x, y, z, core


def place(x, y, z, core):
    aa = 8 * lax.div(x, 2) + 2 * z + core
    ba = 2 * y + lax.rem(x, 2)
    return aa, ba


def offset(step):
    one, two, three = lax.rem(step, 4), lax.rem(lax.div(step, 4), 4), lax.rem(lax.div(step, 16), 4)
    four = lax.div(step, 64)
    return lax.rem(one + two + three, 4), lax.rem(one + two, 4), one, lax.rem(one + four, 2)


def total_wait(ref, sem):
    pltpu.make_async_copy(ref, ref, sem).wait()


def kernel(
    field, m1, m2, out,
    fbuf, tbuf, obuf, sbuf, rbuf, m1t, m2buf, m2t, cc, gs, gr, acc, fr, tr, pmat,
    fsem, send, recv, m2send, m2recv, csend, crecv, gsend, grecv, osend, frecv, trecv,
):
    aa, ba, x, y, z, core = where_am_i()
    tiles = fbuf.shape[0]

    def load(tile):
        return pltpu.make_async_copy(field.at[:, pl.ds(JT * tile, JT), :], fbuf.at[tile], fsem.at[tile])

    load(0).start()

    def partner(step):
        dx, dy, dz, dc = offset(step)
        return place(lax.rem(x + dx, 4), lax.rem(y + dy, 4), lax.rem(z + dz, 4), lax.rem(core + dc, 2))

    barrier = pltpu.get_barrier_semaphore()

    @pl.loop(1, 128)
    def _(step):
        to_aa, to_ba = partner(step)
        pl.semaphore_signal(barrier, inc=1, device_id={"aa": to_aa, "ba": to_ba}, device_id_type=MESH)

    for tile in range(1, tiles):
        load(tile).start()

    row = lax.broadcasted_iota(jnp.int32, (256, 256), 0)
    col = lax.broadcasted_iota(jnp.int32, (256, 256), 1)
    swap = ((row & 15) * 16 + (row >> 4)) == col
    pmat[...] = jnp.where(swap, 1.0, 0.0).astype(BF)
    m1t[...] = m1[...].T

    def send_rows(first_row, rows):
        def block(to_aa, to_ba):
            mine = sbuf.at[pl.ds(2 * (8 * to_aa + to_ba), 2), pl.ds(first_row, rows), :]
            there = rbuf.at[:, ba, pl.ds(pl.multiple_of(64 * aa + first_row, JT), rows), :]
            return mine, there

        @pl.loop(1, 128)
        def _(step):
            to_aa, to_ba = partner(step)
            mine, there = block(to_aa, to_ba)
            pltpu.make_async_remote_copy(
                mine, there, send, recv, device_id={"aa": to_aa, "ba": to_ba}, device_id_type=MESH
            ).start()

        mine, there = block(aa, ba)
        pltpu.make_async_copy(mine, there, recv).start()

    @pl.loop(0, tiles)
    def _(tile):
        load(tile).wait()

        @pl.loop(0, 32, unroll=4)
        def _(group):
            at = 32 * group
            left = fbuf[tile, pl.ds(at, 16)].reshape(256, 128)
            right = fbuf[tile, pl.ds(at + 16, 16)].reshape(256, 128)
            both = jnp.concatenate([left, right], axis=1)
            turned = jnp.dot(pmat[...], both, preferred_element_type=F32).astype(BF)
            here = pl.multiple_of(at, 32)
            tbuf[:, pl.ds(here, 16), :] = turned[:, :128].reshape(16, 16, 128)
            tbuf[:, pl.ds(pl.multiple_of(here + 16, 16), 16), :] = turned[:, 128:].reshape(16, 16, 128)

        @pl.loop(0, JT // 2)
        def _(pair):
            both = jnp.concatenate([tbuf[2 * pair], tbuf[2 * pair + 1]], axis=1)
            got = jnp.dot(m1t[...], both, preferred_element_type=F32).astype(BF)
            obuf[2 * pair] = got[:, :128]
            obuf[2 * pair + 1] = got[:, 128:]

        @pl.loop(0, 8, unroll=2)
        def _(group):
            at = pl.multiple_of(32 * group, 32)
            left = obuf[:, pl.ds(at, 16), :].reshape(256, 128)
            right = obuf[:, pl.ds(pl.multiple_of(at + 16, 16), 16), :].reshape(256, 128)
            both = jnp.concatenate([left, right], axis=1)
            turned = jnp.dot(pmat[...], both, preferred_element_type=F32).astype(BF)
            rows = pl.ds(pl.multiple_of(JT * tile, JT), JT)
            sbuf[pl.ds(at, 16), rows, :] = turned[:, :128].reshape(16, 16, 128)
            sbuf[pl.ds(at + 16, 16), rows, :] = turned[:, 128:].reshape(16, 16, 128)

        @pl.when(tile == 0)
        def _():
            pl.semaphore_wait(barrier, 127)
            mine = m2buf.at[pl.ds(pl.multiple_of(64 * aa, 64), 64), :]

            @pl.loop(1, 16)
            def _(step):
                pltpu.make_async_remote_copy(
                    m2, mine, m2send, m2recv,
                    device_id={"aa": lax.rem(aa + step, 16), "ba": ba}, device_id_type=MESH,
                ).start()

            pltpu.make_async_copy(m2, mine, m2recv).start()

        send_rows(pl.multiple_of(JT * tile, JT), JT)

    total_wait(m2buf, m2recv)
    total_wait(m2buf.at[pl.ds(0, 960), :], m2send)
    m2t[...] = m2buf[...].T
    total_wait(rbuf, recv)

    def share(half):
        return pltpu.make_async_remote_copy(
            cc.at[:, pl.ds(256 * half, 256), :], cc.at[:, pl.ds(512 + 256 * half, 256), :],
            csend.at[half], crecv.at[half],
            device_id={"aa": aa + 1 - 2 * core, "ba": ba}, device_id_type=MESH,
        )

    for half in range(2):
        @pl.loop(0, 4)
        def _(pair):
            both = jnp.concatenate([rbuf[half, 2 * pair], rbuf[half, 2 * pair + 1]], axis=1)
            got = jnp.dot(m2t[...], both, preferred_element_type=F32).astype(BF)
            cc[2 * pair, pl.ds(256 * half, 256), :] = got[:, :128]
            cc[2 * pair + 1, pl.ds(256 * half, 256), :] = got[:, 128:]

        share(half).start()
    for half in range(2):
        share(half).wait()

    chip = 16 * x + 4 * y + z

    @pl.loop(0, 4)
    def _(local):
        block_row = 4 * core + local
        right = jnp.concatenate([cc[lax.rem(block_row + d, 8)] for d in range(ND)], axis=1)
        got = lax.dot_general(cc[block_row], right, (((0,), (0,)), ((), ())), preferred_element_type=F32)
        for d in range(ND):
            gs[local, d] = got[:, 128 * d : 128 * d + 128]

        @pl.loop(0, 16)
        def _(step):
            to_aa = lax.rem(aa + step, 16)
            mine = gs.at[local, :, pl.ds(pl.multiple_of(8 * to_aa, 8), 8), :]
            self = jnp.logical_and(block_row == ba, step == 0)

            @pl.when(self)
            def _():
                pltpu.make_async_copy(mine, gr.at[chip], grecv).start()

            @pl.when(jnp.logical_not(self))
            def _():
                pltpu.make_async_remote_copy(
                    mine, gr.at[chip], gsend, grecv,
                    device_id={"aa": to_aa, "ba": block_row}, device_id_type=MESH,
                ).start()

    total_wait(gr, grecv)
    got = jnp.sum(gr[...], axis=0) * (1.0 / 65536.0)
    acc[...] = got
    own = pl.ds(pl.multiple_of(8 * aa, 8), 8)
    fr[:, own, :] = got

    @pl.loop(1, 16)
    def _(step):
        pltpu.make_async_remote_copy(
            acc, fr.at[:, own, :], osend, frecv,
            device_id={"aa": lax.rem(aa + step, 16), "ba": ba}, device_id_type=MESH,
        ).start()

    for d in range(1, 4):
        @pl.loop(0, 16)
        def _(step):
            pltpu.make_async_remote_copy(
                acc.at[d], tr.at[d - 1, own, :], osend, trecv,
                device_id={"aa": lax.rem(aa + step, 16), "ba": lax.rem(ba + d, 8)}, device_id_type=MESH,
            ).start()

    total_wait(fr.at[:, pl.ds(0, 120), :], frecv)
    for d in range(ND):
        out[:, pl.ds(pl.multiple_of(128 * lax.rem(ba + d, 8), 128), 128)] = fr[d]
    total_wait(tr, trecv)
    for d in range(1, 4):
        out[:, pl.ds(pl.multiple_of(128 * lax.rem(ba + 8 - d, 8), 128), 128)] = tr[d - 1].T

    total_wait(sbuf.at[pl.ds(0, 254)], send)
    inside = lax.div(ba, 4) == core

    @pl.when(inside)
    def _():
        total_wait(gr.at[pl.ds(0, 63)], gsend)

    @pl.when(jnp.logical_not(inside))
    def _():
        total_wait(gr, gsend)

    total_wait(fr.at[:, pl.ds(0, 120), :], osend)
    total_wait(tr, osend)


def shards(field, mode_one, mode_two):
    dma = pltpu.SemaphoreType.DMA
    return pl.pallas_call(
        kernel,
        out_shape=jax.ShapeDtypeStruct((128, 1024), F32),
        in_specs=[
            pl.BlockSpec(memory_space=pl.ANY),
            pl.BlockSpec(memory_space=pltpu.VMEM),
            pl.BlockSpec(memory_space=pltpu.VMEM),
        ],
        out_specs=pl.BlockSpec(memory_space=pltpu.VMEM),
        scratch_shapes=[
            pltpu.VMEM((4, 1024, JT, 128), BF),
            pltpu.VMEM((JT, 1024, 128), BF),
            pltpu.VMEM((JT, 256, 128), BF),
            pltpu.VMEM((256, 64, 128), BF),
            pltpu.VMEM((2, 8, 1024, 128), BF),
            pltpu.VMEM((256, 1024), BF),
            pltpu.VMEM((1024, 256), BF),
            pltpu.VMEM((256, 1024), BF),
            pltpu.VMEM((8, 1024, 128), BF),
            pltpu.VMEM((4, ND, 128, 128), F32),
            pltpu.VMEM((64, ND, 8, 128), F32),
            pltpu.VMEM((ND, 8, 128), F32),
            pltpu.VMEM((ND, 128, 128), F32),
            pltpu.VMEM((3, 128, 128), F32),
            pltpu.VMEM((256, 256), BF),
            dma((4,)),
            dma, dma, dma, dma,
            dma((2,)), dma((2,)),
            dma, dma, dma, dma, dma,
        ],
        compiler_params=pltpu.CompilerParams(
            collective_id=0, has_side_effects=True, vmem_limit_bytes=56 * 1024 * 1024
        ),
        cost_estimate=pl.CostEstimate(flops=13_000_000_000, bytes_accessed=18_000_000, transcendentals=0),
    )(field, mode_one, mode_two)


def solution(mesh):
    in_specs = (P(None, "aa", "ba"), P(), P("aa", None))
    return jax.shard_map(shards, mesh=mesh, in_specs=in_specs, out_specs=P("ba", None), check_vma=False)
```

```python
import functools

import jax
import jax.numpy as jnp
from jax import lax
from jax.experimental import pallas as pl
from jax.experimental.pallas import tpu as pltpu
from jax.sharding import PartitionSpec as P

BF, F32 = jnp.bfloat16, jnp.float32
MESH = pl.DeviceIdType.MESH
JT = 16
ND = 5


def where_am_i():
    aa, ba = lax.axis_index("aa"), lax.axis_index("ba")
    core, z = lax.rem(aa, 2), lax.rem(lax.div(aa, 2), 4)
    x = 2 * lax.div(aa, 8) + lax.rem(ba, 2)
    y = lax.div(ba, 2)
    return aa, ba, x, y, z, core


def place(x, y, z, core):
    aa = 8 * lax.div(x, 2) + 2 * z + core
    ba = 2 * y + lax.rem(x, 2)
    return aa, ba


def offset(step):
    one, two, three = lax.rem(step, 4), lax.rem(lax.div(step, 4), 4), lax.rem(lax.div(step, 16), 4)
    four = lax.div(step, 64)
    return lax.rem(one + two + three, 4), lax.rem(one + two, 4), one, lax.rem(one + four, 2)


DIMS = ((1, 0, 0), (0, 1, 0), (0, 0, 1), (3, 0, 0), (0, 3, 0), (0, 0, 3))
SPLIT = {0: (0, 0), 1: (1, 0), 3: (0, 1), 2: (1, 1)}
JOBS = 16
READY = (0, 2, 3, 5)
GAP = 2
ORDER = (5, 5, 2, 0, 2, 4, 0, 3, 4, 5, 2, 1, 1, 0, 5, 2)


def job(rel, rr, tile):
    return 4 * tile + 2 * rel + rr


def timetable():
    step, free, slots = [0] * JOBS, [READY[n // 4] for n in range(JOBS)], []
    while min(step) < 6:
        now, taken = len(slots), {}
        for n in sorted(range(JOBS), key=lambda n: (step[n], n)):
            dim = (ORDER[n] + step[n]) % 6
            if step[n] < 6 and free[n] <= now and dim not in taken:
                taken[dim] = n
        slots.append([(n, step[n]) for n in sorted(taken.values())])
        for n in taken.values():
            step[n] += 1
            free[n] = now + GAP
    return slots


def landed(n, mask):
    flips = set()
    for axis in range(3):
        for half in range(2):
            if SPLIT[mask[axis]][half]:
                flips.add((axis + 3 * half - ORDER[n]) % 6)
    if not flips:
        return -1, 0
    last = max(flips)
    return last, sum(1 << u for u in flips if u != last)


def total_wait(ref, sem):
    pltpu.make_async_copy(ref, ref, sem).wait()


def kernel(
    field, m1, m2, out,
    fbuf, tbuf, obuf, sbuf, orig, rb0, rb1, rb2, rb3, rb4, rb5, staging,
    m1t, m2buf, m2t, cc, gs, gr, acc, fr, tr, pmat,
    fsem, send, recv, ssend, srecv, m2send, m2recv, m2sem, csend, crecv, gsend, grecv, osend, frecv, trecv,
):
    aa, ba, x, y, z, core = where_am_i()
    rbs = (rb0, rb1, rb2, rb3, rb4, rb5)
    sibling = {"aa": aa + 1 - 2 * core, "ba": ba}

    def load(tile):
        return pltpu.make_async_copy(field.at[:, pl.ds(JT * tile, JT), :], fbuf.at[tile], fsem.at[tile])

    load(0).start()

    def partner(step):
        dx, dy, dz, dc = offset(step)
        return place(lax.rem(x + dx, 4), lax.rem(y + dy, 4), lax.rem(z + dz, 4), lax.rem(core + dc, 2))

    barrier = pltpu.get_barrier_semaphore()

    @pl.loop(1, 128)
    def _(step):
        to_aa, to_ba = partner(step)
        pl.semaphore_signal(barrier, inc=1, device_id={"aa": to_aa, "ba": to_ba}, device_id_type=MESH)

    for tile in range(1, 4):
        load(tile).start()

    row = lax.broadcasted_iota(jnp.int32, (256, 256), 0)
    col = lax.broadcasted_iota(jnp.int32, (256, 256), 1)
    swap = ((row & 15) * 16 + (row >> 4)) == col
    pmat[...] = jnp.where(swap, 1.0, 0.0).astype(BF)
    m1t[...] = m1[...].T

    neighbours = []
    for mx, my, mz in DIMS:
        to_aa, to_ba = place(x ^ mx, y ^ my, z ^ mz, core)
        neighbours.append({"aa": to_aa, "ba": to_ba})

    def turn_input(tile, first, last):
        @pl.loop(first, last, unroll=4)
        def _(group):
            at = 32 * group
            left = fbuf[tile, pl.ds(at, 16)].reshape(256, 128)
            right = fbuf[tile, pl.ds(at + 16, 16)].reshape(256, 128)
            both = jnp.concatenate([left, right], axis=1)
            turned = jnp.dot(pmat[...], both, preferred_element_type=F32).astype(BF)
            here = pl.multiple_of(at, 32)
            tbuf[:, pl.ds(here, 16), :] = turned[:, :128].reshape(16, 16, 128)
            tbuf[:, pl.ds(pl.multiple_of(here + 16, 16), 16), :] = turned[:, 128:].reshape(16, 16, 128)

    def contract(tile):
        @pl.loop(0, JT // 2)
        def _(pair):
            both = jnp.concatenate([tbuf[2 * pair], tbuf[2 * pair + 1]], axis=1)
            got = jnp.dot(m1t[...], both, preferred_element_type=F32).astype(BF)
            obuf[2 * pair] = got[:, :128]
            obuf[2 * pair + 1] = got[:, 128:]

        @pl.loop(0, 8, unroll=2)
        def _(group):
            at = pl.multiple_of(32 * group, 32)
            left = obuf[:, pl.ds(at, 16), :].reshape(256, 128)
            right = obuf[:, pl.ds(pl.multiple_of(at + 16, 16), 16), :].reshape(256, 128)
            both = jnp.concatenate([left, right], axis=1)
            turned = jnp.dot(pmat[...], both, preferred_element_type=F32).astype(BF)
            sbuf[pl.ds(at, 16)] = turned[:, :128].reshape(16, 16, 128)
            sbuf[pl.ds(at + 16, 16)] = turned[:, 128:].reshape(16, 16, 128)

        @pl.loop(0, 64, unroll=4)
        def _(slot):
            bits = [(slot >> (5 - d)) & 1 for d in range(6)]
            chip = 16 * (x ^ bits[0] ^ (3 * bits[3])) + 4 * (y ^ bits[1] ^ (3 * bits[4])) + (z ^ bits[2] ^ (3 * bits[5]))

            def at(n):
                turn = ORDER[n]
                return ((slot << turn) | (slot >> (6 - turn))) & 63

            for rr in range(2):
                own = job(0, rr, tile)
                orig[own, at(own)] = sbuf[128 * core + 2 * chip + rr]
                staging[tile, rr, at(job(1, rr, tile))] = sbuf[128 * (1 - core) + 2 * chip + rr]

    def hand_over(tile, rr):
        n = job(1, rr, tile)
        return pltpu.make_async_remote_copy(
            staging.at[tile, rr], orig.at[n], ssend.at[tile, rr], srecv.at[tile, rr],
            device_id=sibling, device_id_type=MESH,
        )

    def exchange(n, step):
        if step == 0:
            if (n // 2) % 2 == 1:
                hand_over(n // 4, n % 2).wait_recv()
        else:
            total_wait(rbs[step - 1].at[n], recv.at[n, step - 1])
        far = pl.ds(2 ** (5 - step), 2 ** (5 - step))
        pieces = [(orig.at[n, far], rbs[step].at[n, 0])]
        for past in range(step):
            pieces.append((rbs[past].at[n, :, far], rbs[step].at[n, pl.ds(2 ** past, 2 ** past)]))
        for mine, there in pieces:
            pltpu.make_async_remote_copy(
                mine, there, send, recv.at[n, step],
                device_id=neighbours[(ORDER[n] + step) % 6], device_id_type=MESH,
            ).start()

    def spread_m2():
        for mask in range(1, 8):
            to_aa, to_ba = place(x ^ (2 * (mask // 4)), y, z ^ (mask % 4), core)
            pltpu.make_async_remote_copy(
                m2, m2buf.at[pl.ds(64 * mask, 64), :], m2send, m2recv,
                device_id={"aa": to_aa, "ba": to_ba}, device_id_type=MESH,
            ).start()
        pltpu.make_async_copy(m2, m2buf.at[pl.ds(0, 64), :], m2recv).start()

    def pass_m2():
        return pltpu.make_async_remote_copy(
            m2buf.at[pl.ds(0, 512), :], m2buf.at[pl.ds(512, 512), :], m2sem.at[0], m2sem.at[1],
            device_id=sibling, device_id_type=MESH,
        )

    slots = timetable()

    def serve(first, last):
        for n, step in [pair for slot in slots[first:last] for pair in slot]:
            exchange(n, step)

    for tile in range(4):
        load(tile).wait()
        turn_input(tile, 0, 32)
        if tile in (1, 3):
            serve(READY[tile] - 1, READY[tile])
        contract(tile)
        if tile == 0:
            pl.semaphore_wait(barrier, 127)
        for rr in range(2):
            hand_over(tile, rr).start()
        if tile < 3:
            serve(READY[tile], READY[tile + 1] - (1 if tile in (0, 2) else 0))
        if tile == 1:
            spread_m2()
    serve(READY[3], 10)
    total_wait(m2buf.at[pl.ds(0, 512), :], m2recv)
    pass_m2().start()
    serve(10, 12)
    pass_m2().wait()
    m2t[...] = m2buf[...].T
    serve(12, len(slots))
    for n in range(JOBS):
        total_wait(rbs[5].at[n], recv.at[n, 5])

    def block(n, mask):
        where, index = landed(n, mask)
        return orig[n, 0] if where < 0 else rbs[where][n, index, 0]

    def points(rr, y_mask, x_mask):
        return jnp.concatenate([
            block(job(rel, rr, tile), (2 * high + x_mask, y_mask, z_mask))
            for rel in range(2) for high in range(2) for z_mask in range(4) for tile in range(4)
        ], axis=0)

    def share(half):
        return pltpu.make_async_remote_copy(
            cc.at[:, pl.ds(256 * half, 256), :], cc.at[:, pl.ds(512 + 256 * half, 256), :],
            csend.at[half], crecv.at[half],
            device_id={"aa": aa + 1 - 2 * core, "ba": ba}, device_id_type=MESH,
        )

    for half in range(2):
        for y_mask in range(4):
            both = jnp.concatenate([points(half, y_mask, 0), points(half, y_mask, 1)], axis=1)
            got = jnp.dot(m2t[...], both, preferred_element_type=F32).astype(BF)
            for x_mask in range(2):
                source = 2 * (y ^ y_mask) + (lax.rem(x, 2) ^ x_mask)
                cc[source, pl.ds(256 * half, 256), :] = got[:, 128 * x_mask : 128 * x_mask + 128]
        share(half).start()
    for half in range(2):
        share(half).wait()

    chip = 16 * x + 4 * y + z

    @pl.loop(0, 4)
    def _(local):
        block_row = 4 * core + local
        right = jnp.concatenate([cc[lax.rem(block_row + d, 8)] for d in range(ND)], axis=1)
        got = lax.dot_general(cc[block_row], right, (((0,), (0,)), ((), ())), preferred_element_type=F32)
        for d in range(ND):
            gs[local, d] = got[:, 128 * d : 128 * d + 128]

        @pl.loop(0, 16)
        def _(step):
            to_aa = lax.rem(aa + step, 16)
            mine = gs.at[local, :, pl.ds(pl.multiple_of(8 * to_aa, 8), 8), :]
            self = jnp.logical_and(block_row == ba, step == 0)

            @pl.when(self)
            def _():
                pltpu.make_async_copy(mine, gr.at[chip], grecv).start()

            @pl.when(jnp.logical_not(self))
            def _():
                pltpu.make_async_remote_copy(
                    mine, gr.at[chip], gsend, grecv,
                    device_id={"aa": to_aa, "ba": block_row}, device_id_type=MESH,
                ).start()

    total_wait(gr, grecv)
    got = jnp.sum(gr[...], axis=0) * (1.0 / 65536.0)
    acc[...] = got
    own = pl.ds(pl.multiple_of(8 * aa, 8), 8)
    fr[:, own, :] = got

    @pl.loop(1, 16)
    def _(step):
        pltpu.make_async_remote_copy(
            acc, fr.at[:, own, :], osend, frecv,
            device_id={"aa": lax.rem(aa + step, 16), "ba": ba}, device_id_type=MESH,
        ).start()

    for d in range(1, 4):
        @pl.loop(0, 16)
        def _(step):
            pltpu.make_async_remote_copy(
                acc.at[d], tr.at[d - 1, own, :], osend, trecv,
                device_id={"aa": lax.rem(aa + step, 16), "ba": lax.rem(ba + d, 8)}, device_id_type=MESH,
            ).start()

    total_wait(fr.at[:, pl.ds(0, 120), :], frecv)
    for d in range(ND):
        out[:, pl.ds(pl.multiple_of(128 * lax.rem(ba + d, 8), 128), 128)] = fr[d]
    total_wait(tr, trecv)
    for d in range(1, 4):
        out[:, pl.ds(pl.multiple_of(128 * lax.rem(ba + 8 - d, 8), 128), 128)] = tr[d - 1].T

    for step in range(6):
        total_wait(rbs[step], send)
    for tile in range(4):
        for rr in range(2):
            hand_over(tile, rr).wait_send()
    total_wait(m2buf.at[pl.ds(0, 448), :], m2send)
    inside = lax.div(ba, 4) == core

    @pl.when(inside)
    def _():
        total_wait(gr.at[pl.ds(0, 63)], gsend)

    @pl.when(jnp.logical_not(inside))
    def _():
        total_wait(gr, gsend)

    total_wait(fr.at[:, pl.ds(0, 120), :], osend)
    total_wait(tr, osend)


def shards(field, mode_one, mode_two):
    dma = pltpu.SemaphoreType.DMA
    return pl.pallas_call(
        kernel,
        out_shape=jax.ShapeDtypeStruct((128, 1024), F32),
        in_specs=[
            pl.BlockSpec(memory_space=pl.ANY),
            pl.BlockSpec(memory_space=pltpu.VMEM),
            pl.BlockSpec(memory_space=pltpu.VMEM),
        ],
        out_specs=pl.BlockSpec(memory_space=pltpu.VMEM),
        scratch_shapes=[
            pltpu.VMEM((4, 1024, JT, 128), BF),
            pltpu.VMEM((JT, 1024, 128), BF),
            pltpu.VMEM((JT, 256, 128), BF),
            pltpu.VMEM((256, JT, 128), BF),
            pltpu.VMEM((JOBS, 64, JT, 128), BF),
            *[pltpu.VMEM((JOBS, 2 ** step, 2 ** (5 - step), JT, 128), BF) for step in range(6)],
            pltpu.VMEM((4, 2, 64, JT, 128), BF),
            pltpu.VMEM((256, 1024), BF),
            pltpu.VMEM((1024, 256), BF),
            pltpu.VMEM((256, 1024), BF),
            pltpu.VMEM((8, 1024, 128), BF),
            pltpu.VMEM((4, ND, 128, 128), F32),
            pltpu.VMEM((64, ND, 8, 128), F32),
            pltpu.VMEM((ND, 8, 128), F32),
            pltpu.VMEM((ND, 128, 128), F32),
            pltpu.VMEM((3, 128, 128), F32),
            pltpu.VMEM((256, 256), BF),
            dma((4,)),
            dma, dma((JOBS, 6)), dma((4, 2)), dma((4, 2)),
            dma, dma, dma((2,)),
            dma((2,)), dma((2,)),
            dma, dma, dma, dma, dma,
        ],
        compiler_params=pltpu.CompilerParams(
            collective_id=0, has_side_effects=True, vmem_limit_bytes=56 * 1024 * 1024
        ),
        cost_estimate=pl.CostEstimate(flops=13_000_000_000, bytes_accessed=18_000_000, transcendentals=0),
    )(field, mode_one, mode_two)


def solution(mesh):
    in_specs = (P(None, "aa", "ba"), P(), P("aa", None))
    return jax.shard_map(shards, mesh=mesh, in_specs=in_specs, out_specs=P("ba", None), check_vma=False)
```

```python
import functools

import jax
import jax.numpy as jnp
from jax import lax
from jax.experimental import pallas as pl
from jax.experimental.pallas import tpu as pltpu
from jax.sharding import PartitionSpec as P

BF, F32 = jnp.bfloat16, jnp.float32
MESH = pl.DeviceIdType.MESH
JT = 16
ND = 5


def where_am_i():
    aa, ba = lax.axis_index("aa"), lax.axis_index("ba")
    core, z = lax.rem(aa, 2), lax.rem(lax.div(aa, 2), 4)
    x = 2 * lax.div(aa, 8) + lax.rem(ba, 2)
    y = lax.div(ba, 2)
    return aa, ba, x, y, z, core


def place(x, y, z, core):
    aa = 8 * lax.div(x, 2) + 2 * z + core
    ba = 2 * y + lax.rem(x, 2)
    return aa, ba


def offset(step):
    one, two, three = lax.rem(step, 4), lax.rem(lax.div(step, 4), 4), lax.rem(lax.div(step, 16), 4)
    four = lax.div(step, 64)
    return lax.rem(one + two + three, 4), lax.rem(one + two, 4), one, lax.rem(one + four, 2)


def partner_of(x, y, z, core, step):
    dx, dy, dz, dc = offset(step)
    return place(lax.rem(x + dx, 4), lax.rem(y + dy, 4), lax.rem(z + dz, 4), lax.rem(core + dc, 2))


def greet(x, y, z, core):
    barrier = pltpu.get_barrier_semaphore()

    @pl.loop(1, 128)
    def _(step):
        to_aa, to_ba = partner_of(x, y, z, core, step)
        pl.semaphore_signal(barrier, inc=1, device_id={"aa": to_aa, "ba": to_ba}, device_id_type=MESH)

    return barrier


def total_wait(ref, sem):
    pltpu.make_async_copy(ref, ref, sem).wait()


def core_kernel(
    field, m1, m2, core_out,
    fbuf, tbuf, obuf, sbuf, rbuf, m1t, m2buf, m2t, pmat,
    fsem, send, recv, m2send, m2recv,
):
    aa, ba, x, y, z, core = where_am_i()
    tiles = fbuf.shape[0]

    def load(tile):
        return pltpu.make_async_copy(field.at[:, pl.ds(JT * tile, JT), :], fbuf.at[tile], fsem.at[tile])

    load(0).start()

    def partner(step):
        return partner_of(x, y, z, core, step)

    barrier = greet(x, y, z, core)

    for tile in range(1, tiles):
        load(tile).start()

    row = lax.broadcasted_iota(jnp.int32, (256, 256), 0)
    col = lax.broadcasted_iota(jnp.int32, (256, 256), 1)
    swap = ((row & 15) * 16 + (row >> 4)) == col
    pmat[...] = jnp.where(swap, 1.0, 0.0).astype(BF)
    m1t[...] = m1[...].T

    def send_rows(first_row, rows):
        def block(to_aa, to_ba):
            mine = sbuf.at[pl.ds(2 * (8 * to_aa + to_ba), 2), pl.ds(first_row, rows), :]
            there = rbuf.at[:, ba, pl.ds(pl.multiple_of(64 * aa + first_row, JT), rows), :]
            return mine, there

        @pl.loop(1, 128)
        def _(step):
            to_aa, to_ba = partner(step)
            mine, there = block(to_aa, to_ba)
            pltpu.make_async_remote_copy(
                mine, there, send, recv, device_id={"aa": to_aa, "ba": to_ba}, device_id_type=MESH
            ).start()

        mine, there = block(aa, ba)
        pltpu.make_async_copy(mine, there, recv).start()

    @pl.loop(0, tiles)
    def _(tile):
        load(tile).wait()

        @pl.loop(0, 32, unroll=4)
        def _(group):
            at = 32 * group
            left = fbuf[tile, pl.ds(at, 16)].reshape(256, 128)
            right = fbuf[tile, pl.ds(at + 16, 16)].reshape(256, 128)
            both = jnp.concatenate([left, right], axis=1)
            turned = jnp.dot(pmat[...], both, preferred_element_type=F32).astype(BF)
            here = pl.multiple_of(at, 32)
            tbuf[:, pl.ds(here, 16), :] = turned[:, :128].reshape(16, 16, 128)
            tbuf[:, pl.ds(pl.multiple_of(here + 16, 16), 16), :] = turned[:, 128:].reshape(16, 16, 128)

        @pl.loop(0, JT // 2)
        def _(pair):
            both = jnp.concatenate([tbuf[2 * pair], tbuf[2 * pair + 1]], axis=1)
            got = jnp.dot(m1t[...], both, preferred_element_type=F32).astype(BF)
            obuf[2 * pair] = got[:, :128]
            obuf[2 * pair + 1] = got[:, 128:]

        @pl.loop(0, 8, unroll=2)
        def _(group):
            at = pl.multiple_of(32 * group, 32)
            left = obuf[:, pl.ds(at, 16), :].reshape(256, 128)
            right = obuf[:, pl.ds(pl.multiple_of(at + 16, 16), 16), :].reshape(256, 128)
            both = jnp.concatenate([left, right], axis=1)
            turned = jnp.dot(pmat[...], both, preferred_element_type=F32).astype(BF)
            rows = pl.ds(pl.multiple_of(JT * tile, JT), JT)
            sbuf[pl.ds(at, 16), rows, :] = turned[:, :128].reshape(16, 16, 128)
            sbuf[pl.ds(at + 16, 16), rows, :] = turned[:, 128:].reshape(16, 16, 128)

        @pl.when(tile == 0)
        def _():
            pl.semaphore_wait(barrier, 127)
            mine = m2buf.at[pl.ds(pl.multiple_of(64 * aa, 64), 64), :]

            @pl.loop(1, 16)
            def _(step):
                pltpu.make_async_remote_copy(
                    m2, mine, m2send, m2recv,
                    device_id={"aa": lax.rem(aa + step, 16), "ba": ba}, device_id_type=MESH,
                ).start()

            pltpu.make_async_copy(m2, mine, m2recv).start()

        send_rows(pl.multiple_of(JT * tile, JT), JT)

    total_wait(m2buf, m2recv)
    total_wait(m2buf.at[pl.ds(0, 960), :], m2send)
    m2t[...] = m2buf[...].T
    total_wait(rbuf, recv)

    for half in range(2):
        @pl.loop(0, 4)
        def _(pair):
            both = jnp.concatenate([rbuf[half, 2 * pair], rbuf[half, 2 * pair + 1]], axis=1)
            got = jnp.dot(m2t[...], both, preferred_element_type=F32).astype(BF)
            core_out[2 * pair, pl.ds(256 * half, 256), :] = got[:, :128]
            core_out[2 * pair + 1, pl.ds(256 * half, 256), :] = got[:, 128:]

    total_wait(sbuf.at[pl.ds(0, 254)], send)


def gram_kernel(
    mine, out, cc, gs, gr, acc, fr, tr, csend, crecv, gsend, grecv, osend, frecv, trecv
):
    aa, ba, x, y, z, core = where_am_i()
    barrier = greet(x, y, z, core)
    cc[:, pl.ds(0, 512), :] = mine[...]
    pl.semaphore_wait(barrier, 127)

    def share():
        return pltpu.make_async_remote_copy(
            mine, cc.at[:, pl.ds(512, 512), :], csend, crecv,
            device_id={"aa": aa + 1 - 2 * core, "ba": ba}, device_id_type=MESH,
        )

    share().start()
    share().wait()
    chip = 16 * x + 4 * y + z

    @pl.loop(0, 4)
    def _(local):
        block_row = 4 * core + local
        right = jnp.concatenate([cc[lax.rem(block_row + d, 8)] for d in range(ND)], axis=1)
        got = lax.dot_general(cc[block_row], right, (((0,), (0,)), ((), ())), preferred_element_type=F32)
        for d in range(ND):
            gs[local, d] = got[:, 128 * d : 128 * d + 128]

        @pl.loop(0, 16)
        def _(step):
            to_aa = lax.rem(aa + step, 16)
            piece = gs.at[local, :, pl.ds(pl.multiple_of(8 * to_aa, 8), 8), :]
            self = jnp.logical_and(block_row == ba, step == 0)

            @pl.when(self)
            def _():
                pltpu.make_async_copy(piece, gr.at[chip], grecv).start()

            @pl.when(jnp.logical_not(self))
            def _():
                pltpu.make_async_remote_copy(
                    piece, gr.at[chip], gsend, grecv,
                    device_id={"aa": to_aa, "ba": block_row}, device_id_type=MESH,
                ).start()

    total_wait(gr, grecv)
    got = jnp.sum(gr[...], axis=0) * (1.0 / 65536.0)
    acc[...] = got
    own = pl.ds(pl.multiple_of(8 * aa, 8), 8)
    fr[:, own, :] = got

    @pl.loop(1, 16)
    def _(step):
        pltpu.make_async_remote_copy(
            acc, fr.at[:, own, :], osend, frecv,
            device_id={"aa": lax.rem(aa + step, 16), "ba": ba}, device_id_type=MESH,
        ).start()

    for d in range(1, 4):
        @pl.loop(0, 16)
        def _(step):
            pltpu.make_async_remote_copy(
                acc.at[d], tr.at[d - 1, own, :], osend, trecv,
                device_id={"aa": lax.rem(aa + step, 16), "ba": lax.rem(ba + d, 8)}, device_id_type=MESH,
            ).start()

    total_wait(fr.at[:, pl.ds(0, 120), :], frecv)
    for d in range(ND):
        out[:, pl.ds(pl.multiple_of(128 * lax.rem(ba + d, 8), 128), 128)] = fr[d]
    total_wait(tr, trecv)
    for d in range(1, 4):
        out[:, pl.ds(pl.multiple_of(128 * lax.rem(ba + 8 - d, 8), 128), 128)] = tr[d - 1].T

    inside = lax.div(ba, 4) == core

    @pl.when(inside)
    def _():
        total_wait(gr.at[pl.ds(0, 63)], gsend)

    @pl.when(jnp.logical_not(inside))
    def _():
        total_wait(gr, gsend)

    total_wait(fr.at[:, pl.ds(0, 120), :], osend)
    total_wait(tr, osend)


def shards(field, mode_one, mode_two):
    dma = pltpu.SemaphoreType.DMA
    vmem = pl.BlockSpec(memory_space=pltpu.VMEM)
    core = pl.pallas_call(
        core_kernel,
        out_shape=jax.ShapeDtypeStruct((8, 512, 128), BF),
        in_specs=[pl.BlockSpec(memory_space=pl.ANY), vmem, vmem],
        out_specs=vmem,
        scratch_shapes=[
            pltpu.VMEM((4, 1024, JT, 128), BF),
            pltpu.VMEM((JT, 1024, 128), BF),
            pltpu.VMEM((JT, 256, 128), BF),
            pltpu.VMEM((256, 64, 128), BF),
            pltpu.VMEM((2, 8, 1024, 128), BF),
            pltpu.VMEM((256, 1024), BF),
            pltpu.VMEM((1024, 256), BF),
            pltpu.VMEM((256, 1024), BF),
            pltpu.VMEM((256, 256), BF),
            dma((4,)), dma, dma, dma, dma,
        ],
        compiler_params=pltpu.CompilerParams(
            collective_id=0, has_side_effects=True, vmem_limit_bytes=48 * 1024 * 1024
        ),
        cost_estimate=pl.CostEstimate(flops=12_000_000_000, bytes_accessed=18_000_000, transcendentals=0),
    )(field, mode_one, mode_two)
    return pl.pallas_call(
        gram_kernel,
        out_shape=jax.ShapeDtypeStruct((128, 1024), F32),
        in_specs=[vmem],
        out_specs=vmem,
        scratch_shapes=[
            pltpu.VMEM((8, 1024, 128), BF),
            pltpu.VMEM((4, ND, 128, 128), F32),
            pltpu.VMEM((64, ND, 8, 128), F32),
            pltpu.VMEM((ND, 8, 128), F32),
            pltpu.VMEM((ND, 128, 128), F32),
            pltpu.VMEM((3, 128, 128), F32),
            dma, dma, dma, dma, dma, dma, dma,
        ],
        compiler_params=pltpu.CompilerParams(
            collective_id=1, has_side_effects=True, vmem_limit_bytes=16 * 1024 * 1024
        ),
        cost_estimate=pl.CostEstimate(flops=700_000_000, bytes_accessed=2_000_000, transcendentals=0),
    )(core)


def solution(mesh):
    in_specs = (P(None, "aa", "ba"), P(), P("aa", None))
    return jax.shard_map(shards, mesh=mesh, in_specs=in_specs, out_specs=P("ba", None), check_vma=False)
```

```python
import functools

import jax
import jax.numpy as jnp
from jax import lax
from jax.experimental import pallas as pl
from jax.experimental.pallas import tpu as pltpu
from jax.sharding import PartitionSpec as P

BF, F32 = jnp.bfloat16, jnp.float32
MESH = pl.DeviceIdType.MESH
JT = 16
ND = 5


def where_am_i():
    aa, ba = lax.axis_index("aa"), lax.axis_index("ba")
    core, z = lax.rem(aa, 2), lax.rem(lax.div(aa, 2), 4)
    x = 2 * lax.div(aa, 8) + lax.rem(ba, 2)
    y = lax.div(ba, 2)
    return aa, ba, x, y, z, core


def place(x, y, z, core):
    aa = 8 * lax.div(x, 2) + 2 * z + core
    ba = 2 * y + lax.rem(x, 2)
    return aa, ba


def offset(step):
    one, two, three = lax.rem(step, 4), lax.rem(lax.div(step, 4), 4), lax.rem(lax.div(step, 16), 4)
    four = lax.div(step, 64)
    return lax.rem(one + two + three, 4), lax.rem(one + two, 4), one, lax.rem(one + four, 2)


def total_wait(ref, sem):
    pltpu.make_async_copy(ref, ref, sem).wait()


def kernel(
    field, m1_hbm, m2_hbm, out,
    fbuf, tbuf, obuf, sbuf, rbuf, m1, m1t, m2, m2buf, m2t, cacc, cc, gs, gr, acc, fr, tr, pmat,
    fsem, wsem, send, recv, m2send, m2recv, m2sem, csend, crecv, gsend, grecv, osend, frecv, trecv,
):
    aa, ba, x, y, z, core = where_am_i()
    tiles = fbuf.shape[0]
    sibling = {"aa": aa + 1 - 2 * core, "ba": ba}
    place_in_k = 8 * core + 4 * lax.div(x, 2) + z

    def load(tile):
        return pltpu.make_async_copy(field.at[:, pl.ds(JT * tile, JT), :], fbuf.at[tile], fsem.at[tile])

    load_m1 = pltpu.make_async_copy(m1_hbm, m1, wsem.at[0])
    load_m2 = pltpu.make_async_copy(m2_hbm, m2, wsem.at[1])
    load(0).start()
    load_m1.start()
    load_m2.start()

    def partner(step):
        dx, dy, dz, dc = offset(step)
        return place(lax.rem(x + dx, 4), lax.rem(y + dy, 4), lax.rem(z + dz, 4), lax.rem(core + dc, 2))

    barrier = pltpu.get_barrier_semaphore()

    @pl.loop(1, 128)
    def _(step):
        to_aa, to_ba = partner(step)
        pl.semaphore_signal(barrier, inc=1, device_id={"aa": to_aa, "ba": to_ba}, device_id_type=MESH)

    for tile in range(1, tiles):
        load(tile).start()

    row = lax.broadcasted_iota(jnp.int32, (256, 256), 0)
    col = lax.broadcasted_iota(jnp.int32, (256, 256), 1)
    swap = ((row & 15) * 16 + (row >> 4)) == col
    pmat[...] = jnp.where(swap, 1.0, 0.0).astype(BF)
    load_m1.wait()
    m1t[...] = m1[...].T

    def send_rows(tile):
        def block(to_aa, to_ba):
            mine = sbuf.at[tile, pl.ds(2 * (8 * to_aa + to_ba), 2)]
            there = rbuf.at[tile, :, ba, pl.ds(pl.multiple_of(JT * place_in_k, JT), JT), :]
            return mine, there

        @pl.loop(1, 128)
        def _(step):
            to_aa, to_ba = partner(step)
            mine, there = block(to_aa, to_ba)
            pltpu.make_async_remote_copy(
                mine, there, send, recv.at[tile], device_id={"aa": to_aa, "ba": to_ba}, device_id_type=MESH
            ).start()

        mine, there = block(aa, ba)
        pltpu.make_async_copy(mine, there, recv.at[tile]).start()

    @pl.loop(0, tiles)
    def _(tile):
        load(tile).wait()

        @pl.loop(0, 32, unroll=4)
        def _(group):
            at = 32 * group
            left = fbuf[tile, pl.ds(at, 16)].reshape(256, 128)
            right = fbuf[tile, pl.ds(at + 16, 16)].reshape(256, 128)
            both = jnp.concatenate([left, right], axis=1)
            turned = jnp.dot(pmat[...], both, preferred_element_type=F32).astype(BF)
            here = pl.multiple_of(at, 32)
            tbuf[:, pl.ds(here, 16), :] = turned[:, :128].reshape(16, 16, 128)
            tbuf[:, pl.ds(pl.multiple_of(here + 16, 16), 16), :] = turned[:, 128:].reshape(16, 16, 128)

        @pl.loop(0, JT // 2)
        def _(pair):
            both = jnp.concatenate([tbuf[2 * pair], tbuf[2 * pair + 1]], axis=1)
            got = jnp.dot(m1t[...], both, preferred_element_type=F32).astype(BF)
            obuf[2 * pair] = got[:, :128]
            obuf[2 * pair + 1] = got[:, 128:]

        @pl.loop(0, 8, unroll=2)
        def _(group):
            at = pl.multiple_of(32 * group, 32)
            left = obuf[:, pl.ds(at, 16), :].reshape(256, 128)
            right = obuf[:, pl.ds(pl.multiple_of(at + 16, 16), 16), :].reshape(256, 128)
            both = jnp.concatenate([left, right], axis=1)
            turned = jnp.dot(pmat[...], both, preferred_element_type=F32).astype(BF)
            sbuf[tile, pl.ds(at, 16)] = turned[:, :128].reshape(16, 16, 128)
            sbuf[tile, pl.ds(at + 16, 16)] = turned[:, 128:].reshape(16, 16, 128)

        @pl.when(tile == 0)
        def _():
            pl.semaphore_wait(barrier, 127)

        send_rows(tile)

        @pl.when(tile == 1)
        def _():
            load_m2.wait()
            mine = m2buf.at[:, place_in_k]
            for mask in range(1, 8):
                to_aa, to_ba = place(x ^ (2 * (mask // 4)), y, z ^ (mask % 4), core)
                pltpu.make_async_remote_copy(
                    m2, mine, m2send, m2recv, device_id={"aa": to_aa, "ba": to_ba}, device_id_type=MESH
                ).start()
            pltpu.make_async_copy(m2, mine, m2recv).start()

    half_of_m2 = m2buf.at[:, pl.ds(8 * core, 8)]
    total_wait(half_of_m2, m2recv)
    pass_m2 = pltpu.make_async_remote_copy(
        half_of_m2, half_of_m2, m2sem.at[0], m2sem.at[1], device_id=sibling, device_id_type=MESH
    )
    pass_m2.start()
    pass_m2.wait()
    for tile in range(4):
        m2t[tile] = m2buf[tile].reshape(256, 256).T

    def share(half):
        return pltpu.make_async_remote_copy(
            cc.at[:, pl.ds(256 * half, 256), :], cc.at[:, pl.ds(512 + 256 * half, 256), :],
            csend.at[half], crecv.at[half], device_id=sibling, device_id_type=MESH,
        )

    for tile in range(4):
        total_wait(rbuf.at[tile], recv.at[tile])
        for half in range(2):
            @pl.loop(0, 4, unroll=2)
            def _(pair):
                both = jnp.concatenate([rbuf[tile, half, 2 * pair], rbuf[tile, half, 2 * pair + 1]], axis=1)
                got = jnp.dot(m2t[tile], both, preferred_element_type=F32)
                if tile > 0:
                    got += cacc[half, pair]
                if tile < 3:
                    cacc[half, pair] = got
                else:
                    cc[2 * pair, pl.ds(256 * half, 256), :] = got[:, :128].astype(BF)
                    cc[2 * pair + 1, pl.ds(256 * half, 256), :] = got[:, 128:].astype(BF)

            if tile == 3:
                share(half).start()

    chip = 16 * x + 4 * y + z

    def term(block_row, first):
        rows = pl.ds(first, 512)
        right = jnp.concatenate([cc[lax.rem(block_row + d, 8), rows, :] for d in range(ND)], axis=1)
        return lax.dot_general(
            cc[block_row, rows, :], right, (((0,), (0,)), ((), ())), preferred_element_type=F32
        )

    def row_of(local):
        return 4 * core + 2 * (lax.rem(y, 2) ^ (local >> 1)) + (lax.rem(x, 2) ^ (local & 1))

    @pl.loop(0, 4)
    def _(local):
        got = term(row_of(local), 0)
        for d in range(ND):
            gs[local, d] = got[:, 128 * d : 128 * d + 128]

    for half in range(2):
        share(half).wait()

    @pl.loop(0, 4)
    def _(local):
        block_row = row_of(local)
        got = term(block_row, 512)
        for d in range(ND):
            gs[local, d] += got[:, 128 * d : 128 * d + 128]

        @pl.loop(0, 16)
        def _(step):
            dz, dx, dc = step & 3, (step & 1) ^ ((step >> 2) & 1), ((step >> 1) & 1) ^ (step >> 3)
            to_aa = aa ^ (8 * dx + 2 * dz + dc)
            mine = gs.at[local, :, pl.ds(pl.multiple_of(8 * to_aa, 8), 8), :]
            self = jnp.logical_and(block_row == ba, step == 0)

            @pl.when(self)
            def _():
                pltpu.make_async_copy(mine, gr.at[chip], grecv).start()

            @pl.when(jnp.logical_not(self))
            def _():
                pltpu.make_async_remote_copy(
                    mine, gr.at[chip], gsend, grecv,
                    device_id={"aa": to_aa, "ba": block_row}, device_id_type=MESH,
                ).start()

    total_wait(gr, grecv)
    got = jnp.sum(gr[...], axis=0) * (1.0 / 65536.0)
    acc[...] = got
    own = pl.ds(pl.multiple_of(8 * aa, 8), 8)
    fr[:, own, :] = got

    @pl.loop(1, 16)
    def _(step):
        pltpu.make_async_remote_copy(
            acc, fr.at[:, own, :], osend, frecv,
            device_id={"aa": lax.rem(aa + step, 16), "ba": ba}, device_id_type=MESH,
        ).start()

    for d in range(1, 4):
        @pl.loop(0, 16)
        def _(step):
            pltpu.make_async_remote_copy(
                acc.at[d], tr.at[d - 1, own, :], osend, trecv,
                device_id={"aa": lax.rem(aa + step, 16), "ba": lax.rem(ba + d, 8)}, device_id_type=MESH,
            ).start()

    total_wait(fr.at[:, pl.ds(0, 120), :], frecv)
    for d in range(ND):
        out[:, pl.ds(pl.multiple_of(128 * lax.rem(ba + d, 8), 128), 128)] = fr[d]
    total_wait(tr, trecv)
    for d in range(1, 4):
        out[:, pl.ds(pl.multiple_of(128 * lax.rem(ba + 8 - d, 8), 128), 128)] = tr[d - 1].T

    total_wait(sbuf.at[:, pl.ds(0, 254)], send)
    total_wait(m2buf.at[:, pl.ds(0, 7)], m2send)
    inside = lax.div(ba, 4) == core

    @pl.when(inside)
    def _():
        total_wait(gr.at[pl.ds(0, 63)], gsend)

    @pl.when(jnp.logical_not(inside))
    def _():
        total_wait(gr, gsend)

    total_wait(fr.at[:, pl.ds(0, 120), :], osend)
    total_wait(tr, osend)


def shards(field, mode_one, mode_two):
    dma = pltpu.SemaphoreType.DMA
    hbm = pl.BlockSpec(memory_space=pltpu.HBM)
    return pl.pallas_call(
        kernel,
        out_shape=jax.ShapeDtypeStruct((128, 1024), F32),
        in_specs=[hbm, hbm, hbm],
        out_specs=pl.BlockSpec(memory_space=pltpu.VMEM),
        scratch_shapes=[
            pltpu.VMEM((4, 1024, JT, 128), BF),
            pltpu.VMEM((JT, 1024, 128), BF),
            pltpu.VMEM((JT, 256, 128), BF),
            pltpu.VMEM((4, 256, JT, 128), BF),
            pltpu.VMEM((4, 2, 8, 256, 128), BF),
            pltpu.VMEM((1024, 256), BF),
            pltpu.VMEM((256, 1024), BF),
            pltpu.VMEM((4, JT, 256), BF),
            pltpu.VMEM((4, 16, JT, 256), BF),
            pltpu.VMEM((4, 256, 256), BF),
            pltpu.VMEM((2, 4, 256, 256), F32),
            pltpu.VMEM((8, 1024, 128), BF),
            pltpu.VMEM((4, ND, 128, 128), F32),
            pltpu.VMEM((64, ND, 8, 128), F32),
            pltpu.VMEM((ND, 8, 128), F32),
            pltpu.VMEM((ND, 128, 128), F32),
            pltpu.VMEM((3, 128, 128), F32),
            pltpu.VMEM((256, 256), BF),
            dma((4,)), dma((2,)),
            dma, dma((4,)), dma, dma, dma((2,)),
            dma((2,)), dma((2,)),
            dma, dma, dma, dma, dma,
        ],
        compiler_params=pltpu.CompilerParams(
            collective_id=0, has_side_effects=True, vmem_limit_bytes=56 * 1024 * 1024
        ),
        cost_estimate=pl.CostEstimate(flops=13_000_000_000, bytes_accessed=18_000_000, transcendentals=0),
    )(field, mode_one, mode_two.reshape(4, JT, 256))


def solution(mesh):
    in_specs = (P(None, "aa", "ba"), P(), P("aa", None))
    return jax.shard_map(shards, mesh=mesh, in_specs=in_specs, out_specs=P("ba", None), check_vma=False)
```

```python
import functools

import jax
import jax.numpy as jnp
from jax import lax
from jax.experimental import pallas as pl
from jax.experimental.pallas import tpu as pltpu
from jax.sharding import PartitionSpec as P

BF, F32 = jnp.bfloat16, jnp.float32
MESH = pl.DeviceIdType.MESH
JT = 16
CLASSES = ((0, 1), (2, 3), (4,))
ND = 5


def where_am_i():
    aa, ba = lax.axis_index("aa"), lax.axis_index("ba")
    core, z = lax.rem(aa, 2), lax.rem(lax.div(aa, 2), 4)
    x = 2 * lax.div(aa, 8) + lax.rem(ba, 2)
    y = lax.div(ba, 2)
    return aa, ba, x, y, z, core


def place(x, y, z, core):
    aa = 8 * lax.div(x, 2) + 2 * z + core
    ba = 2 * y + lax.rem(x, 2)
    return aa, ba


def masks(step):
    one = step ^ (step >> 2)
    mx, my, mz, mc = (one ^ (step >> 4)) & 3, one & 3, step & 3, (step ^ (step >> 6)) & 1
    return ((mx >> 1) << 3) | (mz << 1) | mc, (my << 1) | (mx & 1)


def total_wait(ref, sem):
    pltpu.make_async_copy(ref, ref, sem).wait()


def kernel(
    field, m1_hbm, m2_hbm, out,
    fbuf, tbuf, obuf, sbuf, rbuf, m1, m1t, m2, m2buf, m2t, cacc, cc, acc, fr, tr, pmat,
    fsem, wsem, send, recv, m2send, m2recv, m2sem, csend, crecv, gsend, grecv, osend, frecv, trecv, *parts,
):
    gs, r1, s1, r2, s2, r3 = (parts[3 * n : 3 * n + 3] for n in range(6))
    aa, ba, x, y, z, core = where_am_i()
    tiles = fbuf.shape[0]
    sibling = {"aa": aa + 1 - 2 * core, "ba": ba}
    place_in_k = 8 * core + 4 * lax.div(x, 2) + z

    def load(tile, part):
        rows = pl.ds(256 * part, 256)
        return pltpu.make_async_copy(
            field.at[rows, pl.ds(JT * tile, JT), :], fbuf.at[tile, rows], fsem.at[tile, part]
        )

    load_m1 = pltpu.make_async_copy(m1_hbm, m1, wsem.at[0])
    load_m2 = pltpu.make_async_copy(m2_hbm, m2, wsem.at[1])
    for part in range(4):
        load(0, part).start()
    load_m1.start()
    load_m2.start()

    barrier = pltpu.get_barrier_semaphore()

    def greet(aa_mask, ba_mask):
        pl.semaphore_signal(
            barrier, inc=1, device_id={"aa": aa ^ aa_mask, "ba": ba ^ ba_mask}, device_id_type=MESH
        )

    for ba_mask in range(1, 8):
        greet(0, ba_mask)

    @pl.loop(1, 16)
    def _(aa_mask):
        for ba_mask in range(8):
            greet(aa_mask, ba_mask)

    for tile in range(1, tiles):
        for part in range(4):
            load(tile, part).start()

    row = lax.broadcasted_iota(jnp.int32, (256, 256), 0)
    col = lax.broadcasted_iota(jnp.int32, (256, 256), 1)
    swap = ((row & 15) * 16 + (row >> 4)) == col
    pmat[...] = jnp.where(swap, 1.0, 0.0).astype(BF)
    load_m1.wait()
    m1t[...] = m1[...].T

    def send_rows(tile):
        def block(to_aa, to_ba):
            mine = sbuf.at[tile, pl.ds(2 * (8 * to_aa + to_ba), 2)]
            there = rbuf.at[tile, :, ba, pl.ds(pl.multiple_of(JT * place_in_k, JT), JT), :]
            return mine, there

        @pl.loop(1, 128)
        def _(step):
            aa_mask, ba_mask = masks(step)
            to_aa, to_ba = aa ^ aa_mask, ba ^ ba_mask
            mine, there = block(to_aa, to_ba)
            pltpu.make_async_remote_copy(
                mine, there, send, recv.at[tile], device_id={"aa": to_aa, "ba": to_ba}, device_id_type=MESH
            ).start()

        mine, there = block(aa, ba)
        pltpu.make_async_copy(mine, there, recv.at[tile]).start()

    @pl.loop(0, tiles)
    def _(tile):
        @pl.loop(0, 4)
        def _(part):
            load(tile, part).wait()

            @pl.loop(0, 8, unroll=4)
            def _(group):
                at = pl.multiple_of(256 * part + 32 * group, 32)
                left = fbuf[tile, pl.ds(at, 16)].reshape(256, 128)
                right = fbuf[tile, pl.ds(at + 16, 16)].reshape(256, 128)
                both = jnp.concatenate([left, right], axis=1)
                turned = jnp.dot(pmat[...], both, preferred_element_type=F32).astype(BF)
                tbuf[:, pl.ds(at, 16), :] = turned[:, :128].reshape(16, 16, 128)
                tbuf[:, pl.ds(pl.multiple_of(at + 16, 16), 16), :] = turned[:, 128:].reshape(16, 16, 128)

        @pl.loop(0, JT // 2)
        def _(pair):
            both = jnp.concatenate([tbuf[2 * pair], tbuf[2 * pair + 1]], axis=1)
            got = jnp.dot(m1t[...], both, preferred_element_type=F32).astype(BF)
            obuf[2 * pair] = got[:, :128]
            obuf[2 * pair + 1] = got[:, 128:]

        @pl.loop(0, 8, unroll=2)
        def _(group):
            at = pl.multiple_of(32 * group, 32)
            left = obuf[:, pl.ds(at, 16), :].reshape(256, 128)
            right = obuf[:, pl.ds(pl.multiple_of(at + 16, 16), 16), :].reshape(256, 128)
            both = jnp.concatenate([left, right], axis=1)
            turned = jnp.dot(pmat[...], both, preferred_element_type=F32).astype(BF)
            sbuf[tile, pl.ds(at, 16)] = turned[:, :128].reshape(16, 16, 128)
            sbuf[tile, pl.ds(at + 16, 16)] = turned[:, 128:].reshape(16, 16, 128)

        @pl.when(tile == 0)
        def _():
            pl.semaphore_wait(barrier, 127)

        send_rows(tile)

        @pl.when(tile == 1)
        def _():
            load_m2.wait()
            mine = m2buf.at[:, place_in_k]
            for mask in range(1, 8):
                to_aa, to_ba = place(x ^ (2 * (mask // 4)), y, z ^ (mask % 4), core)
                pltpu.make_async_remote_copy(
                    m2, mine, m2send, m2recv, device_id={"aa": to_aa, "ba": to_ba}, device_id_type=MESH
                ).start()
            pltpu.make_async_copy(m2, mine, m2recv).start()

    half_of_m2 = m2buf.at[:, pl.ds(8 * core, 8)]
    total_wait(half_of_m2, m2recv)
    pass_m2 = pltpu.make_async_remote_copy(
        half_of_m2, half_of_m2, m2sem.at[0], m2sem.at[1], device_id=sibling, device_id_type=MESH
    )
    pass_m2.start()
    pass_m2.wait()
    for tile in range(4):
        m2t[tile] = m2buf[tile].reshape(256, 256).T

    def share(half):
        return pltpu.make_async_remote_copy(
            cc.at[:, pl.ds(256 * half, 256), :], cc.at[:, pl.ds(512 + 256 * half, 256), :],
            csend.at[half], crecv.at[half], device_id=sibling, device_id_type=MESH,
        )

    for tile in range(4):
        total_wait(rbuf.at[tile], recv.at[tile])
        for half in range(2):
            @pl.loop(0, 4, unroll=2)
            def _(pair):
                both = jnp.concatenate([rbuf[tile, half, 2 * pair], rbuf[tile, half, 2 * pair + 1]], axis=1)
                got = jnp.dot(m2t[tile], both, preferred_element_type=F32)
                if tile > 0:
                    got += cacc[half, pair]
                if tile < 3:
                    cacc[half, pair] = got
                else:
                    cc[2 * pair, pl.ds(256 * half, 256), :] = got[:, :128].astype(BF)
                    cc[2 * pair + 1, pl.ds(256 * half, 256), :] = got[:, 128:].astype(BF)

            if tile == 3:
                share(half).start()

    where = (x, y, z)

    def term(block_row, first):
        rows = pl.ds(first, 512)
        right = jnp.concatenate([cc[lax.rem(block_row + d, 8), rows, :] for d in range(ND)], axis=1)
        return lax.dot_general(
            cc[block_row, rows, :], right, (((0,), (0,)), ((), ())), preferred_element_type=F32
        )

    def pieces(got, low_y, low_x):
        for octet in range(16):
            owner = (2 * (octet >> 3) + low_x, 2 * (octet & 1) + low_y, (octet >> 1) & 3)
            for k, columns in enumerate(CLASSES):
                index = tuple(owner[(k + stage) % 3] for stage in range(3))
                for n, d in enumerate(columns):
                    yield gs[k], index + (n,), got[8 * octet : 8 * octet + 8, 128 * d : 128 * d + 128]

    for low_y in range(2):
        for low_x in range(2):
            for ref, index, value in pieces(term(4 * core + 2 * low_y + low_x, 0), low_y, low_x):
                ref[index] = value
    for half in range(2):
        share(half).wait()
    for low_y in range(2):
        for low_x in range(2):
            for ref, index, value in pieces(term(4 * core + 2 * low_y + low_x, 512), low_y, low_x):
                ref[index] += value

    def scatter(k, stage):
        axis = (k + stage) % 3
        for mask in range(1, 4):
            there = [x, y, z]
            there[axis] = there[axis] ^ mask
            to_aa, to_ba = place(*there, core)
            pltpu.make_async_remote_copy(
                sums[stage][k].at[where[axis] ^ mask], got_from[stage][k].at[mask - 1], gsend, grecv.at[k, stage],
                device_id={"aa": to_aa, "ba": to_ba}, device_id_type=MESH,
            ).start()

    def gathered(k, stage):
        total_wait(got_from[stage][k], grecv.at[k, stage])
        got = got_from[stage][k]
        return sums[stage][k][where[(k + stage) % 3]] + got[0] + got[1] + got[2]

    sums = (gs, s1, s2)
    got_from = (r1, r2, r3)
    for k in range(3):
        scatter(k, 0)
    for stage in range(2):
        for k in range(3):
            sums[stage + 1][k][...] = gathered(k, stage)
            scatter(k, stage + 1)
    for k, columns in enumerate(CLASSES):
        acc[pl.ds(columns[0], len(columns))] = gathered(k, 2) * (1.0 / 65536.0)

    mine = 4 * core + 2 * lax.rem(y, 2) + lax.rem(x, 2)
    own = pl.ds(pl.multiple_of(8 * (8 * lax.div(x, 2) + 2 * z + lax.div(y, 2)), 8), 8)
    inside = mine == ba

    @pl.loop(0, 16)
    def _(step):
        self = jnp.logical_and(inside, step == 0)

        @pl.when(self)
        def _():
            pltpu.make_async_copy(acc, fr.at[:, own, :], frecv).start()

        @pl.when(jnp.logical_not(self))
        def _():
            pltpu.make_async_remote_copy(
                acc, fr.at[:, own, :], osend, frecv,
                device_id={"aa": aa ^ step, "ba": mine}, device_id_type=MESH,
            ).start()

        for d in range(1, 4):
            pltpu.make_async_remote_copy(
                acc.at[d], tr.at[d - 1, own, :], osend, trecv,
                device_id={"aa": aa ^ step, "ba": lax.rem(mine + d, 8)}, device_id_type=MESH,
            ).start()

    total_wait(fr, frecv)
    for d in range(ND):
        out[:, pl.ds(pl.multiple_of(128 * lax.rem(ba + d, 8), 128), 128)] = fr[d]
    total_wait(tr, trecv)
    for d in range(1, 4):
        out[:, pl.ds(pl.multiple_of(128 * lax.rem(ba + 8 - d, 8), 128), 128)] = tr[d - 1].T

    total_wait(sbuf.at[:, pl.ds(0, 254)], send)
    total_wait(m2buf.at[:, pl.ds(0, 7)], m2send)
    for stage in range(3):
        for k in range(3):
            total_wait(got_from[stage][k], gsend)
    total_wait(fr.at[:, pl.ds(0, 120), :], osend)

    @pl.when(jnp.logical_not(inside))
    def _():
        total_wait(fr.at[:, pl.ds(0, 8), :], osend)

    total_wait(tr, osend)


def shards(field, mode_one, mode_two):
    dma = pltpu.SemaphoreType.DMA
    hbm = pl.BlockSpec(memory_space=pltpu.HBM)
    return pl.pallas_call(
        kernel,
        out_shape=jax.ShapeDtypeStruct((128, 1024), F32),
        in_specs=[hbm, hbm, hbm],
        out_specs=pl.BlockSpec(memory_space=pltpu.VMEM),
        scratch_shapes=[
            pltpu.VMEM((4, 1024, JT, 128), BF),
            pltpu.VMEM((JT, 1024, 128), BF),
            pltpu.VMEM((JT, 256, 128), BF),
            pltpu.VMEM((4, 256, JT, 128), BF),
            pltpu.VMEM((4, 2, 8, 256, 128), BF),
            pltpu.VMEM((1024, 256), BF),
            pltpu.VMEM((256, 1024), BF),
            pltpu.VMEM((4, JT, 256), BF),
            pltpu.VMEM((4, 16, JT, 256), BF),
            pltpu.VMEM((4, 256, 256), BF),
            pltpu.VMEM((2, 4, 256, 256), F32),
            pltpu.VMEM((8, 1024, 128), BF),
            pltpu.VMEM((ND, 8, 128), F32),
            pltpu.VMEM((ND, 128, 128), F32),
            pltpu.VMEM((3, 128, 128), F32),
            pltpu.VMEM((256, 256), BF),
            dma((4, 4)), dma((2,)),
            dma, dma((4,)), dma, dma, dma((2,)),
            dma((2,)), dma((2,)),
            dma, dma((3, 3)), dma, dma, dma,
            *[
                pltpu.VMEM(shape + (len(columns), 8, 128), F32)
                for shape in ((4, 4, 4), (3, 4, 4), (4, 4), (3, 4), (4,), (3,))
                for columns in CLASSES
            ],
        ],
        compiler_params=pltpu.CompilerParams(
            collective_id=0, has_side_effects=True, vmem_limit_bytes=56 * 1024 * 1024
        ),
        cost_estimate=pl.CostEstimate(flops=13_000_000_000, bytes_accessed=18_000_000, transcendentals=0),
    )(field, mode_one, mode_two.reshape(4, JT, 256))


def solution(mesh):
    in_specs = (P(None, "aa", "ba"), P(), P("aa", None))
    return jax.shard_map(shards, mesh=mesh, in_specs=in_specs, out_specs=P("ba", None), check_vma=False)
```

```python
import functools

import jax
import jax.numpy as jnp
from jax import lax
from jax.experimental import pallas as pl
from jax.experimental.pallas import tpu as pltpu
from jax.sharding import PartitionSpec as P

BF, F32 = jnp.bfloat16, jnp.float32
MESH = pl.DeviceIdType.MESH
JT = 16
CLASSES = ((0, 1), (2, 3), (4,))
ND = 5


def where_am_i():
    aa, ba = lax.axis_index("aa"), lax.axis_index("ba")
    core, z = lax.rem(aa, 2), lax.rem(lax.div(aa, 2), 4)
    x = 2 * lax.div(aa, 8) + lax.rem(ba, 2)
    y = lax.div(ba, 2)
    return aa, ba, x, y, z, core


def place(x, y, z, core):
    aa = 8 * lax.div(x, 2) + 2 * z + core
    ba = 2 * y + lax.rem(x, 2)
    return aa, ba


def masks(step):
    one = step ^ (step >> 2)
    mx, my, mz, mc = (one ^ (step >> 4)) & 3, one & 3, step & 3, (step ^ (step >> 6)) & 1
    return ((mx >> 1) << 3) | (mz << 1) | mc, (my << 1) | (mx & 1)


def total_wait(ref, sem):
    pltpu.make_async_copy(ref, ref, sem).wait()


def kernel(
    field, m1_hbm, m2_hbm, out,
    fbuf, tbuf, obuf, sbuf, rbuf, m1, m1t, m2, m2buf, m2t, cacc, cc, acc, fr, tr, pmat,
    fsem, wsem, send, recv, m2send, m2recv, m2sem, csend, crecv, gsend, grecv, osend, frecv, trecv, wsend, wrecv, *parts,
):
    gs, r1, s1, r2, s2, r3 = (parts[3 * n : 3 * n + 3] for n in range(6))
    aa, ba, x, y, z, core = where_am_i()
    tiles = fbuf.shape[0]
    sibling = {"aa": aa + 1 - 2 * core, "ba": ba}
    place_in_k = 8 * core + 4 * lax.div(x, 2) + z

    def load(tile, part):
        rows = pl.ds(256 * part, 256)
        return pltpu.make_async_copy(
            field.at[rows, pl.ds(JT * tile, JT), :], fbuf.at[tile, rows], fsem.at[tile, part]
        )

    load_m1 = pltpu.make_async_copy(m1_hbm, m1, wsem.at[0])
    load_m2 = pltpu.make_async_copy(m2_hbm, m2, wsem.at[1])
    load_m1.start()
    for part in range(4):
        load(0, part).start()
    load_m2.start()

    barrier = pltpu.get_barrier_semaphore()

    def greet(aa_mask, ba_mask):
        pl.semaphore_signal(
            barrier, inc=1, device_id={"aa": aa ^ aa_mask, "ba": ba ^ ba_mask}, device_id_type=MESH
        )

    for ba_mask in range(1, 8):
        greet(0, ba_mask)

    @pl.loop(1, 16)
    def _(aa_mask):
        for ba_mask in range(8):
            greet(aa_mask, ba_mask)

    for tile in range(1, tiles):
        for part in range(4):
            load(tile, part).start()

    row = lax.broadcasted_iota(jnp.int32, (256, 256), 0)
    col = lax.broadcasted_iota(jnp.int32, (256, 256), 1)
    swap = ((row & 15) * 16 + (row >> 4)) == col
    pmat[...] = jnp.where(swap, 1.0, 0.0).astype(BF)
    load_m1.wait()
    m1t[...] = m1[...].T

    def send_rows(tile, first, count, sem):
        rows = pl.ds(pl.multiple_of(JT * place_in_k, JT), JT)

        def block(to_aa, to_ba):
            mine = sbuf.at[tile, pl.ds(2 * (8 * to_aa + to_ba) + first, count)]
            return mine, rbuf.at[tile, pl.ds(first, count), ba, rows, :]

        @pl.loop(1, 128)
        def _(step):
            aa_mask, ba_mask = masks(step)
            to_aa, to_ba = aa ^ aa_mask, ba ^ ba_mask
            mine, there = block(to_aa, to_ba)
            pltpu.make_async_remote_copy(
                mine, there, send, sem, device_id={"aa": to_aa, "ba": to_ba}, device_id_type=MESH
            ).start()

        mine, there = block(aa, ba)
        pltpu.make_async_copy(mine, there, sem).start()

    @pl.loop(0, tiles)
    def _(tile):
        @pl.loop(0, 4)
        def _(part):
            load(tile, part).wait()

            @pl.loop(0, 8, unroll=4)
            def _(group):
                at = pl.multiple_of(256 * part + 32 * group, 32)
                left = fbuf[tile, pl.ds(at, 16)].reshape(256, 128)
                right = fbuf[tile, pl.ds(at + 16, 16)].reshape(256, 128)
                both = jnp.concatenate([left, right], axis=1)
                turned = jnp.dot(pmat[...], both, preferred_element_type=F32).astype(BF)
                tbuf[:, pl.ds(at, 16), :] = turned[:, :128].reshape(16, 16, 128)
                tbuf[:, pl.ds(pl.multiple_of(at + 16, 16), 16), :] = turned[:, 128:].reshape(16, 16, 128)

        @pl.loop(0, JT // 2)
        def _(pair):
            both = jnp.concatenate([tbuf[2 * pair], tbuf[2 * pair + 1]], axis=1)
            got = jnp.dot(m1t[...], both, preferred_element_type=F32).astype(BF)
            obuf[2 * pair] = got[:, :128]
            obuf[2 * pair + 1] = got[:, 128:]

        @pl.loop(0, 8, unroll=2)
        def _(group):
            at = pl.multiple_of(32 * group, 32)
            left = obuf[:, pl.ds(at, 16), :].reshape(256, 128)
            right = obuf[:, pl.ds(pl.multiple_of(at + 16, 16), 16), :].reshape(256, 128)
            both = jnp.concatenate([left, right], axis=1)
            turned = jnp.dot(pmat[...], both, preferred_element_type=F32).astype(BF)
            sbuf[tile, pl.ds(at, 16)] = turned[:, :128].reshape(16, 16, 128)
            sbuf[tile, pl.ds(at + 16, 16)] = turned[:, 128:].reshape(16, 16, 128)

        @pl.when(tile == 0)
        def _():
            pl.semaphore_wait(barrier, 127)

        @pl.when(tile < 3)
        def _():
            send_rows(tile, 0, 2, recv.at[tile])

        @pl.when(tile == 3)
        def _():
            for half in range(2):
                send_rows(tile, half, 1, recv.at[3 + half])

        @pl.when(tile == 1)
        def _():
            load_m2.wait()
            mine = m2buf.at[:, place_in_k]
            for mask in range(1, 8):
                to_aa, to_ba = place(x ^ (2 * (mask // 4)), y, z ^ (mask % 4), core)
                pltpu.make_async_remote_copy(
                    m2, mine, m2send, m2recv, device_id={"aa": to_aa, "ba": to_ba}, device_id_type=MESH
                ).start()
            pltpu.make_async_copy(m2, mine, m2recv).start()

    half_of_m2 = m2buf.at[:, pl.ds(8 * core, 8)]
    total_wait(half_of_m2, m2recv)
    pass_m2 = pltpu.make_async_remote_copy(
        half_of_m2, half_of_m2, m2sem.at[0], m2sem.at[1], device_id=sibling, device_id_type=MESH
    )
    pass_m2.start()
    pass_m2.wait()
    for tile in range(4):
        m2t[tile] = m2buf[tile].reshape(256, 256).T

    def share(half):
        return pltpu.make_async_remote_copy(
            cc.at[:, pl.ds(256 * half, 256), :], cc.at[:, pl.ds(512 + 256 * half, 256), :],
            csend.at[half], crecv.at[half], device_id=sibling, device_id_type=MESH,
        )

    for tile in range(4):
        if tile < 3:
            total_wait(rbuf.at[tile], recv.at[tile])
        for half in range(2):
            if tile == 3:
                total_wait(rbuf.at[tile, half], recv.at[3 + half])

            @pl.loop(0, 4, unroll=2)
            def _(pair):
                both = jnp.concatenate([rbuf[tile, half, 2 * pair], rbuf[tile, half, 2 * pair + 1]], axis=1)
                got = jnp.dot(m2t[tile], both, preferred_element_type=F32)
                if tile > 0:
                    got += cacc[half, pair]
                if tile < 3:
                    cacc[half, pair] = got
                else:
                    cc[2 * pair, pl.ds(256 * half, 256), :] = got[:, :128].astype(BF)
                    cc[2 * pair + 1, pl.ds(256 * half, 256), :] = got[:, 128:].astype(BF)

            if tile == 3:
                share(half).start()

    where = (x, y, z)

    def term(block_row, first):
        rows = pl.ds(first, 512)
        right = jnp.concatenate([cc[lax.rem(block_row + d, 8), rows, :] for d in range(ND)], axis=1)
        return lax.dot_general(
            cc[block_row, rows, :], right, (((0,), (0,)), ((), ())), preferred_element_type=F32
        )

    def pieces(got, low_y, low_x):
        for octet in range(16):
            owner = (2 * (octet >> 3) + low_x, 2 * (octet & 1) + low_y, (octet >> 1) & 3)
            for k, columns in enumerate(CLASSES):
                index = tuple(owner[(k + stage) % 3] for stage in range(3))
                for n, d in enumerate(columns):
                    yield gs[k], index + (n,), got[8 * octet : 8 * octet + 8, 128 * d : 128 * d + 128]

    for low_y in range(2):
        for low_x in range(2):
            for ref, index, value in pieces(term(4 * core + 2 * low_y + low_x, 0), low_y, low_x):
                ref[index] = value
    for half in range(2):
        share(half).wait()
    for low_y in range(2):
        for low_x in range(2):
            for ref, index, value in pieces(term(4 * core + 2 * low_y + low_x, 512), low_y, low_x):
                ref[index] += value

    def scatter(k, stage):
        axis = (k + stage) % 3
        for mask in range(1, 4):
            there = [x, y, z]
            there[axis] = there[axis] ^ mask
            to_aa, to_ba = place(*there, core)
            pltpu.make_async_remote_copy(
                sums[stage][k].at[where[axis] ^ mask], got_from[stage][k].at[mask - 1], gsend, grecv.at[k, stage],
                device_id={"aa": to_aa, "ba": to_ba}, device_id_type=MESH,
            ).start()

    def gathered(k, stage):
        total_wait(got_from[stage][k], grecv.at[k, stage])
        got = got_from[stage][k]
        return sums[stage][k][where[(k + stage) % 3]] + got[0] + got[1] + got[2]

    sums = (gs, s1, s2)
    got_from = (r1, r2, r3)
    for k in range(3):
        scatter(k, 0)
    for stage in range(2):
        for k in range(3):
            sums[stage + 1][k][...] = gathered(k, stage)
            scatter(k, stage + 1)
    for k, columns in enumerate(CLASSES):
        acc[pl.ds(columns[0], len(columns))] = gathered(k, 2) * (1.0 / 65536.0)

    mine = 4 * core + 2 * lax.rem(y, 2) + lax.rem(x, 2)
    own = pl.ds(pl.multiple_of(8 * (8 * lax.div(x, 2) + 2 * z + lax.div(y, 2)), 8), 8)
    inside = jnp.logical_and(mine == ba, lax.div(x, 2) == core)

    taker = lax.div(x, 2)

    @pl.loop(0, 8)
    def _(step):
        to_aa = (aa ^ (2 * step) ^ core) | taker
        self = jnp.logical_and(inside, step == 0)

        @pl.when(self)
        def _():
            pltpu.make_async_copy(acc, fr.at[:, own, :], frecv).start()

        @pl.when(jnp.logical_not(self))
        def _():
            pltpu.make_async_remote_copy(
                acc, fr.at[:, own, :], osend, frecv,
                device_id={"aa": to_aa, "ba": mine}, device_id_type=MESH,
            ).start()

        for d in range(1, 4):
            pltpu.make_async_remote_copy(
                acc.at[d], tr.at[d - 1, own, :], osend, trecv,
                device_id={"aa": to_aa, "ba": lax.rem(mine + d, 8)}, device_id_type=MESH,
            ).start()

    half = pl.ds(pl.multiple_of(64 * core, 64), 64)
    swaps = []
    for n, (ref, sem) in enumerate(((fr, frecv), (tr, trecv))):
        total_wait(ref.at[:, half, :], sem)
        swaps.append(pltpu.make_async_remote_copy(
            ref.at[:, half, :], ref.at[:, half, :], wsend.at[n], wrecv.at[n],
            device_id=sibling, device_id_type=MESH,
        ))
        swaps[n].start()

    swaps[0].wait()
    for d in range(ND):
        out[:, pl.ds(pl.multiple_of(128 * lax.rem(ba + d, 8), 128), 128)] = fr[d]
    swaps[1].wait()
    for d in range(1, 4):
        out[:, pl.ds(pl.multiple_of(128 * lax.rem(ba + 8 - d, 8), 128), 128)] = tr[d - 1].T

    total_wait(sbuf.at[:, pl.ds(0, 254)], send)
    total_wait(m2buf.at[:, pl.ds(0, 7)], m2send)
    for stage in range(3):
        for k in range(3):
            total_wait(got_from[stage][k], gsend)
    total_wait(fr.at[:, pl.ds(0, 56), :], osend)

    @pl.when(jnp.logical_not(inside))
    def _():
        total_wait(fr.at[:, pl.ds(0, 8), :], osend)

    total_wait(tr.at[:, pl.ds(0, 64), :], osend)


def shards(field, mode_one, mode_two):
    dma = pltpu.SemaphoreType.DMA
    hbm = pl.BlockSpec(memory_space=pltpu.HBM)
    return pl.pallas_call(
        kernel,
        out_shape=jax.ShapeDtypeStruct((128, 1024), F32),
        in_specs=[hbm, hbm, hbm],
        out_specs=pl.BlockSpec(memory_space=pltpu.VMEM),
        scratch_shapes=[
            pltpu.VMEM((4, 1024, JT, 128), BF),
            pltpu.VMEM((JT, 1024, 128), BF),
            pltpu.VMEM((JT, 256, 128), BF),
            pltpu.VMEM((4, 256, JT, 128), BF),
            pltpu.VMEM((4, 2, 8, 256, 128), BF),
            pltpu.VMEM((1024, 256), BF),
            pltpu.VMEM((256, 1024), BF),
            pltpu.VMEM((4, JT, 256), BF),
            pltpu.VMEM((4, 16, JT, 256), BF),
            pltpu.VMEM((4, 256, 256), BF),
            pltpu.VMEM((2, 4, 256, 256), F32),
            pltpu.VMEM((8, 1024, 128), BF),
            pltpu.VMEM((ND, 8, 128), F32),
            pltpu.VMEM((ND, 128, 128), F32),
            pltpu.VMEM((3, 128, 128), F32),
            pltpu.VMEM((256, 256), BF),
            dma((4, 4)), dma((2,)),
            dma, dma((5,)), dma, dma, dma((2,)),
            dma((2,)), dma((2,)),
            dma, dma((3, 3)), dma, dma, dma, dma((2,)), dma((2,)),
            *[
                pltpu.VMEM(shape + (len(columns), 8, 128), F32)
                for shape in ((4, 4, 4), (3, 4, 4), (4, 4), (3, 4), (4,), (3,))
                for columns in CLASSES
            ],
        ],
        compiler_params=pltpu.CompilerParams(
            collective_id=0, has_side_effects=True, vmem_limit_bytes=53 * 1024 * 1024
        ),
        cost_estimate=pl.CostEstimate(flops=13_000_000_000, bytes_accessed=18_000_000, transcendentals=0),
    )(field, mode_one, mode_two.reshape(4, JT, 256))


def solution(mesh):
    in_specs = (P(None, "aa", "ba"), P(), P("aa", None))
    return jax.shard_map(shards, mesh=mesh, in_specs=in_specs, out_specs=P("ba", None), check_vma=False)
```

```python
import functools

import jax
import jax.numpy as jnp
from jax import lax
from jax.experimental import pallas as pl
from jax.experimental.pallas import tpu as pltpu
from jax.sharding import PartitionSpec as P

BF, F32 = jnp.bfloat16, jnp.float32
MESH = pl.DeviceIdType.MESH
JT = 16
CLASSES = ((0, 1), (2, 3), (4,))
RELAYED = 2
OPPOSITE = 74
ND = 5


def where_am_i():
    aa, ba = lax.axis_index("aa"), lax.axis_index("ba")
    core, z = lax.rem(aa, 2), lax.rem(lax.div(aa, 2), 4)
    x = 2 * lax.div(aa, 8) + lax.rem(ba, 2)
    y = lax.div(ba, 2)
    return aa, ba, x, y, z, core


def place(x, y, z, core):
    aa = 8 * lax.div(x, 2) + 2 * z + core
    ba = 2 * y + lax.rem(x, 2)
    return aa, ba


def masks(step):
    one = step ^ (step >> 2)
    return (one ^ (step >> 4)) & 3, one & 3, step & 3, (step ^ (step >> 6)) & 1


def mesh_masks(mx, my, mz, mc):
    return ((mx >> 1) << 3) | (mz << 1) | mc, (my << 1) | (mx & 1)


def total_wait(ref, sem):
    pltpu.make_async_copy(ref, ref, sem).wait()


def kernel(
    field, m1_hbm, m2_hbm, out,
    fbuf, tbuf, obuf, sbuf, rbuf, relay, m1, m1t, m2, m2buf, m2t, cacc, cc, acc, fr, tr, pmat,
    fsem, wsem, send, recv, arrived, m2send, m2recv, m2sem, csend, crecv, gsend, grecv, osend, frecv, trecv, wsend, wrecv, *parts,
):
    gs, r1, s1, r2, s2, r3 = (parts[3 * n : 3 * n + 3] for n in range(6))
    aa, ba, x, y, z, core = where_am_i()
    tiles = fbuf.shape[0]
    sibling = {"aa": aa + 1 - 2 * core, "ba": ba}
    place_in_k = 8 * core + 4 * lax.div(x, 2) + z

    def load(tile, part):
        rows = pl.ds(256 * part, 256)
        return pltpu.make_async_copy(
            field.at[rows, pl.ds(JT * tile, JT), :], fbuf.at[tile, rows], fsem.at[tile, part]
        )

    load_m1 = pltpu.make_async_copy(m1_hbm, m1, wsem.at[0])
    load_m2 = pltpu.make_async_copy(m2_hbm, m2, wsem.at[1])
    load_m1.start()
    for part in range(4):
        load(0, part).start()
    load_m2.start()

    barrier = pltpu.get_barrier_semaphore()

    def greet(aa_mask, ba_mask):
        pl.semaphore_signal(
            barrier, inc=1, device_id={"aa": aa ^ aa_mask, "ba": ba ^ ba_mask}, device_id_type=MESH
        )

    for ba_mask in range(1, 8):
        greet(0, ba_mask)

    @pl.loop(1, 16)
    def _(aa_mask):
        for ba_mask in range(8):
            greet(aa_mask, ba_mask)

    for tile in range(1, tiles):
        for part in range(4):
            load(tile, part).start()

    row = lax.broadcasted_iota(jnp.int32, (256, 256), 0)
    col = lax.broadcasted_iota(jnp.int32, (256, 256), 1)
    swap = ((row & 15) * 16 + (row >> 4)) == col
    pmat[...] = jnp.where(swap, 1.0, 0.0).astype(BF)
    load_m1.wait()
    m1t[...] = m1[...].T

    def send_rows(tile, first, count, sem):
        rows = pl.ds(pl.multiple_of(JT * place_in_k, JT), JT)

        def block(to_aa, to_ba):
            mine = sbuf.at[tile, pl.ds(2 * (8 * to_aa + to_ba) + first, count)]
            return mine, rbuf.at[tile, pl.ds(first, count), ba, rows, :]

        @pl.loop(1, 128)
        def _(step):
            each = masks(step)
            aa_mask, ba_mask = mesh_masks(*each)
            to_aa, to_ba = aa ^ aa_mask, ba ^ ba_mask
            mine, there = block(to_aa, to_ba)
            by_relay = jnp.logical_and(opposite(each), tile < RELAYED) if count == 2 else False

            @pl.when(by_relay)
            def _():
                if count == 1:
                    return
                via_aa, via_ba = place(*[on_way(p, m, 1) for p, m in zip((x, y, z), each)], core)
                pltpu.make_async_remote_copy(
                    mine, relay.at[jnp.minimum(tile, RELAYED - 1), step], send, arrived.at[tile],
                    device_id={"aa": via_aa, "ba": via_ba}, device_id_type=MESH,
                ).start()

            @pl.when(jnp.logical_not(by_relay))
            def _():
                pltpu.make_async_remote_copy(
                    mine, there, send, sem, device_id={"aa": to_aa, "ba": to_ba}, device_id_type=MESH
                ).start()

        mine, there = block(aa, ba)
        pltpu.make_async_copy(mine, there, sem).start()

    def opposite(each):
        return jnp.logical_or(each[0] == 2, jnp.logical_or(each[1] == 2, each[2] == 2))

    def on_way(p, mask, steps):
        return jnp.where(mask == 2, (p + 3 * steps) & 3, p)

    def forward(tile):
        total_wait(relay.at[tile, pl.ds(0, OPPOSITE)], arrived.at[tile])

        @pl.loop(1, 128)
        def _(step):
            each = masks(step)

            @pl.when(opposite(each))
            def _():
                from_x, from_y, from_z = [on_way(p, m, -1) for p, m in zip((x, y, z), each)]
                _, from_ba = place(from_x, from_y, from_z, core)
                from_place = 8 * core + 4 * lax.div(from_x, 2) + from_z
                to = [jnp.where(m == 2, on_way(p, m, 1), p ^ m) for p, m in zip((x, y, z), each)]
                to_aa, to_ba = place(*to, core ^ each[3])
                rows = pl.ds(pl.multiple_of(JT * from_place, JT), JT)
                pltpu.make_async_remote_copy(
                    relay.at[tile, step], rbuf.at[tile, :, from_ba, rows, :], send, recv.at[tile],
                    device_id={"aa": to_aa, "ba": to_ba}, device_id_type=MESH,
                ).start()

    @pl.loop(0, tiles)
    def _(tile):
        @pl.loop(0, 4)
        def _(part):
            load(tile, part).wait()

            @pl.loop(0, 8, unroll=4)
            def _(group):
                at = pl.multiple_of(256 * part + 32 * group, 32)
                left = fbuf[tile, pl.ds(at, 16)].reshape(256, 128)
                right = fbuf[tile, pl.ds(at + 16, 16)].reshape(256, 128)
                both = jnp.concatenate([left, right], axis=1)
                turned = jnp.dot(pmat[...], both, preferred_element_type=F32).astype(BF)
                tbuf[:, pl.ds(at, 16), :] = turned[:, :128].reshape(16, 16, 128)
                tbuf[:, pl.ds(pl.multiple_of(at + 16, 16), 16), :] = turned[:, 128:].reshape(16, 16, 128)

        @pl.loop(0, JT // 2)
        def _(pair):
            both = jnp.concatenate([tbuf[2 * pair], tbuf[2 * pair + 1]], axis=1)
            got = jnp.dot(m1t[...], both, preferred_element_type=F32).astype(BF)
            obuf[2 * pair] = got[:, :128]
            obuf[2 * pair + 1] = got[:, 128:]

        @pl.loop(0, 8, unroll=2)
        def _(group):
            at = pl.multiple_of(32 * group, 32)
            left = obuf[:, pl.ds(at, 16), :].reshape(256, 128)
            right = obuf[:, pl.ds(pl.multiple_of(at + 16, 16), 16), :].reshape(256, 128)
            both = jnp.concatenate([left, right], axis=1)
            turned = jnp.dot(pmat[...], both, preferred_element_type=F32).astype(BF)
            sbuf[tile, pl.ds(at, 16)] = turned[:, :128].reshape(16, 16, 128)
            sbuf[tile, pl.ds(at + 16, 16)] = turned[:, 128:].reshape(16, 16, 128)

        @pl.when(tile == 0)
        def _():
            pl.semaphore_wait(barrier, 127)

        @pl.when(tile >= 4 - RELAYED)
        def _():
            forward(tile - (4 - RELAYED))

        @pl.when(tile < 3)
        def _():
            send_rows(tile, 0, 2, recv.at[tile])

        @pl.when(tile == 3)
        def _():
            for half in range(2):
                send_rows(tile, half, 1, recv.at[3 + half])

        @pl.when(tile == 1)
        def _():
            load_m2.wait()
            mine = m2buf.at[:, place_in_k]
            for mask in range(1, 8):
                to_aa, to_ba = place(x ^ (2 * (mask // 4)), y, z ^ (mask % 4), core)
                pltpu.make_async_remote_copy(
                    m2, mine, m2send, m2recv, device_id={"aa": to_aa, "ba": to_ba}, device_id_type=MESH
                ).start()
            pltpu.make_async_copy(m2, mine, m2recv).start()

    half_of_m2 = m2buf.at[:, pl.ds(8 * core, 8)]
    total_wait(half_of_m2, m2recv)
    pass_m2 = pltpu.make_async_remote_copy(
        half_of_m2, half_of_m2, m2sem.at[0], m2sem.at[1], device_id=sibling, device_id_type=MESH
    )
    pass_m2.start()
    pass_m2.wait()
    for tile in range(4):
        m2t[tile] = m2buf[tile].reshape(256, 256).T

    def share(half):
        return pltpu.make_async_remote_copy(
            cc.at[:, pl.ds(256 * half, 256), :], cc.at[:, pl.ds(512 + 256 * half, 256), :],
            csend.at[half], crecv.at[half], device_id=sibling, device_id_type=MESH,
        )

    for tile in range(4):
        if tile < 3:
            total_wait(rbuf.at[tile], recv.at[tile])
        for half in range(2):
            if tile == 3:
                total_wait(rbuf.at[tile, half], recv.at[3 + half])

            @pl.loop(0, 4, unroll=2)
            def _(pair):
                both = jnp.concatenate([rbuf[tile, half, 2 * pair], rbuf[tile, half, 2 * pair + 1]], axis=1)
                got = jnp.dot(m2t[tile], both, preferred_element_type=F32)
                if tile > 0:
                    got += cacc[half, pair]
                if tile < 3:
                    cacc[half, pair] = got
                else:
                    cc[2 * pair, pl.ds(256 * half, 256), :] = got[:, :128].astype(BF)
                    cc[2 * pair + 1, pl.ds(256 * half, 256), :] = got[:, 128:].astype(BF)

            if tile == 3:
                share(half).start()

    where = (x, y, z)

    def term(block_row, first):
        rows = pl.ds(first, 512)
        right = jnp.concatenate([cc[lax.rem(block_row + d, 8), rows, :] for d in range(ND)], axis=1)
        return lax.dot_general(
            cc[block_row, rows, :], right, (((0,), (0,)), ((), ())), preferred_element_type=F32
        )

    def pieces(got, low_y, low_x):
        for octet in range(16):
            owner = (2 * (octet >> 3) + low_x, 2 * (octet & 1) + low_y, (octet >> 1) & 3)
            for k, columns in enumerate(CLASSES):
                index = tuple(owner[(k + stage) % 3] for stage in range(3))
                for n, d in enumerate(columns):
                    yield gs[k], index + (n,), got[8 * octet : 8 * octet + 8, 128 * d : 128 * d + 128]

    for low_y in range(2):
        for low_x in range(2):
            for ref, index, value in pieces(term(4 * core + 2 * low_y + low_x, 0), low_y, low_x):
                ref[index] = value
    for half in range(2):
        share(half).wait()
    for low_y in range(2):
        for low_x in range(2):
            for ref, index, value in pieces(term(4 * core + 2 * low_y + low_x, 512), low_y, low_x):
                ref[index] += value

    def scatter(k, stage):
        axis = (k + stage) % 3
        for mask in range(1, 4):
            there = [x, y, z]
            there[axis] = there[axis] ^ mask
            to_aa, to_ba = place(*there, core)
            pltpu.make_async_remote_copy(
                sums[stage][k].at[where[axis] ^ mask], got_from[stage][k].at[mask - 1], gsend, grecv.at[k, stage],
                device_id={"aa": to_aa, "ba": to_ba}, device_id_type=MESH,
            ).start()

    def gathered(k, stage):
        total_wait(got_from[stage][k], grecv.at[k, stage])
        got = got_from[stage][k]
        return sums[stage][k][where[(k + stage) % 3]] + got[0] + got[1] + got[2]

    sums = (gs, s1, s2)
    got_from = (r1, r2, r3)
    for k in range(3):
        scatter(k, 0)
    for stage in range(2):
        for k in range(3):
            sums[stage + 1][k][...] = gathered(k, stage)
            scatter(k, stage + 1)
    for k, columns in enumerate(CLASSES):
        acc[pl.ds(columns[0], len(columns))] = gathered(k, 2) * (1.0 / 65536.0)

    mine = 4 * core + 2 * lax.rem(y, 2) + lax.rem(x, 2)
    own = pl.ds(pl.multiple_of(8 * (8 * lax.div(x, 2) + 2 * z + lax.div(y, 2)), 8), 8)
    inside = jnp.logical_and(mine == ba, lax.div(x, 2) == core)

    taker = lax.div(x, 2)

    @pl.loop(0, 8)
    def _(step):
        to_aa = (aa ^ (2 * step) ^ core) | taker
        self = jnp.logical_and(inside, step == 0)

        @pl.when(self)
        def _():
            pltpu.make_async_copy(acc, fr.at[:, own, :], frecv).start()

        @pl.when(jnp.logical_not(self))
        def _():
            pltpu.make_async_remote_copy(
                acc, fr.at[:, own, :], osend, frecv,
                device_id={"aa": to_aa, "ba": mine}, device_id_type=MESH,
            ).start()

        for d in range(1, 4):
            pltpu.make_async_remote_copy(
                acc.at[d], tr.at[d - 1, own, :], osend, trecv,
                device_id={"aa": to_aa, "ba": lax.rem(mine + d, 8)}, device_id_type=MESH,
            ).start()

    half = pl.ds(pl.multiple_of(64 * core, 64), 64)
    swaps = []
    for n, (ref, sem) in enumerate(((fr, frecv), (tr, trecv))):
        total_wait(ref.at[:, half, :], sem)
        swaps.append(pltpu.make_async_remote_copy(
            ref.at[:, half, :], ref.at[:, half, :], wsend.at[n], wrecv.at[n],
            device_id=sibling, device_id_type=MESH,
        ))
        swaps[n].start()

    swaps[0].wait()
    for d in range(ND):
        out[:, pl.ds(pl.multiple_of(128 * lax.rem(ba + d, 8), 128), 128)] = fr[d]
    swaps[1].wait()
    for d in range(1, 4):
        out[:, pl.ds(pl.multiple_of(128 * lax.rem(ba + 8 - d, 8), 128), 128)] = tr[d - 1].T

    total_wait(sbuf.at[:, pl.ds(0, 254)], send)
    total_wait(relay.at[:, pl.ds(0, OPPOSITE)], send)
    total_wait(m2buf.at[:, pl.ds(0, 7)], m2send)
    for stage in range(3):
        for k in range(3):
            total_wait(got_from[stage][k], gsend)
    total_wait(fr.at[:, pl.ds(0, 56), :], osend)

    @pl.when(jnp.logical_not(inside))
    def _():
        total_wait(fr.at[:, pl.ds(0, 8), :], osend)

    total_wait(tr.at[:, pl.ds(0, 64), :], osend)


def shards(field, mode_one, mode_two):
    dma = pltpu.SemaphoreType.DMA
    hbm = pl.BlockSpec(memory_space=pltpu.HBM)
    return pl.pallas_call(
        kernel,
        out_shape=jax.ShapeDtypeStruct((128, 1024), F32),
        in_specs=[hbm, hbm, hbm],
        out_specs=pl.BlockSpec(memory_space=pltpu.VMEM),
        scratch_shapes=[
            pltpu.VMEM((4, 1024, JT, 128), BF),
            pltpu.VMEM((JT, 1024, 128), BF),
            pltpu.VMEM((JT, 256, 128), BF),
            pltpu.VMEM((4, 256, JT, 128), BF),
            pltpu.VMEM((4, 2, 8, 256, 128), BF),
            pltpu.VMEM((RELAYED, 128, 2, JT, 128), BF),
            pltpu.VMEM((1024, 256), BF),
            pltpu.VMEM((256, 1024), BF),
            pltpu.VMEM((4, JT, 256), BF),
            pltpu.VMEM((4, 16, JT, 256), BF),
            pltpu.VMEM((4, 256, 256), BF),
            pltpu.VMEM((2, 4, 256, 256), F32),
            pltpu.VMEM((8, 1024, 128), BF),
            pltpu.VMEM((ND, 8, 128), F32),
            pltpu.VMEM((ND, 128, 128), F32),
            pltpu.VMEM((3, 128, 128), F32),
            pltpu.VMEM((256, 256), BF),
            dma((4, 4)), dma((2,)),
            dma, dma((5,)), dma((4,)), dma, dma, dma((2,)),
            dma((2,)), dma((2,)),
            dma, dma((3, 3)), dma, dma, dma, dma((2,)), dma((2,)),
            *[
                pltpu.VMEM(shape + (len(columns), 8, 128), F32)
                for shape in ((4, 4, 4), (3, 4, 4), (4, 4), (3, 4), (4,), (3,))
                for columns in CLASSES
            ],
        ],
        compiler_params=pltpu.CompilerParams(
            collective_id=0, has_side_effects=True, vmem_limit_bytes=53 * 1024 * 1024
        ),
        cost_estimate=pl.CostEstimate(flops=13_000_000_000, bytes_accessed=18_000_000, transcendentals=0),
    )(field, mode_one, mode_two.reshape(4, JT, 256))


def solution(mesh):
    in_specs = (P(None, "aa", "ba"), P(), P("aa", None))
    return jax.shard_map(shards, mesh=mesh, in_specs=in_specs, out_specs=P("ba", None), check_vma=False)
```

```python
import functools

import jax
import jax.numpy as jnp
from jax import lax
from jax.experimental import pallas as pl
from jax.experimental.pallas import tpu as pltpu
from jax.sharding import PartitionSpec as P

BF, F32 = jnp.bfloat16, jnp.float32
MESH = pl.DeviceIdType.MESH
JT = 16
CLASSES = ((0, 1), (2, 3), (4,))
ND = 5


def where_am_i():
    aa, ba = lax.axis_index("aa"), lax.axis_index("ba")
    core, z = lax.rem(aa, 2), lax.rem(lax.div(aa, 2), 4)
    x = 2 * lax.div(aa, 8) + lax.rem(ba, 2)
    y = lax.div(ba, 2)
    return aa, ba, x, y, z, core


def place(x, y, z, core):
    aa = 8 * lax.div(x, 2) + 2 * z + core
    ba = 2 * y + lax.rem(x, 2)
    return aa, ba


def masks(step):
    low, high = step & 1, (step >> 1) & 1
    middle, top = (step >> 2) & 3, (step >> 4) & 3
    twice, thrice = ((low ^ high) << 1) | high, (low << 1) | (low ^ high)
    mz, my, mx, mc = step & 3, twice ^ middle, thrice ^ middle ^ top, (step ^ (step >> 6)) & 1
    return ((mx >> 1) << 3) | (mz << 1) | mc, (my << 1) | (mx & 1)


def total_wait(ref, sem):
    pltpu.make_async_copy(ref, ref, sem).wait()


def kernel(
    field, m1_hbm, m2_hbm, out,
    fbuf, tbuf, obuf, sbuf, rbuf, m1, m1t, m2, m2buf, m2t, cacc, cc, left, acc, fr, tr, pmat,
    fsem, wsem, send, recv, m2send, m2recv, m2sem, csend, crecv, gsend, grecv, osend, frecv, trecv, wsend, wrecv, *parts,
):
    gs, r1, s1, r2, s2, r3 = (parts[3 * n : 3 * n + 3] for n in range(6))
    aa, ba, x, y, z, core = where_am_i()
    tiles = fbuf.shape[0]
    sibling = {"aa": aa + 1 - 2 * core, "ba": ba}
    place_in_k = 8 * core + 4 * lax.div(x, 2) + z

    def load(tile, part):
        rows = pl.ds(256 * part, 256)
        return pltpu.make_async_copy(
            field.at[rows, pl.ds(JT * tile, JT), :], fbuf.at[tile, rows], fsem.at[tile, part]
        )

    load_m1 = pltpu.make_async_copy(m1_hbm, m1, wsem.at[0])
    load_m2 = pltpu.make_async_copy(m2_hbm, m2, wsem.at[1])
    load_m1.start()
    for part in range(4):
        load(0, part).start()
    load_m2.start()

    barrier = pltpu.get_barrier_semaphore()

    def greet(aa_mask, ba_mask):
        pl.semaphore_signal(
            barrier, inc=1, device_id={"aa": aa ^ aa_mask, "ba": ba ^ ba_mask}, device_id_type=MESH
        )

    for ba_mask in range(1, 8):
        greet(0, ba_mask)

    @pl.loop(1, 16)
    def _(aa_mask):
        for ba_mask in range(8):
            greet(aa_mask, ba_mask)

    for tile in range(1, tiles):
        for part in range(4):
            load(tile, part).start()

    row = lax.broadcasted_iota(jnp.int32, (256, 256), 0)
    col = lax.broadcasted_iota(jnp.int32, (256, 256), 1)
    swap = ((row & 15) * 16 + (row >> 4)) == col
    pmat[...] = jnp.where(swap, 1.0, 0.0).astype(BF)
    load_m1.wait()
    m1t[...] = m1[...].T

    def send_rows(tile, first, count, sem):
        rows = pl.ds(pl.multiple_of(JT * place_in_k, JT), JT)

        def block(to_aa, to_ba):
            mine = sbuf.at[tile, pl.ds(2 * (8 * to_aa + to_ba) + first, count)]
            return mine, rbuf.at[tile, pl.ds(first, count), ba, rows, :]

        @pl.loop(0, 128)
        def _(step):
            aa_mask, ba_mask = masks(step ^ (2 * core))
            to_aa, to_ba = aa ^ aa_mask, ba ^ ba_mask

            @pl.when((aa_mask | ba_mask) > 0)
            def _():
                mine, there = block(to_aa, to_ba)
                pltpu.make_async_remote_copy(
                    mine, there, send, sem, device_id={"aa": to_aa, "ba": to_ba}, device_id_type=MESH
                ).start()

        mine, there = block(aa, ba)
        pltpu.make_async_copy(mine, there, sem).start()

    @pl.loop(0, tiles)
    def _(tile):
        @pl.loop(0, 4)
        def _(part):
            load(tile, part).wait()

            @pl.loop(0, 8, unroll=4)
            def _(group):
                at = pl.multiple_of(256 * part + 32 * group, 32)
                left = fbuf[tile, pl.ds(at, 16)].reshape(256, 128)
                right = fbuf[tile, pl.ds(at + 16, 16)].reshape(256, 128)
                both = jnp.concatenate([left, right], axis=1)
                turned = jnp.dot(pmat[...], both, preferred_element_type=F32).astype(BF)
                tbuf[:, pl.ds(at, 16), :] = turned[:, :128].reshape(16, 16, 128)
                tbuf[:, pl.ds(pl.multiple_of(at + 16, 16), 16), :] = turned[:, 128:].reshape(16, 16, 128)

        @pl.loop(0, JT // 2)
        def _(pair):
            both = jnp.concatenate([tbuf[2 * pair], tbuf[2 * pair + 1]], axis=1)
            got = jnp.dot(m1t[...], both, preferred_element_type=F32).astype(BF)
            obuf[2 * pair] = got[:, :128]
            obuf[2 * pair + 1] = got[:, 128:]

        @pl.loop(0, 8, unroll=2)
        def _(group):
            at = pl.multiple_of(32 * group, 32)
            left = obuf[:, pl.ds(at, 16), :].reshape(256, 128)
            right = obuf[:, pl.ds(pl.multiple_of(at + 16, 16), 16), :].reshape(256, 128)
            both = jnp.concatenate([left, right], axis=1)
            turned = jnp.dot(pmat[...], both, preferred_element_type=F32).astype(BF)
            sbuf[tile, pl.ds(at, 16)] = turned[:, :128].reshape(16, 16, 128)
            sbuf[tile, pl.ds(at + 16, 16)] = turned[:, 128:].reshape(16, 16, 128)

        @pl.when(tile == 0)
        def _():
            pl.semaphore_wait(barrier, 127)

        @pl.when(tile < 3)
        def _():
            send_rows(tile, 0, 2, recv.at[tile])

        @pl.when(tile == 3)
        def _():
            for half in range(2):
                send_rows(tile, half, 1, recv.at[3 + half])

        @pl.when(tile == 1)
        def _():
            load_m2.wait()
            mine = m2buf.at[:, place_in_k]
            for mask in range(1, 8):
                to_aa, to_ba = place(x ^ (2 * (mask // 4)), y, z ^ (mask % 4), core)
                pltpu.make_async_remote_copy(
                    m2, mine, m2send, m2recv, device_id={"aa": to_aa, "ba": to_ba}, device_id_type=MESH
                ).start()
            pltpu.make_async_copy(m2, mine, m2recv).start()

    half_of_m2 = m2buf.at[:, pl.ds(8 * core, 8)]
    total_wait(half_of_m2, m2recv)
    pass_m2 = pltpu.make_async_remote_copy(
        half_of_m2, half_of_m2, m2sem.at[0], m2sem.at[1], device_id=sibling, device_id_type=MESH
    )
    pass_m2.start()
    pass_m2.wait()
    for tile in range(4):
        m2t[tile] = m2buf[tile].reshape(256, 256).T

    def share(half, pair):
        blocks = pl.ds(2 * pair, 2)
        return pltpu.make_async_remote_copy(
            cc.at[blocks, pl.ds(256 * half, 256), :], cc.at[blocks, pl.ds(512 + 256 * half, 256), :],
            csend.at[half, pair], crecv.at[half, pair], device_id=sibling, device_id_type=MESH,
        )

    for tile in range(4):
        if tile < 3:
            total_wait(rbuf.at[tile], recv.at[tile])
        for half in range(2):
            if tile == 3:
                total_wait(rbuf.at[tile, half], recv.at[3 + half])

            @pl.loop(0, 4, unroll=2)
            def _(pair):
                both = jnp.concatenate([rbuf[tile, half, 2 * pair], rbuf[tile, half, 2 * pair + 1]], axis=1)
                got = jnp.dot(m2t[tile], both, preferred_element_type=F32)
                if tile > 0:
                    got += cacc[half, pair]
                if tile < 3:
                    cacc[half, pair] = got
                else:
                    cc[2 * pair, pl.ds(256 * half, 256), :] = got[:, :128].astype(BF)
                    cc[2 * pair + 1, pl.ds(256 * half, 256), :] = got[:, 128:].astype(BF)
                    share(half, pair).start()

    where = (x, y, z)

    def term(rows_of_k, left, block_row, columns):
        right = jnp.concatenate([cc[lax.rem(block_row + d, 8), rows_of_k, :] for d in columns], axis=1)
        return jnp.dot(left, right, preferred_element_type=F32)

    def pieces(got, low_y, low_x, k):
        for octet in range(16):
            owner = (2 * (octet >> 3) + low_x, 2 * (octet & 1) + low_y, (octet >> 1) & 3)
            index = tuple(owner[(k + stage) % 3] for stage in range(3))
            for n in range(len(CLASSES[k])):
                yield gs[k], index + (n,), got[8 * octet : 8 * octet + 8, 128 * n : 128 * n + 128]

    own_k, their_k = pl.ds(0, 512), pl.ds(512, 512)
    for low_y in range(2):
        for low_x in range(2):
            block_row = 4 * core + 2 * low_y + low_x
            got = term(own_k, cc[block_row, own_k, :].T, block_row, range(ND))
            for k, columns in enumerate(CLASSES):
                part = got[:, 128 * columns[0] : 128 * columns[-1] + 128]
                for ref, index, value in pieces(part, low_y, low_x, k):
                    ref[index] = value
    for half in range(2):
        for pair in range(4):
            share(half, pair).wait()

    def scatter(k, stage):
        axis = (k + stage) % 3
        for mask in range(1, 4):
            there = [x, y, z]
            there[axis] = there[axis] ^ mask
            to_aa, to_ba = place(*there, core)
            pltpu.make_async_remote_copy(
                sums[stage][k].at[where[axis] ^ mask], got_from[stage][k].at[mask - 1], gsend, grecv.at[k, stage],
                device_id={"aa": to_aa, "ba": to_ba}, device_id_type=MESH,
            ).start()

    def gathered(k, stage):
        total_wait(got_from[stage][k], grecv.at[k, stage])
        got = got_from[stage][k]
        return sums[stage][k][where[(k + stage) % 3]] + got[0] + got[1] + got[2]

    sums = (gs, s1, s2)
    got_from = (r1, r2, r3)
    for low_y in range(2):
        for low_x in range(2):
            left[2 * low_y + low_x] = cc[4 * core + 2 * low_y + low_x, their_k, :].T
    for k, columns in enumerate(CLASSES):
        for low_y in range(2):
            for low_x in range(2):
                got = term(their_k, left[2 * low_y + low_x], 4 * core + 2 * low_y + low_x, columns)
                for ref, index, value in pieces(got, low_y, low_x, k):
                    ref[index] += value
        scatter(k, 0)
    for stage in range(2):
        for k in range(3):
            sums[stage + 1][k][...] = gathered(k, stage)
            scatter(k, stage + 1)
    for k, columns in enumerate(CLASSES):
        acc[pl.ds(columns[0], len(columns))] = gathered(k, 2) * (1.0 / 65536.0)

    mine = 4 * core + 2 * lax.rem(y, 2) + lax.rem(x, 2)
    own = pl.ds(pl.multiple_of(8 * (8 * lax.div(x, 2) + 2 * z + lax.div(y, 2)), 8), 8)
    inside = jnp.logical_and(mine == ba, lax.div(x, 2) == core)

    taker = lax.div(x, 2)

    @pl.loop(0, 8)
    def _(step):
        to_aa = (aa ^ (2 * step) ^ core) | taker
        self = jnp.logical_and(inside, step == 0)

        @pl.when(self)
        def _():
            pltpu.make_async_copy(acc, fr.at[:, own, :], frecv).start()

        @pl.when(jnp.logical_not(self))
        def _():
            pltpu.make_async_remote_copy(
                acc, fr.at[:, own, :], osend, frecv,
                device_id={"aa": to_aa, "ba": mine}, device_id_type=MESH,
            ).start()

        for d in range(1, 4):
            pltpu.make_async_remote_copy(
                acc.at[d], tr.at[d - 1, own, :], osend, trecv,
                device_id={"aa": to_aa, "ba": lax.rem(mine + d, 8)}, device_id_type=MESH,
            ).start()

    half = pl.ds(pl.multiple_of(64 * core, 64), 64)
    swaps = []
    for n, (ref, sem) in enumerate(((fr, frecv), (tr, trecv))):
        total_wait(ref.at[:, half, :], sem)
        swaps.append(pltpu.make_async_remote_copy(
            ref.at[:, half, :], ref.at[:, half, :], wsend.at[n], wrecv.at[n],
            device_id=sibling, device_id_type=MESH,
        ))
        swaps[n].start()

    swaps[0].wait()
    for d in range(ND):
        out[:, pl.ds(pl.multiple_of(128 * lax.rem(ba + d, 8), 128), 128)] = fr[d]
    swaps[1].wait()
    for d in range(1, 4):
        out[:, pl.ds(pl.multiple_of(128 * lax.rem(ba + 8 - d, 8), 128), 128)] = tr[d - 1].T

    total_wait(sbuf.at[:, pl.ds(0, 254)], send)
    total_wait(m2buf.at[:, pl.ds(0, 7)], m2send)
    for stage in range(3):
        for k in range(3):
            total_wait(got_from[stage][k], gsend)
    total_wait(fr.at[:, pl.ds(0, 56), :], osend)

    @pl.when(jnp.logical_not(inside))
    def _():
        total_wait(fr.at[:, pl.ds(0, 8), :], osend)

    total_wait(tr.at[:, pl.ds(0, 64), :], osend)


def shards(field, mode_one, mode_two):
    dma = pltpu.SemaphoreType.DMA
    hbm = pl.BlockSpec(memory_space=pltpu.HBM)
    return pl.pallas_call(
        kernel,
        out_shape=jax.ShapeDtypeStruct((128, 1024), F32),
        in_specs=[hbm, hbm, hbm],
        out_specs=pl.BlockSpec(memory_space=pltpu.VMEM),
        scratch_shapes=[
            pltpu.VMEM((4, 1024, JT, 128), BF),
            pltpu.VMEM((JT, 1024, 128), BF),
            pltpu.VMEM((JT, 256, 128), BF),
            pltpu.VMEM((4, 256, JT, 128), BF),
            pltpu.VMEM((4, 2, 8, 256, 128), BF),
            pltpu.VMEM((1024, 256), BF),
            pltpu.VMEM((256, 1024), BF),
            pltpu.VMEM((4, JT, 256), BF),
            pltpu.VMEM((4, 16, JT, 256), BF),
            pltpu.VMEM((4, 256, 256), BF),
            pltpu.VMEM((2, 4, 256, 256), F32),
            pltpu.VMEM((8, 1024, 128), BF),
            pltpu.VMEM((4, 128, 512), BF),
            pltpu.VMEM((ND, 8, 128), F32),
            pltpu.VMEM((ND, 128, 128), F32),
            pltpu.VMEM((3, 128, 128), F32),
            pltpu.VMEM((256, 256), BF),
            dma((4, 4)), dma((2,)),
            dma, dma((5,)), dma, dma, dma((2,)),
            dma((2, 4)), dma((2, 4)),
            dma, dma((3, 3)), dma, dma, dma, dma((2,)), dma((2,)),
            *[
                pltpu.VMEM(shape + (len(columns), 8, 128), F32)
                for shape in ((4, 4, 4), (3, 4, 4), (4, 4), (3, 4), (4,), (3,))
                for columns in CLASSES
            ],
        ],
        compiler_params=pltpu.CompilerParams(
            collective_id=0, has_side_effects=True, vmem_limit_bytes=53 * 1024 * 1024
        ),
        cost_estimate=pl.CostEstimate(flops=13_000_000_000, bytes_accessed=18_000_000, transcendentals=0),
    )(field, mode_one, mode_two.reshape(4, JT, 256))


def solution(mesh):
    in_specs = (P(None, "aa", "ba"), P(), P("aa", None))
    return jax.shard_map(shards, mesh=mesh, in_specs=in_specs, out_specs=P("ba", None), check_vma=False)
```

```python
import functools

import jax
import jax.numpy as jnp
from jax import lax
from jax.experimental import pallas as pl
from jax.experimental.pallas import tpu as pltpu
from jax.sharding import PartitionSpec as P

BF, F32 = jnp.bfloat16, jnp.float32
MESH = pl.DeviceIdType.MESH
JT = 16
CLASSES = ((0, 1), (2, 3), (4,))
ND = 5


def where_am_i():
    aa, ba = lax.axis_index("aa"), lax.axis_index("ba")
    core, z = lax.rem(aa, 2), lax.rem(lax.div(aa, 2), 4)
    x = 2 * lax.div(aa, 8) + lax.rem(ba, 2)
    y = lax.div(ba, 2)
    return aa, ba, x, y, z, core


def place(x, y, z, core):
    aa = 8 * lax.div(x, 2) + 2 * z + core
    ba = 2 * y + lax.rem(x, 2)
    return aa, ba


def total_wait(ref, sem):
    pltpu.make_async_copy(ref, ref, sem).wait()


def kernel(
    field, m1_hbm, m2_hbm, out,
    fbuf, wide, obuf, sbuf, rbuf, m1, m1t, m2, m2buf, m2t, cacc, cc, left, acc, fr, tr,
    fsem, wsem, send, recv, m2send, m2recv, m2sem, csend, crecv, gsend, grecv, osend, frecv, trecv, wsend, wrecv, *parts,
):
    gs, r1, s1, r2, s2, r3 = (parts[3 * n : 3 * n + 3] for n in range(6))
    aa, ba, x, y, z, core = where_am_i()
    tiles = fbuf.shape[0]
    me = 8 * aa + ba
    sibling = {"aa": aa + 1 - 2 * core, "ba": ba}
    place_in_k = 8 * core + 4 * lax.div(x, 2) + z

    def load(tile, part):
        rows = pl.ds(256 * part, 256)
        return pltpu.make_async_copy(
            field.at[rows, pl.ds(JT * tile, JT), :], fbuf.at[tile, rows], fsem.at[tile, part]
        )

    load_m1 = pltpu.make_async_copy(m1_hbm, m1, wsem.at[0])
    load_m2 = pltpu.make_async_copy(m2_hbm, m2, wsem.at[1])
    load_m1.start()
    for part in range(4):
        load(0, part).start()
    load_m2.start()

    barrier = pltpu.get_barrier_semaphore()

    def greet(aa_mask, ba_mask):
        pl.semaphore_signal(
            barrier, inc=1, device_id={"aa": aa ^ aa_mask, "ba": ba ^ ba_mask}, device_id_type=MESH
        )

    for ba_mask in range(1, 8):
        greet(0, ba_mask)

    @pl.loop(1, 16)
    def _(aa_mask):
        for ba_mask in range(8):
            greet(aa_mask, ba_mask)

    for tile in range(1, tiles):
        for part in range(4):
            load(tile, part).start()

    load_m1.wait()
    m1t[...] = m1[...].T

    def send_rows(tile, first, count, sem):
        rows = pl.ds(pl.multiple_of(JT * place_in_k, JT), JT)

        def block(to):
            mine = sbuf.at[tile, pl.ds(2 * to + first, count)]
            return mine, rbuf.at[tile, pl.ds(first, count), ba, rows, :]

        def start(step):
            to = me ^ ((37 * step) & 127)
            mine, there = block(to)
            pltpu.make_async_remote_copy(
                mine, there, send, sem, device_id={"aa": to >> 3, "ba": to & 7}, device_id_type=MESH
            ).start()

        for step in range(1, 8):
            start(step)
        pl.loop(1, 16)(lambda turn: [start(8 * turn + step) for step in range(8)] and None)

        mine, there = block(me)
        pltpu.make_async_copy(mine, there, sem).start()

    @pl.loop(0, tiles)
    def _(tile):
        @pl.loop(0, 4)
        def _(part):
            load(tile, part).wait()

            @pl.loop(0, 32, unroll=4)
            def _(group):
                at = 256 * part + 8 * group
                wide[pl.ds(pl.multiple_of(JT * at, 128), 128), :] = (
                    fbuf[tile, pl.ds(at, 8)].reshape(128, 128).astype(F32)
                )

        @pl.loop(0, JT // 2)
        def _(pair):
            both = jnp.concatenate(
                [wide[pl.ds(2 * pair + n, 1024, stride=JT), :] for n in range(2)], axis=1
            ).astype(BF)
            got = jnp.dot(m1t[...], both, preferred_element_type=F32)
            for n in range(2):
                obuf[pl.ds(pl.multiple_of(512 * pair + 256 * n, 256), 256), :] = got[:, 128 * n : 128 * n + 128]

        @pl.loop(0, 256, unroll=8)
        def _(r):
            sbuf[tile, r] = obuf[pl.ds(r, JT, stride=256), :].astype(BF)

        @pl.when(tile == 0)
        def _():
            pl.semaphore_wait(barrier, 127)

        @pl.when(tile < 3)
        def _():
            send_rows(tile, 0, 2, recv.at[tile])

        @pl.when(tile == 3)
        def _():
            for half in range(2):
                send_rows(tile, half, 1, recv.at[3 + half])

        @pl.when(tile == 1)
        def _():
            load_m2.wait()
            mine = m2buf.at[:, place_in_k]
            for mask in range(1, 8):
                to_aa, to_ba = place(x ^ (2 * (mask // 4)), y, z ^ (mask % 4), core)
                pltpu.make_async_remote_copy(
                    m2, mine, m2send, m2recv, device_id={"aa": to_aa, "ba": to_ba}, device_id_type=MESH
                ).start()
            pltpu.make_async_copy(m2, mine, m2recv).start()

    half_of_m2 = m2buf.at[:, pl.ds(8 * core, 8)]
    total_wait(half_of_m2, m2recv)
    pass_m2 = pltpu.make_async_remote_copy(
        half_of_m2, half_of_m2, m2sem.at[0], m2sem.at[1], device_id=sibling, device_id_type=MESH
    )
    pass_m2.start()
    pass_m2.wait()
    for tile in range(4):
        m2t[tile] = m2buf[tile].reshape(256, 256).T

    def share(half, pair):
        blocks = pl.ds(2 * pair, 2)
        return pltpu.make_async_remote_copy(
            cc.at[blocks, pl.ds(256 * half, 256), :], cc.at[blocks, pl.ds(512 + 256 * half, 256), :],
            csend.at[half, pair], crecv.at[half, pair], device_id=sibling, device_id_type=MESH,
        )

    for tile in range(4):
        if tile < 3:
            total_wait(rbuf.at[tile], recv.at[tile])
        for half in range(2):
            if tile == 3:
                total_wait(rbuf.at[tile, half], recv.at[3 + half])

            @pl.loop(0, 4, unroll=2)
            def _(pair):
                both = jnp.concatenate([rbuf[tile, half, 2 * pair], rbuf[tile, half, 2 * pair + 1]], axis=1)
                got = jnp.dot(m2t[tile], both, preferred_element_type=F32)
                if tile > 0:
                    got += cacc[half, pair]
                if tile < 3:
                    cacc[half, pair] = got
                else:
                    cc[2 * pair, pl.ds(256 * half, 256), :] = got[:, :128].astype(BF)
                    cc[2 * pair + 1, pl.ds(256 * half, 256), :] = got[:, 128:].astype(BF)
                    share(half, pair).start()

    where = (x, y, z)

    def term(rows_of_k, left, block_row, columns):
        right = jnp.concatenate([cc[lax.rem(block_row + d, 8), rows_of_k, :] for d in columns], axis=1)
        return jnp.dot(left, right, preferred_element_type=F32)

    def pieces(got, low_y, low_x, k):
        for octet in range(16):
            owner = (2 * (octet >> 3) + low_x, 2 * (octet & 1) + low_y, (octet >> 1) & 3)
            index = tuple(owner[(k + stage) % 3] for stage in range(3))
            for n in range(len(CLASSES[k])):
                yield gs[k], index + (n,), got[8 * octet : 8 * octet + 8, 128 * n : 128 * n + 128]

    own_k, their_k = pl.ds(0, 512), pl.ds(512, 512)
    for low_y in range(2):
        for low_x in range(2):
            block_row = 4 * core + 2 * low_y + low_x
            got = term(own_k, cc[block_row, own_k, :].T, block_row, range(ND))
            for k, columns in enumerate(CLASSES):
                part = got[:, 128 * columns[0] : 128 * columns[-1] + 128]
                for ref, index, value in pieces(part, low_y, low_x, k):
                    ref[index] = value
    for half in range(2):
        for pair in range(4):
            share(half, pair).wait()

    def scatter(k, stage):
        axis = (k + stage) % 3
        for mask in range(1, 4):
            there = [x, y, z]
            there[axis] = there[axis] ^ mask
            to_aa, to_ba = place(*there, core)
            pltpu.make_async_remote_copy(
                sums[stage][k].at[where[axis] ^ mask], got_from[stage][k].at[mask - 1], gsend, grecv.at[k, stage],
                device_id={"aa": to_aa, "ba": to_ba}, device_id_type=MESH,
            ).start()

    def gathered(k, stage):
        total_wait(got_from[stage][k], grecv.at[k, stage])
        got = got_from[stage][k]
        return sums[stage][k][where[(k + stage) % 3]] + got[0] + got[1] + got[2]

    sums = (gs, s1, s2)
    got_from = (r1, r2, r3)
    for low_y in range(2):
        for low_x in range(2):
            left[2 * low_y + low_x] = cc[4 * core + 2 * low_y + low_x, their_k, :].T
    for k, columns in enumerate(CLASSES):
        for low_y in range(2):
            for low_x in range(2):
                got = term(their_k, left[2 * low_y + low_x], 4 * core + 2 * low_y + low_x, columns)
                for ref, index, value in pieces(got, low_y, low_x, k):
                    ref[index] += value
        scatter(k, 0)
    for stage in range(2):
        for k in range(3):
            sums[stage + 1][k][...] = gathered(k, stage)
            scatter(k, stage + 1)
    for k, columns in enumerate(CLASSES):
        acc[pl.ds(columns[0], len(columns))] = gathered(k, 2) * (1.0 / 65536.0)

    mine = 4 * core + 2 * lax.rem(y, 2) + lax.rem(x, 2)
    own = pl.ds(pl.multiple_of(8 * (8 * lax.div(x, 2) + 2 * z + lax.div(y, 2)), 8), 8)
    inside = jnp.logical_and(mine == ba, lax.div(x, 2) == core)

    taker = lax.div(x, 2)

    @pl.loop(0, 8)
    def _(step):
        to_aa = (aa ^ (2 * step) ^ core) | taker
        self = jnp.logical_and(inside, step == 0)

        @pl.when(self)
        def _():
            pltpu.make_async_copy(acc, fr.at[:, own, :], frecv).start()

        @pl.when(jnp.logical_not(self))
        def _():
            pltpu.make_async_remote_copy(
                acc, fr.at[:, own, :], osend, frecv,
                device_id={"aa": to_aa, "ba": mine}, device_id_type=MESH,
            ).start()

        for d in range(1, 4):
            pltpu.make_async_remote_copy(
                acc.at[d], tr.at[d - 1, own, :], osend, trecv,
                device_id={"aa": to_aa, "ba": lax.rem(mine + d, 8)}, device_id_type=MESH,
            ).start()

    half = pl.ds(pl.multiple_of(64 * core, 64), 64)
    swaps = []
    for n, (ref, sem) in enumerate(((fr, frecv), (tr, trecv))):
        total_wait(ref.at[:, half, :], sem)
        swaps.append(pltpu.make_async_remote_copy(
            ref.at[:, half, :], ref.at[:, half, :], wsend.at[n], wrecv.at[n],
            device_id=sibling, device_id_type=MESH,
        ))
        swaps[n].start()

    swaps[0].wait()
    for d in range(ND):
        out[:, pl.ds(pl.multiple_of(128 * lax.rem(ba + d, 8), 128), 128)] = fr[d]
    swaps[1].wait()
    for d in range(1, 4):
        out[:, pl.ds(pl.multiple_of(128 * lax.rem(ba + 8 - d, 8), 128), 128)] = tr[d - 1].T

    total_wait(sbuf.at[:, pl.ds(0, 254)], send)
    total_wait(m2buf.at[:, pl.ds(0, 7)], m2send)
    for stage in range(3):
        for k in range(3):
            total_wait(got_from[stage][k], gsend)
    total_wait(fr.at[:, pl.ds(0, 56), :], osend)

    @pl.when(jnp.logical_not(inside))
    def _():
        total_wait(fr.at[:, pl.ds(0, 8), :], osend)

    total_wait(tr.at[:, pl.ds(0, 64), :], osend)


def shards(field, mode_one, mode_two):
    dma = pltpu.SemaphoreType.DMA
    hbm = pl.BlockSpec(memory_space=pltpu.HBM)
    return pl.pallas_call(
        kernel,
        out_shape=jax.ShapeDtypeStruct((128, 1024), F32),
        in_specs=[hbm, hbm, hbm],
        out_specs=pl.BlockSpec(memory_space=pltpu.VMEM),
        scratch_shapes=[
            pltpu.VMEM((4, 1024, JT, 128), BF),
            pltpu.VMEM((1024 * JT, 128), F32),
            pltpu.VMEM((JT * 256, 128), F32),
            pltpu.VMEM((4, 256, JT, 128), BF),
            pltpu.VMEM((4, 2, 8, 256, 128), BF),
            pltpu.VMEM((1024, 256), BF),
            pltpu.VMEM((256, 1024), BF),
            pltpu.VMEM((4, JT, 256), BF),
            pltpu.VMEM((4, 16, JT, 256), BF),
            pltpu.VMEM((4, 256, 256), BF),
            pltpu.VMEM((2, 4, 256, 256), F32),
            pltpu.VMEM((8, 1024, 128), BF),
            pltpu.VMEM((4, 128, 512), BF),
            pltpu.VMEM((ND, 8, 128), F32),
            pltpu.VMEM((ND, 128, 128), F32),
            pltpu.VMEM((3, 128, 128), F32),
            dma((4, 4)), dma((2,)),
            dma, dma((5,)), dma, dma, dma((2,)),
            dma((2, 4)), dma((2, 4)),
            dma, dma((3, 3)), dma, dma, dma, dma((2,)), dma((2,)),
            *[
                pltpu.VMEM(shape + (len(columns), 8, 128), F32)
                for shape in ((4, 4, 4), (3, 4, 4), (4, 4), (3, 4), (4,), (3,))
                for columns in CLASSES
            ],
        ],
        compiler_params=pltpu.CompilerParams(
            collective_id=0, has_side_effects=True, vmem_limit_bytes=53 * 1024 * 1024
        ),
        cost_estimate=pl.CostEstimate(flops=13_000_000_000, bytes_accessed=18_000_000, transcendentals=0),
    )(field, mode_one, mode_two.reshape(4, JT, 256))


def solution(mesh):
    in_specs = (P(None, "aa", "ba"), P(), P("aa", None))
    return jax.shard_map(shards, mesh=mesh, in_specs=in_specs, out_specs=P("ba", None), check_vma=False)
```

```python
import functools

import jax
import jax.numpy as jnp
from jax import lax
from jax.experimental import pallas as pl
from jax.experimental.pallas import tpu as pltpu
from jax.sharding import PartitionSpec as P

BF, F32 = jnp.bfloat16, jnp.float32
MESH = pl.DeviceIdType.MESH
JT = 16
CLASSES = ((0, 1), (2, 3), (4,))
ND = 5


def where_am_i():
    aa, ba = lax.axis_index("aa"), lax.axis_index("ba")
    core, z = lax.rem(aa, 2), lax.rem(lax.div(aa, 2), 4)
    x = 2 * lax.div(aa, 8) + lax.rem(ba, 2)
    y = lax.div(ba, 2)
    return aa, ba, x, y, z, core


def place(x, y, z, core):
    aa = 8 * lax.div(x, 2) + 2 * z + core
    ba = 2 * y + lax.rem(x, 2)
    return aa, ba


JOBS = 16
READY = (0, 1, 2, 3)
GAP = 2
FIRST = tuple(n % 3 for n in range(JOBS))


def job(rel, rr, tile):
    return 4 * tile + 2 * rel + rr


def timetable():
    step, free, slots = [0] * JOBS, [READY[n // 4] for n in range(JOBS)], []
    while min(step) < 3:
        now, taken = len(slots), {}
        for n in sorted(range(JOBS), key=lambda n: (step[n] - n // 4, n)):
            axis = (FIRST[n] + step[n]) % 3
            if step[n] < 3 and free[n] <= now and axis not in taken:
                taken[axis] = n
        slots.append([(n, step[n]) for n in sorted(taken.values())])
        for n in taken.values():
            step[n] += 1
            free[n] = now + GAP
    return slots


def in_order(n, triple):
    return tuple(triple[(FIRST[n] + step) % 3] for step in range(3))


def total_wait(ref, sem):
    pltpu.make_async_copy(ref, ref, sem).wait()


def kernel(
    field, m1_hbm, m2_hbm, out,
    fbuf, wide, obuf, orig, r_one, r_two, r_three, staging, m1, m1t, m2, m2buf, m2t, cacc, cc, left, acc, fr, tr,
    fsem, wsem, send, recv, ssend, srecv, m2send, m2recv, m2sem, csend, crecv, gsend, grecv, osend, frecv, trecv, wsend, wrecv, *parts,
):
    gs, r1, s1, r2, s2, r3 = (parts[3 * n : 3 * n + 3] for n in range(6))
    aa, ba, x, y, z, core = where_am_i()
    sibling = {"aa": aa + 1 - 2 * core, "ba": ba}
    rounds = (r_one, r_two, r_three)

    def load(tile, part):
        rows = pl.ds(256 * part, 256)
        return pltpu.make_async_copy(
            field.at[rows, pl.ds(JT * tile, JT), :], fbuf.at[tile % 3, rows], fsem.at[tile, part]
        )

    load_m1 = pltpu.make_async_copy(m1_hbm, m1, wsem.at[0])
    load_m2 = pltpu.make_async_copy(m2_hbm, m2, wsem.at[1])
    load_m1.start()
    for part in range(4):
        load(0, part).start()
    load_m2.start()

    barrier = pltpu.get_barrier_semaphore()

    def greet(aa_mask, ba_mask):
        pl.semaphore_signal(
            barrier, inc=1, device_id={"aa": aa ^ aa_mask, "ba": ba ^ ba_mask}, device_id_type=MESH
        )

    for ba_mask in range(1, 8):
        greet(0, ba_mask)

    @pl.loop(1, 16)
    def _(aa_mask):
        for ba_mask in range(8):
            greet(aa_mask, ba_mask)

    for tile in range(1, 3):
        for part in range(4):
            load(tile, part).start()

    load_m1.wait()
    m1t[...] = m1[...].T

    def widen(tile):
        @pl.loop(0, 4)
        def _(part):
            load(tile, part).wait()

            @pl.loop(0, 32, unroll=4)
            def _(group):
                at = 256 * part + 8 * group
                wide[pl.ds(pl.multiple_of(JT * at, 128), 128), :] = (
                    fbuf[tile % 3, pl.ds(at, 8)].reshape(128, 128).astype(F32)
                )

        if tile == 0:
            for part in range(4):
                load(3, part).start()

    def contract(tile):
        @pl.loop(0, JT // 2)
        def _(pair):
            both = jnp.concatenate(
                [wide[pl.ds(2 * pair + n, 1024, stride=JT), :] for n in range(2)], axis=1
            ).astype(BF)
            got = jnp.dot(m1t[...], both, preferred_element_type=F32)
            for n in range(2):
                obuf[pl.ds(pl.multiple_of(512 * pair + 256 * n, 256), 256), :] = got[:, 128 * n : 128 * n + 128]

        @pl.loop(0, 64, unroll=4)
        def _(slot):
            masks = (slot >> 4, (slot >> 2) & 3, slot & 3)
            row = 2 * (16 * (x ^ masks[0]) + 4 * (y ^ masks[1]) + (z ^ masks[2]))
            for rr in range(2):
                n = job(0, rr, tile)
                orig[(n,) + in_order(n, masks)] = obuf[pl.ds(row + 128 * core + rr, JT, stride=256), :].astype(BF)
                n = job(1, rr, tile)
                staging[(tile, rr) + in_order(n, masks)] = (
                    obuf[pl.ds(row + 128 * (1 - core) + rr, JT, stride=256), :].astype(BF)
                )

    def hand_over(tile, rr):
        return pltpu.make_async_remote_copy(
            staging.at[tile, rr], orig.at[job(1, rr, tile)], ssend.at[tile, rr], srecv.at[tile, rr],
            device_id=sibling, device_id_type=MESH,
        )

    def exchange(n, step):
        if step > 0:
            total_wait(rounds[step - 1].at[n], recv.at[n, step - 1])
        elif (n // 2) % 2 == 1:
            hand_over(n // 4, n % 2).wait_recv()
        axis = (FIRST[n] + step) % 3
        after = pl.ds(1, 3)
        for mask in range(1, 4):
            there = [x, y, z]
            there[axis] = there[axis] ^ mask
            to_aa, to_ba = place(*there, core)
            if step == 0:
                pieces = [(orig.at[n, mask], r_one.at[n, mask - 1])]
            elif step == 1:
                pieces = [
                    (r_one.at[n, :, mask], r_two.at[n, mask - 1, after]),
                    (orig.at[n, 0, mask], r_two.at[n, mask - 1, 0]),
                ]
            else:
                pieces = [
                    (r_two.at[n, :, :, mask], r_three.at[n, mask - 1, after]),
                    (r_one.at[n, :, 0, mask], r_three.at[n, mask - 1, 0, after]),
                    (orig.at[n, 0, 0, mask], r_three.at[n, mask - 1, 0, 0]),
                ]
            for mine, target in pieces:
                pltpu.make_async_remote_copy(
                    mine, target, send, recv.at[n, step],
                    device_id={"aa": to_aa, "ba": to_ba}, device_id_type=MESH,
                ).start()

    def block(n, masks):
        one, two, three = in_order(n, masks)
        if three:
            return r_three[n, three - 1, two, one]
        if two:
            return r_two[n, two - 1, one, 0]
        if one:
            return r_one[n, one - 1, 0, 0]
        return orig[n, 0, 0, 0]

    def spread_m2():
        load_m2.wait()
        for mask in range(1, 8):
            to_aa, to_ba = place(x ^ (2 * (mask // 4)), y, z ^ (mask % 4), core)
            pltpu.make_async_remote_copy(
                m2, m2buf.at[:, mask], m2send, m2recv,
                device_id={"aa": to_aa, "ba": to_ba}, device_id_type=MESH,
            ).start()
        pltpu.make_async_copy(m2, m2buf.at[:, 0], m2recv).start()

    def pass_m2():
        return pltpu.make_async_remote_copy(
            m2buf.at[:, pl.ds(0, 8)], m2buf.at[:, pl.ds(8, 8)], m2sem.at[0], m2sem.at[1],
            device_id=sibling, device_id_type=MESH,
        )

    def share(half, pair):
        blocks = pl.ds(2 * pair, 2)
        return pltpu.make_async_remote_copy(
            cc.at[blocks, pl.ds(256 * half, 256), :], cc.at[blocks, pl.ds(512 + 256 * half, 256), :],
            csend.at[half, pair], crecv.at[half, pair], device_id=sibling, device_id_type=MESH,
        )

    done = [0, 0]

    def add_core(rr, tile):
        for rel in range(2):
            n = job(rel, rr, tile)
            total_wait(r_three.at[n], recv.at[n, 2])
        for y_mask in range(4):
            both = jnp.concatenate([
                jnp.concatenate([
                    block(job(rel, rr, tile), (2 * high + low, y_mask, z_mask))
                    for rel in range(2) for high in range(2) for z_mask in range(4)
                ], axis=0) for low in range(2)
            ], axis=1)
            got = jnp.dot(m2t[tile], both, preferred_element_type=F32)
            if done[rr] > 0:
                got += cacc[rr, y_mask]
            if done[rr] < 3:
                cacc[rr, y_mask] = got
            else:
                for low in range(2):
                    source = 2 * (y ^ y_mask) + (lax.rem(x, 2) ^ low)
                    cc[source, pl.ds(256 * rr, 256), :] = got[:, 128 * low : 128 * low + 128].astype(BF)
                share(rr, y ^ y_mask).start()
        done[rr] += 1

    slots = timetable()
    finished = {n: now for now, slot in enumerate(slots) for n, step in slot if step == 2}
    pairs = sorted(
        (max(finished[job(rel, rr, tile)] for rel in range(2)), rr, tile) for rr in range(2) for tile in range(4)
    )

    for tile in range(4):
        widen(tile)
        contract(tile)
        if tile == 0:
            pl.semaphore_wait(barrier, 127)
        for rr in range(2):
            hand_over(tile, rr).start()
        last = READY[tile + 1] if tile < 3 else 6
        for now in range(READY[tile], last):
            for n, step in slots[now]:
                exchange(n, step)
        if tile == 1:
            spread_m2()
    total_wait(m2buf.at[:, pl.ds(0, 8)], m2recv)
    pass_m2().start()
    for now in range(6, len(slots)):
        for n, step in slots[now]:
            exchange(n, step)
        if now == 7:
            pass_m2().wait()
            for tile in range(4):
                m2t[tile] = m2buf[tile].reshape(256, 256).T
        while now >= 8 and pairs and pairs[0][0] <= now - GAP:
            _, rr, tile = pairs.pop(0)
            add_core(rr, tile)
    for _, rr, tile in pairs:
        add_core(rr, tile)

    where = (x, y, z)

    def term(rows_of_k, left, block_row, columns):
        right = jnp.concatenate([cc[lax.rem(block_row + d, 8), rows_of_k, :] for d in columns], axis=1)
        return jnp.dot(left, right, preferred_element_type=F32)

    def pieces(got, low_y, low_x, k):
        for octet in range(16):
            owner = (2 * (octet >> 3) + low_x, 2 * (octet & 1) + low_y, (octet >> 1) & 3)
            index = tuple(owner[(k + stage) % 3] for stage in range(3))
            for n in range(len(CLASSES[k])):
                yield gs[k], index + (n,), got[8 * octet : 8 * octet + 8, 128 * n : 128 * n + 128]

    own_k, their_k = pl.ds(0, 512), pl.ds(512, 512)
    for low_y in range(2):
        for low_x in range(2):
            block_row = 4 * core + 2 * low_y + low_x
            got = term(own_k, cc[block_row, own_k, :].T, block_row, range(ND))
            for k, columns in enumerate(CLASSES):
                part = got[:, 128 * columns[0] : 128 * columns[-1] + 128]
                for ref, index, value in pieces(part, low_y, low_x, k):
                    ref[index] = value
    for half in range(2):
        for pair in range(4):
            share(half, pair).wait()

    def scatter(k, stage):
        axis = (k + stage) % 3
        for mask in range(1, 4):
            there = [x, y, z]
            there[axis] = there[axis] ^ mask
            to_aa, to_ba = place(*there, core)
            pltpu.make_async_remote_copy(
                sums[stage][k].at[where[axis] ^ mask], got_from[stage][k].at[mask - 1], gsend, grecv.at[k, stage],
                device_id={"aa": to_aa, "ba": to_ba}, device_id_type=MESH,
            ).start()

    def gathered(k, stage):
        total_wait(got_from[stage][k], grecv.at[k, stage])
        got = got_from[stage][k]
        return sums[stage][k][where[(k + stage) % 3]] + got[0] + got[1] + got[2]

    sums = (gs, s1, s2)
    got_from = (r1, r2, r3)
    for low_y in range(2):
        for low_x in range(2):
            left[2 * low_y + low_x] = cc[4 * core + 2 * low_y + low_x, their_k, :].T
    for k, columns in enumerate(CLASSES):
        for low_y in range(2):
            for low_x in range(2):
                got = term(their_k, left[2 * low_y + low_x], 4 * core + 2 * low_y + low_x, columns)
                for ref, index, value in pieces(got, low_y, low_x, k):
                    ref[index] += value
        scatter(k, 0)
    for stage in range(2):
        for k in range(3):
            sums[stage + 1][k][...] = gathered(k, stage)
            scatter(k, stage + 1)
    for k, columns in enumerate(CLASSES):
        acc[pl.ds(columns[0], len(columns))] = gathered(k, 2) * (1.0 / 65536.0)

    mine = 4 * core + 2 * lax.rem(y, 2) + lax.rem(x, 2)
    own = pl.ds(pl.multiple_of(8 * (8 * lax.div(x, 2) + 2 * z + lax.div(y, 2)), 8), 8)
    inside = jnp.logical_and(mine == ba, lax.div(x, 2) == core)

    taker = lax.div(x, 2)

    @pl.loop(0, 8)
    def _(step):
        to_aa = (aa ^ (2 * step) ^ core) | taker
        self = jnp.logical_and(inside, step == 0)

        @pl.when(self)
        def _():
            pltpu.make_async_copy(acc, fr.at[:, own, :], frecv).start()

        @pl.when(jnp.logical_not(self))
        def _():
            pltpu.make_async_remote_copy(
                acc, fr.at[:, own, :], osend, frecv,
                device_id={"aa": to_aa, "ba": mine}, device_id_type=MESH,
            ).start()

        for d in range(1, 4):
            pltpu.make_async_remote_copy(
                acc.at[d], tr.at[d - 1, own, :], osend, trecv,
                device_id={"aa": to_aa, "ba": lax.rem(mine + d, 8)}, device_id_type=MESH,
            ).start()

    half = pl.ds(pl.multiple_of(64 * core, 64), 64)
    swaps = []
    for n, (ref, sem) in enumerate(((fr, frecv), (tr, trecv))):
        total_wait(ref.at[:, half, :], sem)
        swaps.append(pltpu.make_async_remote_copy(
            ref.at[:, half, :], ref.at[:, half, :], wsend.at[n], wrecv.at[n],
            device_id=sibling, device_id_type=MESH,
        ))
        swaps[n].start()

    swaps[0].wait()
    for d in range(ND):
        out[:, pl.ds(pl.multiple_of(128 * lax.rem(ba + d, 8), 128), 128)] = fr[d]
    swaps[1].wait()
    for d in range(1, 4):
        out[:, pl.ds(pl.multiple_of(128 * lax.rem(ba + 8 - d, 8), 128), 128)] = tr[d - 1].T

    for ref in rounds:
        total_wait(ref, send)
    for tile in range(4):
        for rr in range(2):
            hand_over(tile, rr).wait_send()
    total_wait(m2buf.at[:, pl.ds(0, 7)], m2send)
    for stage in range(3):
        for k in range(3):
            total_wait(got_from[stage][k], gsend)
    total_wait(fr.at[:, pl.ds(0, 56), :], osend)

    @pl.when(jnp.logical_not(inside))
    def _():
        total_wait(fr.at[:, pl.ds(0, 8), :], osend)

    total_wait(tr.at[:, pl.ds(0, 64), :], osend)


def shards(field, mode_one, mode_two):
    dma = pltpu.SemaphoreType.DMA
    hbm = pl.BlockSpec(memory_space=pltpu.HBM)
    return pl.pallas_call(
        kernel,
        out_shape=jax.ShapeDtypeStruct((128, 1024), F32),
        in_specs=[hbm, hbm, hbm],
        out_specs=pl.BlockSpec(memory_space=pltpu.VMEM),
        scratch_shapes=[
            pltpu.VMEM((3, 1024, JT, 128), BF),
            pltpu.VMEM((1024 * JT, 128), F32),
            pltpu.VMEM((JT * 256, 128), F32),
            pltpu.VMEM((JOBS, 4, 4, 4, JT, 128), BF),
            *[pltpu.VMEM((JOBS, 3, 4, 4, JT, 128), BF) for _ in range(3)],
            pltpu.VMEM((4, 2, 4, 4, 4, JT, 128), BF),
            pltpu.VMEM((1024, 256), BF),
            pltpu.VMEM((256, 1024), BF),
            pltpu.VMEM((4, JT, 256), BF),
            pltpu.VMEM((4, 16, JT, 256), BF),
            pltpu.VMEM((4, 256, 256), BF),
            pltpu.VMEM((2, 4, 256, 256), F32),
            pltpu.VMEM((8, 1024, 128), BF),
            pltpu.VMEM((4, 128, 512), BF),
            pltpu.VMEM((ND, 8, 128), F32),
            pltpu.VMEM((ND, 128, 128), F32),
            pltpu.VMEM((3, 128, 128), F32),
            dma((4, 4)), dma((2,)),
            dma, dma((JOBS, 3)), dma((4, 2)), dma((4, 2)), dma, dma, dma((2,)),
            dma((2, 4)), dma((2, 4)),
            dma, dma((3, 3)), dma, dma, dma, dma((2,)), dma((2,)),
            *[
                pltpu.VMEM(shape + (len(columns), 8, 128), F32)
                for shape in ((4, 4, 4), (3, 4, 4), (4, 4), (3, 4), (4,), (3,))
                for columns in CLASSES
            ],
        ],
        compiler_params=pltpu.CompilerParams(
            collective_id=0, has_side_effects=True, vmem_limit_bytes=53 * 1024 * 1024
        ),
        cost_estimate=pl.CostEstimate(flops=13_000_000_000, bytes_accessed=18_000_000, transcendentals=0),
    )(field, mode_one, mode_two.reshape(4, JT, 256))


def solution(mesh):
    in_specs = (P(None, "aa", "ba"), P(), P("aa", None))
    return jax.shard_map(shards, mesh=mesh, in_specs=in_specs, out_specs=P("ba", None), check_vma=False)
```

```python
import functools

import jax
import jax.numpy as jnp
from jax import lax
from jax.experimental import pallas as pl
from jax.experimental.pallas import tpu as pltpu
from jax.sharding import PartitionSpec as P

BF, F32 = jnp.bfloat16, jnp.float32
MESH = pl.DeviceIdType.MESH
JT = 16
CLASSES = (((0, 1), (2, 3), (4,)), ((2, 3), (0,), (1,)))
START = ((0, 1, 2), (2, 0, 1))
ROOM = (2, 2, 1)


def where_am_i():
    aa, ba = lax.axis_index("aa"), lax.axis_index("ba")
    core, z = lax.rem(aa, 2), lax.rem(lax.div(aa, 2), 4)
    x = 2 * lax.div(aa, 8) + lax.rem(ba, 2)
    y = lax.div(ba, 2)
    return aa, ba, x, y, z, core


def place(x, y, z, core):
    aa = 8 * lax.div(x, 2) + 2 * z + core
    ba = 2 * y + lax.rem(x, 2)
    return aa, ba


def total_wait(ref, sem):
    pltpu.make_async_copy(ref, ref, sem).wait()


def kernel(
    field, m1_hbm, m2_hbm, out,
    fbuf, wide, obuf, sbuf, rbuf, m1, m1t, m2, m2buf, m2t, cacc, cc, left, acc, blocks,
    fsem, wsem, send, recv, m2send, m2recv, m2sem, csend, crecv, gsend, grecv, osend, brecv, wsend, wrecv, *parts,
):
    gs, r1, s1, r2, s2, r3 = (parts[3 * n : 3 * n + 3] for n in range(6))
    aa, ba, x, y, z, core = where_am_i()
    tiles = fbuf.shape[0]
    me = 8 * aa + ba
    sibling = {"aa": aa + 1 - 2 * core, "ba": ba}
    place_in_k = 8 * core + 4 * lax.div(x, 2) + z

    def load(tile, part):
        rows = pl.ds(256 * part, 256)
        return pltpu.make_async_copy(
            field.at[rows, pl.ds(JT * tile, JT), :], fbuf.at[tile, rows], fsem.at[tile, part]
        )

    barrier = pltpu.get_barrier_semaphore()

    def greet(aa_mask, ba_mask):
        pl.semaphore_signal(
            barrier, inc=1, device_id={"aa": aa ^ aa_mask, "ba": ba ^ ba_mask}, device_id_type=MESH
        )

    for ba_mask in range(1, 8):
        greet(0, ba_mask)

    @pl.loop(1, 16)
    def _(aa_mask):
        for ba_mask in range(8):
            greet(aa_mask, ba_mask)

    load_m1 = pltpu.make_async_copy(m1_hbm, m1, wsem.at[0])
    load_m2 = pltpu.make_async_copy(m2_hbm, m2, wsem.at[1])
    load_m1.start()
    for part in range(4):
        load(0, part).start()
    load_m2.start()

    for tile in range(1, tiles):
        for part in range(4):
            load(tile, part).start()

    load_m1.wait()
    m1t[...] = m1[...].T

    def send_rows(tile, first, count, sem):
        rows = pl.ds(pl.multiple_of(JT * place_in_k, JT), JT)

        def block(to):
            mine = sbuf.at[tile, pl.ds(2 * to + first, count)]
            return mine, rbuf.at[tile, pl.ds(first, count), ba, rows, :]

        def start(step):
            to = me ^ ((37 * step) & 127)
            mine, there = block(to)
            pltpu.make_async_remote_copy(
                mine, there, send, sem, device_id={"aa": to >> 3, "ba": to & 7}, device_id_type=MESH
            ).start()

        for step in range(1, 8):
            start(step)
        pl.loop(1, 16)(lambda turn: [start(8 * turn + step) for step in range(8)] and None)

        mine, there = block(me)
        pltpu.make_async_copy(mine, there, sem).start()

    @pl.loop(0, tiles)
    def _(tile):
        @pl.loop(0, 4)
        def _(part):
            load(tile, part).wait()

            @pl.loop(0, 32, unroll=4)
            def _(group):
                at = 256 * part + 8 * group
                wide[pl.ds(pl.multiple_of(JT * at, 128), 128), :] = (
                    fbuf[tile, pl.ds(at, 8)].reshape(128, 128).astype(F32)
                )

        @pl.loop(0, JT // 2)
        def _(pair):
            both = jnp.concatenate(
                [wide[pl.ds(2 * pair + n, 1024, stride=JT), :] for n in range(2)], axis=1
            ).astype(BF)
            got = jnp.dot(m1t[...], both, preferred_element_type=F32)
            for n in range(2):
                obuf[pl.ds(pl.multiple_of(512 * pair + 256 * n, 256), 256), :] = got[:, 128 * n : 128 * n + 128]

        @pl.loop(0, 256, unroll=8)
        def _(r):
            sbuf[tile, r] = obuf[pl.ds(r, JT, stride=256), :].astype(BF)

        @pl.when(tile == 0)
        def _():
            pl.semaphore_wait(barrier, 127)

        @pl.when(tile < 3)
        def _():
            send_rows(tile, 0, 2, recv.at[tile])

        @pl.when(tile == 3)
        def _():
            for half in range(2):
                send_rows(tile, half, 1, recv.at[3 + half])

        @pl.when(tile == 1)
        def _():
            load_m2.wait()
            mine = m2buf.at[:, place_in_k]
            for mask in range(1, 8):
                to_aa, to_ba = place(x ^ (2 * (mask // 4)), y, z ^ (mask % 4), core)
                pltpu.make_async_remote_copy(
                    m2, mine, m2send, m2recv, device_id={"aa": to_aa, "ba": to_ba}, device_id_type=MESH
                ).start()
            pltpu.make_async_copy(m2, mine, m2recv).start()

    half_of_m2 = m2buf.at[:, pl.ds(8 * core, 8)]
    total_wait(half_of_m2, m2recv)
    pass_m2 = pltpu.make_async_remote_copy(
        half_of_m2, half_of_m2, m2sem.at[0], m2sem.at[1], device_id=sibling, device_id_type=MESH
    )
    pass_m2.start()
    pass_m2.wait()
    for tile in range(4):
        m2t[tile] = m2buf[tile].reshape(256, 256).T

    def share(half, pair):
        blocks = pl.ds(2 * pair, 2)
        return pltpu.make_async_remote_copy(
            cc.at[blocks, pl.ds(256 * half, 256), :], cc.at[blocks, pl.ds(512 + 256 * half, 256), :],
            csend.at[half, pair], crecv.at[half, pair], device_id=sibling, device_id_type=MESH,
        )

    for tile in range(4):
        if tile < 3:
            total_wait(rbuf.at[tile], recv.at[tile])
        for half in range(2):
            if tile == 3:
                total_wait(rbuf.at[tile, half], recv.at[3 + half])

            @pl.loop(0, 4, unroll=2)
            def _(pair):
                both = jnp.concatenate([rbuf[tile, half, 2 * pair], rbuf[tile, half, 2 * pair + 1]], axis=1)
                got = jnp.dot(m2t[tile], both, preferred_element_type=F32)
                if tile > 0:
                    got += cacc[half, pair]
                if tile < 3:
                    cacc[half, pair] = got
                else:
                    cc[2 * pair, pl.ds(256 * half, 256), :] = got[:, :128].astype(BF)
                    cc[2 * pair + 1, pl.ds(256 * half, 256), :] = got[:, 128:].astype(BF)
                    share(half, pair).start()

    where = (x, y, z)
    sums, got_from = (gs, s1, s2), (r1, r2, r3)
    own_k, their_k = pl.ds(0, 512), pl.ds(512, 512)
    rows = [(low_y, low_x) for low_y in range(2) for low_x in range(2)]

    def row_of(low_y, low_x):
        return 4 * core + 2 * low_y + low_x

    def on_core(which):
        return lambda body: pl.when(core == which)(lambda: body(which))

    def term(rows_of_k, left, block_row, columns):
        right = jnp.concatenate([cc[lax.rem(block_row + d, 8), rows_of_k, :] for d in columns], axis=1)
        return jnp.dot(left, right, preferred_element_type=F32)

    def pieces(which, got, low_y, low_x, k):
        for octet in range(16):
            owner = (2 * (octet >> 3) + low_x, 2 * (octet & 1) + low_y, (octet >> 1) & 3)
            index = tuple(owner[(START[which][k] + stage) % 3] for stage in range(3))
            for n in range(len(CLASSES[which][k])):
                yield gs[k], index + (n,), got[8 * octet : 8 * octet + 8, 128 * n : 128 * n + 128]

    def filled(which, ref, k):
        before = (slice(None),) * (len(ref.shape) - 3)
        return ref.at[before + (pl.ds(0, len(CLASSES[which][k])),)]

    def own_part(which):
        columns = sum(sorted(CLASSES[which]), ())
        for low_y, low_x in rows:
            block_row = row_of(low_y, low_x)
            got = term(own_k, cc[block_row, own_k, :].T, block_row, columns)
            for k, mine in enumerate(CLASSES[which]):
                part = got[:, 128 * mine[0] : 128 * mine[-1] + 128]
                for ref, index, value in pieces(which, part, low_y, low_x, k):
                    ref[index] = value

    def scatter(which, k, stage):
        axis = (START[which][k] + stage) % 3
        for mask in range(1, 4):
            there = [x, y, z]
            there[axis] = there[axis] ^ mask
            to_aa, to_ba = place(*there, core)
            pltpu.make_async_remote_copy(
                filled(which, sums[stage][k], k).at[where[axis] ^ mask],
                filled(which, got_from[stage][k], k).at[mask - 1], gsend, grecv.at[k, stage],
                device_id={"aa": to_aa, "ba": to_ba}, device_id_type=MESH,
            ).start()

    def gathered(which, k, stage):
        total_wait(filled(which, got_from[stage][k], k), grecv.at[k, stage])
        got = filled(which, got_from[stage][k], k)
        own = filled(which, sums[stage][k], k)[where[(START[which][k] + stage) % 3]]
        return own + got[0] + got[1] + got[2]

    def sum_up(which):
        for k, columns in enumerate(CLASSES[which]):
            for low_y, low_x in rows:
                got = term(their_k, left[2 * low_y + low_x], row_of(low_y, low_x), columns)
                for ref, index, value in pieces(which, got, low_y, low_x, k):
                    ref[index] += value
            scatter(which, k, 0)
        for stage in range(2):
            for k in range(3):
                filled(which, sums[stage + 1][k], k)[...] = gathered(which, k, stage)
                scatter(which, k, stage + 1)
        for k, columns in enumerate(CLASSES[which]):
            acc[pl.ds(columns[0], len(columns))] = gathered(which, k, 2) * (1.0 / 65536.0)

    mine = 4 * core + 2 * lax.rem(y, 2) + lax.rem(x, 2)
    taker = lax.div(x, 2)
    own = pl.ds(pl.multiple_of(8 * (8 * taker + 2 * z + lax.div(y, 2)), 8), 8)
    inside = jnp.logical_and(mine == ba, taker == core)
    across = jnp.logical_and(mine + 4 == ba, taker == core)

    def spread(which):
        count = 5 - which

        @pl.loop(0, 8)
        def _(step):
            to_aa = (aa ^ (2 * step) ^ core) | taker
            self = jnp.logical_and(inside, step == 0)
            source, target = acc.at[pl.ds(0, count)], blocks.at[pl.ds(0, count), own, :]

            @pl.when(self)
            def _():
                pltpu.make_async_copy(source, target, brecv).start()

            @pl.when(jnp.logical_not(self))
            def _():
                pltpu.make_async_remote_copy(
                    source, target, osend, brecv, device_id={"aa": to_aa, "ba": mine}, device_id_type=MESH
                ).start()

            for d in range(1, 4):
                pltpu.make_async_remote_copy(
                    acc.at[d], blocks.at[4 + d, own, :], osend, brecv,
                    device_id={"aa": to_aa, "ba": lax.rem(mine + d, 8)}, device_id_type=MESH,
                ).start()

            if which == 0:
                self = jnp.logical_and(across, step == 0)

                @pl.when(self)
                def _():
                    pltpu.make_async_copy(acc.at[4], blocks.at[4, own, :], brecv).start()

                @pl.when(jnp.logical_not(self))
                def _():
                    pltpu.make_async_remote_copy(
                        acc.at[4], blocks.at[4, own, :], osend, brecv,
                        device_id={"aa": to_aa, "ba": mine + 4}, device_id_type=MESH,
                    ).start()

    for which in range(2):
        on_core(which)(own_part)
    for half in range(2):
        for pair in range(4):
            share(half, pair).wait()
    for low_y, low_x in rows:
        left[2 * low_y + low_x] = cc[row_of(low_y, low_x), their_k, :].T
    for which in range(2):
        on_core(which)(sum_up)
    for which in range(2):
        on_core(which)(spread)

    half = blocks.at[:, pl.ds(pl.multiple_of(64 * core, 64), 64), :]
    total_wait(half, brecv)
    swap = pltpu.make_async_remote_copy(
        half, half, wsend, wrecv, device_id=sibling, device_id_type=MESH
    )
    swap.start()
    swap.wait()

    def put(d, value):
        out[:, pl.ds(pl.multiple_of(128 * lax.rem(ba + d, 8), 128), 128)] = value

    for d in range(4):
        put(d, blocks[d])
    for d in range(1, 4):
        put(8 - d, blocks[4 + d].T)

    @pl.when(ba < 4)
    def _():
        put(4, blocks[4])

    @pl.when(ba >= 4)
    def _():
        put(4, blocks[4].T)

    total_wait(sbuf.at[:, pl.ds(0, 254)], send)
    total_wait(m2buf.at[:, pl.ds(0, 7)], m2send)

    def sent(which):
        for stage in range(3):
            for k in range(3):
                total_wait(filled(which, got_from[stage][k], k), gsend)
        count = 5 - which
        total_wait(blocks.at[pl.ds(0, 3), pl.ds(0, 64), :], osend)
        total_wait(blocks.at[pl.ds(0, count), pl.ds(0, 56), :], osend)

        @pl.when(jnp.logical_not(inside))
        def _():
            total_wait(blocks.at[pl.ds(0, count), pl.ds(0, 8), :], osend)

        if which == 0:
            total_wait(blocks.at[pl.ds(0, 1), pl.ds(0, 56), :], osend)

            @pl.when(jnp.logical_not(across))
            def _():
                total_wait(blocks.at[pl.ds(0, 1), pl.ds(0, 8), :], osend)

    for which in range(2):
        on_core(which)(sent)


def shards(field, mode_one, mode_two):
    dma = pltpu.SemaphoreType.DMA
    hbm = pl.BlockSpec(memory_space=pltpu.HBM)
    return pl.pallas_call(
        kernel,
        out_shape=jax.ShapeDtypeStruct((128, 1024), F32),
        in_specs=[hbm, hbm, hbm],
        out_specs=pl.BlockSpec(memory_space=pltpu.VMEM),
        scratch_shapes=[
            pltpu.VMEM((4, 1024, JT, 128), BF),
            pltpu.VMEM((1024 * JT, 128), F32),
            pltpu.VMEM((JT * 256, 128), F32),
            pltpu.VMEM((4, 256, JT, 128), BF),
            pltpu.VMEM((4, 2, 8, 256, 128), BF),
            pltpu.VMEM((1024, 256), BF),
            pltpu.VMEM((256, 1024), BF),
            pltpu.VMEM((4, JT, 256), BF),
            pltpu.VMEM((4, 16, JT, 256), BF),
            pltpu.VMEM((4, 256, 256), BF),
            pltpu.VMEM((2, 4, 256, 256), F32),
            pltpu.VMEM((8, 1024, 128), BF),
            pltpu.VMEM((4, 128, 512), BF),
            pltpu.VMEM((5, 8, 128), F32),
            pltpu.VMEM((8, 128, 128), F32),
            dma((4, 4)), dma((2,)),
            dma, dma((5,)), dma, dma, dma((2,)),
            dma((2, 4)), dma((2, 4)),
            dma, dma((3, 3)), dma, dma, dma, dma,
            *[
                pltpu.VMEM(shape + (room, 8, 128), F32)
                for shape in ((4, 4, 4), (3, 4, 4), (4, 4), (3, 4), (4,), (3,))
                for room in ROOM
            ],
        ],
        compiler_params=pltpu.CompilerParams(
            collective_id=0, has_side_effects=True, vmem_limit_bytes=53 * 1024 * 1024
        ),
        cost_estimate=pl.CostEstimate(flops=13_000_000_000, bytes_accessed=18_000_000, transcendentals=0),
    )(field, mode_one, mode_two.reshape(4, JT, 256))


def solution(mesh):
    in_specs = (P(None, "aa", "ba"), P(), P("aa", None))
    return jax.shard_map(shards, mesh=mesh, in_specs=in_specs, out_specs=P("ba", None), check_vma=False)
```

```python
import functools

import jax
import jax.numpy as jnp
from jax import lax
from jax.experimental import pallas as pl
from jax.experimental.pallas import tpu as pltpu
from jax.sharding import PartitionSpec as P

BF, F32 = jnp.bfloat16, jnp.float32
MESH = pl.DeviceIdType.MESH
JT = 16
CLASSES = ((0, 1), (2, 3), (4,))
ND = 5


def where_am_i():
    aa, ba = lax.axis_index("aa"), lax.axis_index("ba")
    core, z = lax.rem(aa, 2), lax.rem(lax.div(aa, 2), 4)
    x = 2 * lax.div(aa, 8) + lax.rem(ba, 2)
    y = lax.div(ba, 2)
    return aa, ba, x, y, z, core


def place(x, y, z, core):
    aa = 8 * lax.div(x, 2) + 2 * z + core
    ba = 2 * y + lax.rem(x, 2)
    return aa, ba


JOBS = 16
READY = (0, 1, 2, 3)
GAP = 3
ISSUE = ((0, 1), (1, 2), (2, 4), (4, 6))
FIRST = tuple(n % 3 for n in range(JOBS))


def job(rel, rr, tile):
    return 4 * tile + 2 * rel + rr


def timetable():
    step, free, slots = [0] * JOBS, [READY[n // 4] for n in range(JOBS)], []
    while min(step) < 3:
        now, taken = len(slots), {}
        for n in sorted(range(JOBS), key=lambda n: (step[n], n % 2 if step[n] == 2 else 0, n)):
            axis = (FIRST[n] + step[n]) % 3
            if step[n] < 3 and free[n] <= now and axis not in taken:
                taken[axis] = n
        slots.append([(n, step[n]) for n in sorted(taken.values())])
        for n in taken.values():
            step[n] += 1
            free[n] = now + GAP
    return slots


def in_order(n, triple):
    return tuple(triple[(FIRST[n] + step) % 3] for step in range(3))


def total_wait(ref, sem):
    pltpu.make_async_copy(ref, ref, sem).wait()


def kernel(
    field, m1_hbm, m2_hbm, out,
    fbuf, wide, obuf, orig, r_one, r_two, r_three, staging, m1, m1t, m2, m2buf, m2t, cacc, cc, left, acc, fr, tr,
    fsem, wsem, send, recv, ssend, srecv, m2send, m2recv, m2sem, csend, crecv, gsend, grecv, osend, frecv, trecv, wsend, wrecv, *parts,
):
    gs, r1, s1, r2, s2, r3 = (parts[3 * n : 3 * n + 3] for n in range(6))
    aa, ba, x, y, z, core = where_am_i()
    sibling = {"aa": aa + 1 - 2 * core, "ba": ba}
    rounds = (r_one, r_two, r_three)

    def load(tile, part):
        rows = pl.ds(256 * part, 256)
        return pltpu.make_async_copy(
            field.at[rows, pl.ds(JT * tile, JT), :], fbuf.at[tile % 3, rows], fsem.at[tile, part]
        )

    load_m1 = pltpu.make_async_copy(m1_hbm, m1, wsem.at[0])
    load_m2 = pltpu.make_async_copy(m2_hbm, m2, wsem.at[1])
    load_m1.start()
    for part in range(4):
        load(0, part).start()
    load_m2.start()

    barrier = pltpu.get_barrier_semaphore()

    def greet(aa_mask, ba_mask):
        pl.semaphore_signal(
            barrier, inc=1, device_id={"aa": aa ^ aa_mask, "ba": ba ^ ba_mask}, device_id_type=MESH
        )

    for ba_mask in range(1, 8):
        greet(0, ba_mask)

    @pl.loop(1, 16)
    def _(aa_mask):
        for ba_mask in range(8):
            greet(aa_mask, ba_mask)

    for tile in range(1, 3):
        for part in range(4):
            load(tile, part).start()

    load_m1.wait()
    m1t[...] = m1[...].T

    def widen(tile):
        @pl.loop(0, 4)
        def _(part):
            load(tile, part).wait()

            @pl.loop(0, 32, unroll=4)
            def _(group):
                at = 256 * part + 8 * group
                wide[pl.ds(pl.multiple_of(JT * at, 128), 128), :] = (
                    fbuf[tile % 3, pl.ds(at, 8)].reshape(128, 128).astype(F32)
                )

        if tile == 0:
            for part in range(4):
                load(3, part).start()

    def contract(tile):
        @pl.loop(0, JT // 2)
        def _(pair):
            both = jnp.concatenate(
                [wide[pl.ds(2 * pair + n, 1024, stride=JT), :] for n in range(2)], axis=1
            ).astype(BF)
            got = jnp.dot(m1t[...], both, preferred_element_type=F32)
            for n in range(2):
                obuf[pl.ds(pl.multiple_of(512 * pair + 256 * n, 256), 256), :] = got[:, 128 * n : 128 * n + 128]

        @pl.loop(0, 64, unroll=4)
        def _(slot):
            masks = (slot >> 4, (slot >> 2) & 3, slot & 3)
            row = 2 * (16 * (x ^ masks[0]) + 4 * (y ^ masks[1]) + (z ^ masks[2]))
            for rr in range(2):
                n = job(0, rr, tile)
                orig[(n,) + in_order(n, masks)] = obuf[pl.ds(row + 128 * core + rr, JT, stride=256), :].astype(BF)
                n = job(1, rr, tile)
                staging[(tile, rr) + in_order(n, masks)] = (
                    obuf[pl.ds(row + 128 * (1 - core) + rr, JT, stride=256), :].astype(BF)
                )

    def hand_over(tile, rr):
        return pltpu.make_async_remote_copy(
            staging.at[tile, rr], orig.at[job(1, rr, tile)], ssend.at[tile, rr], srecv.at[tile, rr],
            device_id=sibling, device_id_type=MESH,
        )

    def exchange(n, step):
        if step > 0:
            total_wait(rounds[step - 1].at[n], recv.at[n, step - 1])
        elif (n // 2) % 2 == 1:
            hand_over(n // 4, n % 2).wait_recv()
        axis = (FIRST[n] + step) % 3
        after = pl.ds(1, 3)
        for mask in range(1, 4):
            there = [x, y, z]
            there[axis] = there[axis] ^ mask
            to_aa, to_ba = place(*there, core)
            if step == 0:
                pieces = [(orig.at[n, mask], r_one.at[n, mask - 1])]
            elif step == 1:
                pieces = [
                    (r_one.at[n, :, mask], r_two.at[n, mask - 1, after]),
                    (orig.at[n, 0, mask], r_two.at[n, mask - 1, 0]),
                ]
            else:
                pieces = [
                    (r_two.at[n, :, :, mask], r_three.at[n, mask - 1, after]),
                    (r_one.at[n, :, 0, mask], r_three.at[n, mask - 1, 0, after]),
                    (orig.at[n, 0, 0, mask], r_three.at[n, mask - 1, 0, 0]),
                ]
            for mine, target in pieces:
                pltpu.make_async_remote_copy(
                    mine, target, send, recv.at[n, step],
                    device_id={"aa": to_aa, "ba": to_ba}, device_id_type=MESH,
                ).start()

    def block(n, masks):
        one, two, three = in_order(n, masks)
        if three:
            return r_three[n, three - 1, two, one]
        if two:
            return r_two[n, two - 1, one, 0]
        if one:
            return r_one[n, one - 1, 0, 0]
        return orig[n, 0, 0, 0]

    def spread_m2():
        load_m2.wait()
        for mask in range(1, 8):
            to_aa, to_ba = place(x ^ (2 * (mask // 4)), y, z ^ (mask % 4), core)
            pltpu.make_async_remote_copy(
                m2, m2buf.at[:, mask], m2send, m2recv,
                device_id={"aa": to_aa, "ba": to_ba}, device_id_type=MESH,
            ).start()
        pltpu.make_async_copy(m2, m2buf.at[:, 0], m2recv).start()

    def pass_m2():
        return pltpu.make_async_remote_copy(
            m2buf.at[:, pl.ds(0, 8)], m2buf.at[:, pl.ds(8, 8)], m2sem.at[0], m2sem.at[1],
            device_id=sibling, device_id_type=MESH,
        )

    def share(half, pair):
        blocks = pl.ds(2 * pair, 2)
        return pltpu.make_async_remote_copy(
            cc.at[blocks, pl.ds(256 * half, 256), :], cc.at[blocks, pl.ds(512 + 256 * half, 256), :],
            csend.at[half, pair], crecv.at[half, pair], device_id=sibling, device_id_type=MESH,
        )

    done = [0, 0]

    def add_core(rr, tile):
        for rel in range(2):
            n = job(rel, rr, tile)
            total_wait(r_three.at[n], recv.at[n, 2])
        for y_mask in range(4):
            both = jnp.concatenate([
                jnp.concatenate([
                    block(job(rel, rr, tile), (2 * high + low, y_mask, z_mask))
                    for rel in range(2) for high in range(2) for z_mask in range(4)
                ], axis=0) for low in range(2)
            ], axis=1)
            got = jnp.dot(m2t[tile], both, preferred_element_type=F32)
            if done[rr] > 0:
                got += cacc[rr, y_mask]
            if done[rr] < 3:
                cacc[rr, y_mask] = got
            else:
                for low in range(2):
                    source = 2 * (y ^ y_mask) + (lax.rem(x, 2) ^ low)
                    cc[source, pl.ds(256 * rr, 256), :] = got[:, 128 * low : 128 * low + 128].astype(BF)
                share(rr, y ^ y_mask).start()
        done[rr] += 1

    slots = timetable()
    finished = {n: now for now, slot in enumerate(slots) for n, step in slot if step == 2}
    pairs = sorted(
        (max(finished[job(rel, rr, tile)] for rel in range(2)), rr, tile) for rr in range(2) for tile in range(4)
    )

    for tile in range(4):
        widen(tile)
        contract(tile)
        if tile == 0:
            pl.semaphore_wait(barrier, 127)
        for rr in range(2):
            hand_over(tile, rr).start()
        for now in range(*ISSUE[tile]):
            for n, step in slots[now]:
                exchange(n, step)
        if tile == 1:
            spread_m2()
    total_wait(m2buf.at[:, pl.ds(0, 8)], m2recv)
    pass_m2().start()
    for now in range(6, len(slots)):
        for n, step in slots[now]:
            exchange(n, step)
        if now == 9:
            pass_m2().wait()
            for tile in range(4):
                m2t[tile] = m2buf[tile].reshape(256, 256).T
    for _, rr, tile in pairs:
        add_core(rr, tile)

    where = (x, y, z)

    def term(rows_of_k, left, block_row, columns):
        right = jnp.concatenate([cc[lax.rem(block_row + d, 8), rows_of_k, :] for d in columns], axis=1)
        return jnp.dot(left, right, preferred_element_type=F32)

    def pieces(got, low_y, low_x, k):
        for octet in range(16):
            owner = (2 * (octet >> 3) + low_x, 2 * (octet & 1) + low_y, (octet >> 1) & 3)
            index = tuple(owner[(k + stage) % 3] for stage in range(3))
            for n in range(len(CLASSES[k])):
                yield gs[k], index + (n,), got[8 * octet : 8 * octet + 8, 128 * n : 128 * n + 128]

    own_k, their_k = pl.ds(0, 512), pl.ds(512, 512)
    for low_y in range(2):
        for low_x in range(2):
            block_row = 4 * core + 2 * low_y + low_x
            got = term(own_k, cc[block_row, own_k, :].T, block_row, range(ND))
            for k, columns in enumerate(CLASSES):
                part = got[:, 128 * columns[0] : 128 * columns[-1] + 128]
                for ref, index, value in pieces(part, low_y, low_x, k):
                    ref[index] = value
    for half in range(2):
        for pair in range(4):
            share(half, pair).wait()

    def scatter(k, stage):
        axis = (k + stage) % 3
        for mask in range(1, 4):
            there = [x, y, z]
            there[axis] = there[axis] ^ mask
            to_aa, to_ba = place(*there, core)
            pltpu.make_async_remote_copy(
                sums[stage][k].at[where[axis] ^ mask], got_from[stage][k].at[mask - 1], gsend, grecv.at[k, stage],
                device_id={"aa": to_aa, "ba": to_ba}, device_id_type=MESH,
            ).start()

    def gathered(k, stage):
        total_wait(got_from[stage][k], grecv.at[k, stage])
        got = got_from[stage][k]
        return sums[stage][k][where[(k + stage) % 3]] + got[0] + got[1] + got[2]

    sums = (gs, s1, s2)
    got_from = (r1, r2, r3)
    for low_y in range(2):
        for low_x in range(2):
            left[2 * low_y + low_x] = cc[4 * core + 2 * low_y + low_x, their_k, :].T
    for k, columns in enumerate(CLASSES):
        for low_y in range(2):
            for low_x in range(2):
                got = term(their_k, left[2 * low_y + low_x], 4 * core + 2 * low_y + low_x, columns)
                for ref, index, value in pieces(got, low_y, low_x, k):
                    ref[index] += value
        scatter(k, 0)
    for stage in range(2):
        for k in range(3):
            sums[stage + 1][k][...] = gathered(k, stage)
            scatter(k, stage + 1)
    for k, columns in enumerate(CLASSES):
        acc[pl.ds(columns[0], len(columns))] = gathered(k, 2) * (1.0 / 65536.0)

    mine = 4 * core + 2 * lax.rem(y, 2) + lax.rem(x, 2)
    own = pl.ds(pl.multiple_of(8 * (8 * lax.div(x, 2) + 2 * z + lax.div(y, 2)), 8), 8)
    inside = jnp.logical_and(mine == ba, lax.div(x, 2) == core)

    taker = lax.div(x, 2)

    @pl.loop(0, 8)
    def _(step):
        to_aa = (aa ^ (2 * step) ^ core) | taker
        self = jnp.logical_and(inside, step == 0)

        @pl.when(self)
        def _():
            pltpu.make_async_copy(acc, fr.at[:, own, :], frecv).start()

        @pl.when(jnp.logical_not(self))
        def _():
            pltpu.make_async_remote_copy(
                acc, fr.at[:, own, :], osend, frecv,
                device_id={"aa": to_aa, "ba": mine}, device_id_type=MESH,
            ).start()

        for d in range(1, 4):
            pltpu.make_async_remote_copy(
                acc.at[d], tr.at[d - 1, own, :], osend, trecv,
                device_id={"aa": to_aa, "ba": lax.rem(mine + d, 8)}, device_id_type=MESH,
            ).start()

    half = pl.ds(pl.multiple_of(64 * core, 64), 64)
    swaps = []
    for n, (ref, sem) in enumerate(((fr, frecv), (tr, trecv))):
        total_wait(ref.at[:, half, :], sem)
        swaps.append(pltpu.make_async_remote_copy(
            ref.at[:, half, :], ref.at[:, half, :], wsend.at[n], wrecv.at[n],
            device_id=sibling, device_id_type=MESH,
        ))
        swaps[n].start()

    swaps[0].wait()
    for d in range(ND):
        out[:, pl.ds(pl.multiple_of(128 * lax.rem(ba + d, 8), 128), 128)] = fr[d]
    swaps[1].wait()
    for d in range(1, 4):
        out[:, pl.ds(pl.multiple_of(128 * lax.rem(ba + 8 - d, 8), 128), 128)] = tr[d - 1].T

    for ref in rounds:
        total_wait(ref, send)
    for tile in range(4):
        for rr in range(2):
            hand_over(tile, rr).wait_send()
    total_wait(m2buf.at[:, pl.ds(0, 7)], m2send)
    for stage in range(3):
        for k in range(3):
            total_wait(got_from[stage][k], gsend)
    total_wait(fr.at[:, pl.ds(0, 56), :], osend)

    @pl.when(jnp.logical_not(inside))
    def _():
        total_wait(fr.at[:, pl.ds(0, 8), :], osend)

    total_wait(tr.at[:, pl.ds(0, 64), :], osend)


def shards(field, mode_one, mode_two):
    dma = pltpu.SemaphoreType.DMA
    hbm = pl.BlockSpec(memory_space=pltpu.HBM)
    return pl.pallas_call(
        kernel,
        out_shape=jax.ShapeDtypeStruct((128, 1024), F32),
        in_specs=[hbm, hbm, hbm],
        out_specs=pl.BlockSpec(memory_space=pltpu.VMEM),
        scratch_shapes=[
            pltpu.VMEM((3, 1024, JT, 128), BF),
            pltpu.VMEM((1024 * JT, 128), F32),
            pltpu.VMEM((JT * 256, 128), F32),
            pltpu.VMEM((JOBS, 4, 4, 4, JT, 128), BF),
            *[pltpu.VMEM((JOBS, 3, 4, 4, JT, 128), BF) for _ in range(3)],
            pltpu.VMEM((4, 2, 4, 4, 4, JT, 128), BF),
            pltpu.VMEM((1024, 256), BF),
            pltpu.VMEM((256, 1024), BF),
            pltpu.VMEM((4, JT, 256), BF),
            pltpu.VMEM((4, 16, JT, 256), BF),
            pltpu.VMEM((4, 256, 256), BF),
            pltpu.VMEM((2, 4, 256, 256), F32),
            pltpu.VMEM((8, 1024, 128), BF),
            pltpu.VMEM((4, 128, 512), BF),
            pltpu.VMEM((ND, 8, 128), F32),
            pltpu.VMEM((ND, 128, 128), F32),
            pltpu.VMEM((3, 128, 128), F32),
            dma((4, 4)), dma((2,)),
            dma, dma((JOBS, 3)), dma((4, 2)), dma((4, 2)), dma, dma, dma((2,)),
            dma((2, 4)), dma((2, 4)),
            dma, dma((3, 3)), dma, dma, dma, dma((2,)), dma((2,)),
            *[
                pltpu.VMEM(shape + (len(columns), 8, 128), F32)
                for shape in ((4, 4, 4), (3, 4, 4), (4, 4), (3, 4), (4,), (3,))
                for columns in CLASSES
            ],
        ],
        compiler_params=pltpu.CompilerParams(
            collective_id=0, has_side_effects=True, vmem_limit_bytes=53 * 1024 * 1024
        ),
        cost_estimate=pl.CostEstimate(flops=13_000_000_000, bytes_accessed=18_000_000, transcendentals=0),
    )(field, mode_one, mode_two.reshape(4, JT, 256))


def solution(mesh):
    in_specs = (P(None, "aa", "ba"), P(), P("aa", None))
    return jax.shard_map(shards, mesh=mesh, in_specs=in_specs, out_specs=P("ba", None), check_vma=False)
```

```python
import functools

import jax
import jax.numpy as jnp
from jax import lax
from jax.experimental import pallas as pl
from jax.experimental.pallas import tpu as pltpu
from jax.sharding import PartitionSpec as P

BF, F32 = jnp.bfloat16, jnp.float32
MESH = pl.DeviceIdType.MESH
JT = 16
CLASSES = ((0, 1), (2, 3), (4,))
RELAYED = 2
OPPOSITE = 74
ND = 5


def where_am_i():
    aa, ba = lax.axis_index("aa"), lax.axis_index("ba")
    core, z = lax.rem(aa, 2), lax.rem(lax.div(aa, 2), 4)
    x = 2 * lax.div(aa, 8) + lax.rem(ba, 2)
    y = lax.div(ba, 2)
    return aa, ba, x, y, z, core


def place(x, y, z, core):
    aa = 8 * lax.div(x, 2) + 2 * z + core
    ba = 2 * y + lax.rem(x, 2)
    return aa, ba


def masks(step):
    one = step ^ (step >> 2)
    return (one ^ (step >> 4)) & 3, one & 3, step & 3, (step ^ (step >> 6)) & 1


def mesh_masks(mx, my, mz, mc):
    return ((mx >> 1) << 3) | (mz << 1) | mc, (my << 1) | (mx & 1)


def total_wait(ref, sem):
    pltpu.make_async_copy(ref, ref, sem).wait()


def kernel(
    field, m1_hbm, m2_hbm, out,
    fbuf, tbuf, obuf, sbuf, rbuf, relay, m1, m1t, m2, m2buf, m2t, cacc, cc, acc, fr, tr, pmat,
    fsem, wsem, send, recv, arrived, m2send, m2recv, m2sem, csend, crecv, gsend, grecv, osend, frecv, trecv, wsend, wrecv, *parts,
):
    gs, r1, s1, r2, s2, r3 = (parts[3 * n : 3 * n + 3] for n in range(6))
    aa, ba, x, y, z, core = where_am_i()
    tiles = fbuf.shape[0]
    sibling = {"aa": aa + 1 - 2 * core, "ba": ba}
    place_in_k = 8 * core + 4 * lax.div(x, 2) + z

    def load(tile, part):
        rows = pl.ds(256 * part, 256)
        return pltpu.make_async_copy(
            field.at[rows, pl.ds(JT * tile, JT), :], fbuf.at[tile, rows], fsem.at[tile, part]
        )

    load_m1 = pltpu.make_async_copy(m1_hbm, m1, wsem.at[0])
    load_m2 = pltpu.make_async_copy(m2_hbm, m2, wsem.at[1])
    load_m1.start()
    for part in range(4):
        load(0, part).start()
    load_m2.start()

    barrier = pltpu.get_barrier_semaphore()

    def greet(aa_mask, ba_mask):
        pl.semaphore_signal(
            barrier, inc=1, device_id={"aa": aa ^ aa_mask, "ba": ba ^ ba_mask}, device_id_type=MESH
        )

    for ba_mask in range(1, 8):
        greet(0, ba_mask)

    @pl.loop(1, 16)
    def _(aa_mask):
        for ba_mask in range(8):
            greet(aa_mask, ba_mask)

    for tile in range(1, tiles):
        for part in range(4):
            load(tile, part).start()

    row = lax.broadcasted_iota(jnp.int32, (256, 256), 0)
    col = lax.broadcasted_iota(jnp.int32, (256, 256), 1)
    swap = ((row & 15) * 16 + (row >> 4)) == col
    pmat[...] = jnp.where(swap, 1.0, 0.0).astype(BF)
    load_m1.wait()
    m1t[...] = m1[...].T

    def send_rows(tile, first, count, sem):
        rows = pl.ds(pl.multiple_of(JT * place_in_k, JT), JT)

        def block(to_aa, to_ba):
            mine = sbuf.at[tile, pl.ds(2 * (8 * to_aa + to_ba) + first, count)]
            return mine, rbuf.at[tile, pl.ds(first, count), ba, rows, :]

        @pl.loop(1, 128)
        def _(step):
            each = masks(step)
            aa_mask, ba_mask = mesh_masks(*each)
            to_aa, to_ba = aa ^ aa_mask, ba ^ ba_mask
            mine, there = block(to_aa, to_ba)
            by_relay = jnp.logical_and(opposite(each), tile < RELAYED) if count == 2 else False

            @pl.when(by_relay)
            def _():
                if count == 1:
                    return
                via_aa, via_ba = place(*[on_way(p, m, 1) for p, m in zip((x, y, z), each)], core)
                pltpu.make_async_remote_copy(
                    mine, relay.at[jnp.minimum(tile, RELAYED - 1), step], send, arrived.at[tile],
                    device_id={"aa": via_aa, "ba": via_ba}, device_id_type=MESH,
                ).start()

            @pl.when(jnp.logical_not(by_relay))
            def _():
                pltpu.make_async_remote_copy(
                    mine, there, send, sem, device_id={"aa": to_aa, "ba": to_ba}, device_id_type=MESH
                ).start()

        mine, there = block(aa, ba)
        pltpu.make_async_copy(mine, there, sem).start()

    def opposite(each):
        return jnp.logical_or(each[0] == 2, jnp.logical_or(each[1] == 2, each[2] == 2))

    def on_way(p, mask, steps):
        return jnp.where(mask == 2, (p + 1 * steps) & 3, p)

    def forward(tile):
        total_wait(relay.at[tile, pl.ds(0, OPPOSITE)], arrived.at[tile])

        @pl.loop(1, 128)
        def _(step):
            each = masks(step)

            @pl.when(opposite(each))
            def _():
                from_x, from_y, from_z = [on_way(p, m, -1) for p, m in zip((x, y, z), each)]
                _, from_ba = place(from_x, from_y, from_z, core)
                from_place = 8 * core + 4 * lax.div(from_x, 2) + from_z
                to = [jnp.where(m == 2, on_way(p, m, 1), p ^ m) for p, m in zip((x, y, z), each)]
                to_aa, to_ba = place(*to, core ^ each[3])
                rows = pl.ds(pl.multiple_of(JT * from_place, JT), JT)
                pltpu.make_async_remote_copy(
                    relay.at[tile, step], rbuf.at[tile, :, from_ba, rows, :], send, recv.at[tile],
                    device_id={"aa": to_aa, "ba": to_ba}, device_id_type=MESH,
                ).start()

    @pl.loop(0, tiles)
    def _(tile):
        @pl.loop(0, 4)
        def _(part):
            load(tile, part).wait()

            @pl.loop(0, 8, unroll=4)
            def _(group):
                at = pl.multiple_of(256 * part + 32 * group, 32)
                left = fbuf[tile, pl.ds(at, 16)].reshape(256, 128)
                right = fbuf[tile, pl.ds(at + 16, 16)].reshape(256, 128)
                both = jnp.concatenate([left, right], axis=1)
                turned = jnp.dot(pmat[...], both, preferred_element_type=F32).astype(BF)
                tbuf[:, pl.ds(at, 16), :] = turned[:, :128].reshape(16, 16, 128)
                tbuf[:, pl.ds(pl.multiple_of(at + 16, 16), 16), :] = turned[:, 128:].reshape(16, 16, 128)

        @pl.loop(0, JT // 2)
        def _(pair):
            both = jnp.concatenate([tbuf[2 * pair], tbuf[2 * pair + 1]], axis=1)
            got = jnp.dot(m1t[...], both, preferred_element_type=F32).astype(BF)
            obuf[2 * pair] = got[:, :128]
            obuf[2 * pair + 1] = got[:, 128:]

        @pl.loop(0, 8, unroll=2)
        def _(group):
            at = pl.multiple_of(32 * group, 32)
            left = obuf[:, pl.ds(at, 16), :].reshape(256, 128)
            right = obuf[:, pl.ds(pl.multiple_of(at + 16, 16), 16), :].reshape(256, 128)
            both = jnp.concatenate([left, right], axis=1)
            turned = jnp.dot(pmat[...], both, preferred_element_type=F32).astype(BF)
            sbuf[tile, pl.ds(at, 16)] = turned[:, :128].reshape(16, 16, 128)
            sbuf[tile, pl.ds(at + 16, 16)] = turned[:, 128:].reshape(16, 16, 128)

        @pl.when(tile == 0)
        def _():
            pl.semaphore_wait(barrier, 127)

        @pl.when(tile >= 4 - RELAYED)
        def _():
            forward(tile - (4 - RELAYED))

        @pl.when(tile < 3)
        def _():
            send_rows(tile, 0, 2, recv.at[tile])

        @pl.when(tile == 3)
        def _():
            for half in range(2):
                send_rows(tile, half, 1, recv.at[3 + half])

        @pl.when(tile == 1)
        def _():
            load_m2.wait()
            mine = m2buf.at[:, place_in_k]
            for mask in range(1, 8):
                to_aa, to_ba = place(x ^ (2 * (mask // 4)), y, z ^ (mask % 4), core)
                pltpu.make_async_remote_copy(
                    m2, mine, m2send, m2recv, device_id={"aa": to_aa, "ba": to_ba}, device_id_type=MESH
                ).start()
            pltpu.make_async_copy(m2, mine, m2recv).start()

    half_of_m2 = m2buf.at[:, pl.ds(8 * core, 8)]
    total_wait(half_of_m2, m2recv)
    pass_m2 = pltpu.make_async_remote_copy(
        half_of_m2, half_of_m2, m2sem.at[0], m2sem.at[1], device_id=sibling, device_id_type=MESH
    )
    pass_m2.start()
    pass_m2.wait()
    for tile in range(4):
        m2t[tile] = m2buf[tile].reshape(256, 256).T

    def share(half):
        return pltpu.make_async_remote_copy(
            cc.at[:, pl.ds(256 * half, 256), :], cc.at[:, pl.ds(512 + 256 * half, 256), :],
            csend.at[half], crecv.at[half], device_id=sibling, device_id_type=MESH,
        )

    for tile in range(4):
        if tile < 3:
            total_wait(rbuf.at[tile], recv.at[tile])
        for half in range(2):
            if tile == 3:
                total_wait(rbuf.at[tile, half], recv.at[3 + half])

            @pl.loop(0, 4, unroll=2)
            def _(pair):
                both = jnp.concatenate([rbuf[tile, half, 2 * pair], rbuf[tile, half, 2 * pair + 1]], axis=1)
                got = jnp.dot(m2t[tile], both, preferred_element_type=F32)
                if tile > 0:
                    got += cacc[half, pair]
                if tile < 3:
                    cacc[half, pair] = got
                else:
                    cc[2 * pair, pl.ds(256 * half, 256), :] = got[:, :128].astype(BF)
                    cc[2 * pair + 1, pl.ds(256 * half, 256), :] = got[:, 128:].astype(BF)

            if tile == 3:
                share(half).start()

    where = (x, y, z)

    def term(block_row, first):
        rows = pl.ds(first, 512)
        right = jnp.concatenate([cc[lax.rem(block_row + d, 8), rows, :] for d in range(ND)], axis=1)
        return lax.dot_general(
            cc[block_row, rows, :], right, (((0,), (0,)), ((), ())), preferred_element_type=F32
        )

    def pieces(got, low_y, low_x):
        for octet in range(16):
            owner = (2 * (octet >> 3) + low_x, 2 * (octet & 1) + low_y, (octet >> 1) & 3)
            for k, columns in enumerate(CLASSES):
                index = tuple(owner[(k + stage) % 3] for stage in range(3))
                for n, d in enumerate(columns):
                    yield gs[k], index + (n,), got[8 * octet : 8 * octet + 8, 128 * d : 128 * d + 128]

    for low_y in range(2):
        for low_x in range(2):
            for ref, index, value in pieces(term(4 * core + 2 * low_y + low_x, 0), low_y, low_x):
                ref[index] = value
    for half in range(2):
        share(half).wait()
    for low_y in range(2):
        for low_x in range(2):
            for ref, index, value in pieces(term(4 * core + 2 * low_y + low_x, 512), low_y, low_x):
                ref[index] += value

    def scatter(k, stage):
        axis = (k + stage) % 3
        for mask in range(1, 4):
            there = [x, y, z]
            there[axis] = there[axis] ^ mask
            to_aa, to_ba = place(*there, core)
            pltpu.make_async_remote_copy(
                sums[stage][k].at[where[axis] ^ mask], got_from[stage][k].at[mask - 1], gsend, grecv.at[k, stage],
                device_id={"aa": to_aa, "ba": to_ba}, device_id_type=MESH,
            ).start()

    def gathered(k, stage):
        total_wait(got_from[stage][k], grecv.at[k, stage])
        got = got_from[stage][k]
        return sums[stage][k][where[(k + stage) % 3]] + got[0] + got[1] + got[2]

    sums = (gs, s1, s2)
    got_from = (r1, r2, r3)
    for k in range(3):
        scatter(k, 0)
    for stage in range(2):
        for k in range(3):
            sums[stage + 1][k][...] = gathered(k, stage)
            scatter(k, stage + 1)
    for k, columns in enumerate(CLASSES):
        acc[pl.ds(columns[0], len(columns))] = gathered(k, 2) * (1.0 / 65536.0)

    mine = 4 * core + 2 * lax.rem(y, 2) + lax.rem(x, 2)
    own = pl.ds(pl.multiple_of(8 * (8 * lax.div(x, 2) + 2 * z + lax.div(y, 2)), 8), 8)
    inside = jnp.logical_and(mine == ba, lax.div(x, 2) == core)

    taker = lax.div(x, 2)

    @pl.loop(0, 8)
    def _(step):
        to_aa = (aa ^ (2 * step) ^ core) | taker
        self = jnp.logical_and(inside, step == 0)

        @pl.when(self)
        def _():
            pltpu.make_async_copy(acc, fr.at[:, own, :], frecv).start()

        @pl.when(jnp.logical_not(self))
        def _():
            pltpu.make_async_remote_copy(
                acc, fr.at[:, own, :], osend, frecv,
                device_id={"aa": to_aa, "ba": mine}, device_id_type=MESH,
            ).start()

        for d in range(1, 4):
            pltpu.make_async_remote_copy(
                acc.at[d], tr.at[d - 1, own, :], osend, trecv,
                device_id={"aa": to_aa, "ba": lax.rem(mine + d, 8)}, device_id_type=MESH,
            ).start()

    half = pl.ds(pl.multiple_of(64 * core, 64), 64)
    swaps = []
    for n, (ref, sem) in enumerate(((fr, frecv), (tr, trecv))):
        total_wait(ref.at[:, half, :], sem)
        swaps.append(pltpu.make_async_remote_copy(
            ref.at[:, half, :], ref.at[:, half, :], wsend.at[n], wrecv.at[n],
            device_id=sibling, device_id_type=MESH,
        ))
        swaps[n].start()

    swaps[0].wait()
    for d in range(ND):
        out[:, pl.ds(pl.multiple_of(128 * lax.rem(ba + d, 8), 128), 128)] = fr[d]
    swaps[1].wait()
    for d in range(1, 4):
        out[:, pl.ds(pl.multiple_of(128 * lax.rem(ba + 8 - d, 8), 128), 128)] = tr[d - 1].T

    total_wait(sbuf.at[:, pl.ds(0, 254)], send)
    total_wait(relay.at[:, pl.ds(0, OPPOSITE)], send)
    total_wait(m2buf.at[:, pl.ds(0, 7)], m2send)
    for stage in range(3):
        for k in range(3):
            total_wait(got_from[stage][k], gsend)
    total_wait(fr.at[:, pl.ds(0, 56), :], osend)

    @pl.when(jnp.logical_not(inside))
    def _():
        total_wait(fr.at[:, pl.ds(0, 8), :], osend)

    total_wait(tr.at[:, pl.ds(0, 64), :], osend)


def shards(field, mode_one, mode_two):
    dma = pltpu.SemaphoreType.DMA
    hbm = pl.BlockSpec(memory_space=pltpu.HBM)
    return pl.pallas_call(
        kernel,
        out_shape=jax.ShapeDtypeStruct((128, 1024), F32),
        in_specs=[hbm, hbm, hbm],
        out_specs=pl.BlockSpec(memory_space=pltpu.VMEM),
        scratch_shapes=[
            pltpu.VMEM((4, 1024, JT, 128), BF),
            pltpu.VMEM((JT, 1024, 128), BF),
            pltpu.VMEM((JT, 256, 128), BF),
            pltpu.VMEM((4, 256, JT, 128), BF),
            pltpu.VMEM((4, 2, 8, 256, 128), BF),
            pltpu.VMEM((RELAYED, 128, 2, JT, 128), BF),
            pltpu.VMEM((1024, 256), BF),
            pltpu.VMEM((256, 1024), BF),
            pltpu.VMEM((4, JT, 256), BF),
            pltpu.VMEM((4, 16, JT, 256), BF),
            pltpu.VMEM((4, 256, 256), BF),
            pltpu.VMEM((2, 4, 256, 256), F32),
            pltpu.VMEM((8, 1024, 128), BF),
            pltpu.VMEM((ND, 8, 128), F32),
            pltpu.VMEM((ND, 128, 128), F32),
            pltpu.VMEM((3, 128, 128), F32),
            pltpu.VMEM((256, 256), BF),
            dma((4, 4)), dma((2,)),
            dma, dma((5,)), dma((4,)), dma, dma, dma((2,)),
            dma((2,)), dma((2,)),
            dma, dma((3, 3)), dma, dma, dma, dma((2,)), dma((2,)),
            *[
                pltpu.VMEM(shape + (len(columns), 8, 128), F32)
                for shape in ((4, 4, 4), (3, 4, 4), (4, 4), (3, 4), (4,), (3,))
                for columns in CLASSES
            ],
        ],
        compiler_params=pltpu.CompilerParams(
            collective_id=0, has_side_effects=True, vmem_limit_bytes=53 * 1024 * 1024
        ),
        cost_estimate=pl.CostEstimate(flops=13_000_000_000, bytes_accessed=18_000_000, transcendentals=0),
    )(field, mode_one, mode_two.reshape(4, JT, 256))


def solution(mesh):
    in_specs = (P(None, "aa", "ba"), P(), P("aa", None))
    return jax.shard_map(shards, mesh=mesh, in_specs=in_specs, out_specs=P("ba", None), check_vma=False)
```

```python
import functools

import jax
import jax.numpy as jnp
from jax import lax
from jax.experimental import pallas as pl
from jax.experimental.pallas import tpu as pltpu
from jax.sharding import PartitionSpec as P

BF, F32 = jnp.bfloat16, jnp.float32
MESH = pl.DeviceIdType.MESH
JT = 16
CLASSES = ((0, 1), (2, 3), (4,))
ND = 5


def where_am_i():
    aa, ba = lax.axis_index("aa"), lax.axis_index("ba")
    core, z = lax.rem(aa, 2), lax.rem(lax.div(aa, 2), 4)
    x = 2 * lax.div(aa, 8) + lax.rem(ba, 2)
    y = lax.div(ba, 2)
    return aa, ba, x, y, z, core


def place(x, y, z, core):
    aa = 8 * lax.div(x, 2) + 2 * z + core
    ba = 2 * y + lax.rem(x, 2)
    return aa, ba


def masks(step):
    one = step ^ (step >> 2)
    mx, my, mz, mc = (one ^ (step >> 4)) & 3, one & 3, step & 3, (step ^ (step >> 6)) & 1
    return ((mx >> 1) << 3) | (mz << 1) | mc, (my << 1) | (mx & 1)


def total_wait(ref, sem):
    pltpu.make_async_copy(ref, ref, sem).wait()


def kernel(
    field, m1_hbm, m2_hbm, out,
    fbuf, tbuf, obuf, sbuf, rbuf, m1, m1t, m2, m2buf, m2t, cacc, cc, acc, fr, tr, pmat,
    fsem, wsem, send, recv, m2send, m2recv, m2sem, m2ysend, m2yrecv, csend, crecv, gsend, grecv, osend, frecv, trecv, wsend, wrecv, *parts,
):
    gs, r1, s1, r2, s2, r3 = (parts[3 * n : 3 * n + 3] for n in range(6))
    aa, ba, x, y, z, core = where_am_i()
    tiles = fbuf.shape[0]
    sibling = {"aa": aa + 1 - 2 * core, "ba": ba}
    place_in_k = 8 * core + 4 * lax.div(x, 2) + z

    def load(tile, part):
        rows = pl.ds(256 * part, 256)
        return pltpu.make_async_copy(
            field.at[rows, pl.ds(JT * tile, JT), :], fbuf.at[tile, rows], fsem.at[tile, part]
        )

    barrier = pltpu.get_barrier_semaphore()

    def greet(aa_mask, ba_mask):
        pl.semaphore_signal(
            barrier, inc=1, device_id={"aa": aa ^ aa_mask, "ba": ba ^ ba_mask}, device_id_type=MESH
        )

    for ba_mask in range(1, 8):
        greet(0, ba_mask)

    @pl.loop(1, 16)
    def _(aa_mask):
        for ba_mask in range(8):
            greet(aa_mask, ba_mask)

    load_m1 = pltpu.make_async_copy(m1_hbm, m1, wsem.at[0])
    load_m2 = pltpu.make_async_copy(m2_hbm, m2, wsem.at[1])
    load_m1.start()
    for part in range(4):
        load(0, part).start()
    load_m2.start()

    for tile in range(1, tiles):
        for part in range(4):
            load(tile, part).start()

    row = lax.broadcasted_iota(jnp.int32, (256, 256), 0)
    col = lax.broadcasted_iota(jnp.int32, (256, 256), 1)
    swap = ((row & 15) * 16 + (row >> 4)) == col
    pmat[...] = jnp.where(swap, 1.0, 0.0).astype(BF)
    load_m1.wait()
    m1t[...] = m1[...].T

    def send_rows(tile, first, count, sem):
        rows = pl.ds(pl.multiple_of(JT * place_in_k, JT), JT)

        def block(to_aa, to_ba):
            mine = sbuf.at[tile, pl.ds(2 * (8 * to_aa + to_ba) + first, count)]
            return mine, rbuf.at[tile, pl.ds(first, count), ba, rows, :]

        @pl.loop(1, 128)
        def _(step):
            aa_mask, ba_mask = masks(step)
            to_aa, to_ba = aa ^ aa_mask, ba ^ ba_mask
            mine, there = block(to_aa, to_ba)
            pltpu.make_async_remote_copy(
                mine, there, send, sem, device_id={"aa": to_aa, "ba": to_ba}, device_id_type=MESH
            ).start()

        mine, there = block(aa, ba)
        pltpu.make_async_copy(mine, there, sem).start()

    parity = lax.rem(y, 2)

    def trade_m2(n):
        gathered = m2buf.at[parity + 2 * n, pl.ds(8 * core, 8)]
        to_aa, to_ba = place(x, y ^ (1 + 2 * n), z, core)
        return pltpu.make_async_remote_copy(
            gathered, gathered, m2ysend.at[n], m2yrecv.at[n],
            device_id={"aa": to_aa, "ba": to_ba}, device_id_type=MESH,
        )

    @pl.loop(0, tiles)
    def _(tile):
        @pl.loop(0, 4)
        def _(part):
            load(tile, part).wait()

            @pl.loop(0, 8, unroll=4)
            def _(group):
                at = pl.multiple_of(256 * part + 32 * group, 32)
                left = fbuf[tile, pl.ds(at, 16)].reshape(256, 128)
                right = fbuf[tile, pl.ds(at + 16, 16)].reshape(256, 128)
                both = jnp.concatenate([left, right], axis=1)
                turned = jnp.dot(pmat[...], both, preferred_element_type=F32).astype(BF)
                tbuf[:, pl.ds(at, 16), :] = turned[:, :128].reshape(16, 16, 128)
                tbuf[:, pl.ds(pl.multiple_of(at + 16, 16), 16), :] = turned[:, 128:].reshape(16, 16, 128)

        @pl.loop(0, JT // 2)
        def _(pair):
            both = jnp.concatenate([tbuf[2 * pair], tbuf[2 * pair + 1]], axis=1)
            got = jnp.dot(m1t[...], both, preferred_element_type=F32).astype(BF)
            obuf[2 * pair] = got[:, :128]
            obuf[2 * pair + 1] = got[:, 128:]

        @pl.loop(0, 8, unroll=2)
        def _(group):
            at = pl.multiple_of(32 * group, 32)
            left = obuf[:, pl.ds(at, 16), :].reshape(256, 128)
            right = obuf[:, pl.ds(pl.multiple_of(at + 16, 16), 16), :].reshape(256, 128)
            both = jnp.concatenate([left, right], axis=1)
            turned = jnp.dot(pmat[...], both, preferred_element_type=F32).astype(BF)
            sbuf[tile, pl.ds(at, 16)] = turned[:, :128].reshape(16, 16, 128)
            sbuf[tile, pl.ds(at + 16, 16)] = turned[:, 128:].reshape(16, 16, 128)

        @pl.when(tile == 0)
        def _():
            pl.semaphore_wait(barrier, 127)

        @pl.when(tile < 3)
        def _():
            send_rows(tile, 0, 2, recv.at[tile])

        @pl.when(tile == 3)
        def _():
            for half in range(2):
                send_rows(tile, half, 1, recv.at[3 + half])

        @pl.when(tile == 0)
        def _():
            load_m2.wait()
            for mask in range(1, 8):
                to_aa, to_ba = place(x ^ (2 * (mask // 4)), y, z ^ (mask % 4), core)
                for n in range(2):
                    pltpu.make_async_remote_copy(
                        m2.at[parity + 2 * n], m2buf.at[parity + 2 * n, place_in_k], m2send, m2recv,
                        device_id={"aa": to_aa, "ba": to_ba}, device_id_type=MESH,
                    ).start()
            for n in range(2):
                pltpu.make_async_copy(
                    m2.at[parity + 2 * n], m2buf.at[parity + 2 * n, place_in_k], m2recv
                ).start()

        @pl.when(tile == 2)
        def _():
            total_wait(m2buf.at[pl.ds(0, 2), pl.ds(0, 8)], m2recv)
            for n in range(2):
                trade_m2(n).start()

    for n in range(2):
        trade_m2(n).wait()
    half_of_m2 = m2buf.at[:, pl.ds(8 * core, 8)]
    pass_m2 = pltpu.make_async_remote_copy(
        half_of_m2, half_of_m2, m2sem.at[0], m2sem.at[1], device_id=sibling, device_id_type=MESH
    )
    pass_m2.start()
    pass_m2.wait()
    for tile in range(4):
        m2t[tile] = m2buf[tile].reshape(256, 256).T

    def share(half):
        return pltpu.make_async_remote_copy(
            cc.at[:, pl.ds(256 * half, 256), :], cc.at[:, pl.ds(512 + 256 * half, 256), :],
            csend.at[half], crecv.at[half], device_id=sibling, device_id_type=MESH,
        )

    for tile in range(4):
        if tile < 3:
            total_wait(rbuf.at[tile], recv.at[tile])
        for half in range(2):
            if tile == 3:
                total_wait(rbuf.at[tile, half], recv.at[3 + half])

            @pl.loop(0, 4, unroll=2)
            def _(pair):
                both = jnp.concatenate([rbuf[tile, half, 2 * pair], rbuf[tile, half, 2 * pair + 1]], axis=1)
                got = jnp.dot(m2t[tile], both, preferred_element_type=F32)
                if tile > 0:
                    got += cacc[half, pair]
                if tile < 3:
                    cacc[half, pair] = got
                else:
                    cc[2 * pair, pl.ds(256 * half, 256), :] = got[:, :128].astype(BF)
                    cc[2 * pair + 1, pl.ds(256 * half, 256), :] = got[:, 128:].astype(BF)

            if tile == 3:
                share(half).start()

    where = (x, y, z)

    def term(block_row, first):
        rows = pl.ds(first, 512)
        right = jnp.concatenate([cc[lax.rem(block_row + d, 8), rows, :] for d in range(ND)], axis=1)
        return lax.dot_general(
            cc[block_row, rows, :], right, (((0,), (0,)), ((), ())), preferred_element_type=F32
        )

    def pieces(got, low_y, low_x):
        for octet in range(16):
            owner = (2 * (octet >> 3) + low_x, 2 * (octet & 1) + low_y, (octet >> 1) & 3)
            for k, columns in enumerate(CLASSES):
                index = tuple(owner[(k + stage) % 3] for stage in range(3))
                for n, d in enumerate(columns):
                    yield gs[k], index + (n,), got[8 * octet : 8 * octet + 8, 128 * d : 128 * d + 128]

    for low_y in range(2):
        for low_x in range(2):
            for ref, index, value in pieces(term(4 * core + 2 * low_y + low_x, 0), low_y, low_x):
                ref[index] = value
    for half in range(2):
        share(half).wait()
    for low_y in range(2):
        for low_x in range(2):
            for ref, index, value in pieces(term(4 * core + 2 * low_y + low_x, 512), low_y, low_x):
                ref[index] += value

    def scatter(k, stage):
        axis = (k + stage) % 3
        for mask in range(1, 4):
            there = [x, y, z]
            there[axis] = there[axis] ^ mask
            to_aa, to_ba = place(*there, core)
            pltpu.make_async_remote_copy(
                sums[stage][k].at[where[axis] ^ mask], got_from[stage][k].at[mask - 1], gsend, grecv.at[k, stage],
                device_id={"aa": to_aa, "ba": to_ba}, device_id_type=MESH,
            ).start()

    def gathered(k, stage):
        total_wait(got_from[stage][k], grecv.at[k, stage])
        got = got_from[stage][k]
        return sums[stage][k][where[(k + stage) % 3]] + got[0] + got[1] + got[2]

    sums = (gs, s1, s2)
    got_from = (r1, r2, r3)
    for k in range(3):
        scatter(k, 0)
    for stage in range(2):
        for k in range(3):
            sums[stage + 1][k][...] = gathered(k, stage)
            scatter(k, stage + 1)
    for k, columns in enumerate(CLASSES):
        acc[pl.ds(columns[0], len(columns))] = gathered(k, 2) * (1.0 / 65536.0)

    mine = 4 * core + 2 * lax.rem(y, 2) + lax.rem(x, 2)
    own = pl.ds(pl.multiple_of(8 * (8 * lax.div(x, 2) + 2 * z + lax.div(y, 2)), 8), 8)
    inside = jnp.logical_and(mine == ba, lax.div(x, 2) == core)

    taker = lax.div(x, 2)

    @pl.loop(0, 8)
    def _(step):
        to_aa = (aa ^ (2 * step) ^ core) | taker
        self = jnp.logical_and(inside, step == 0)

        @pl.when(self)
        def _():
            pltpu.make_async_copy(acc, fr.at[:, own, :], frecv).start()

        @pl.when(jnp.logical_not(self))
        def _():
            pltpu.make_async_remote_copy(
                acc, fr.at[:, own, :], osend, frecv,
                device_id={"aa": to_aa, "ba": mine}, device_id_type=MESH,
            ).start()

        for d in range(1, 4):
            pltpu.make_async_remote_copy(
                acc.at[d], tr.at[d - 1, own, :], osend, trecv,
                device_id={"aa": to_aa, "ba": lax.rem(mine + d, 8)}, device_id_type=MESH,
            ).start()

    half = pl.ds(pl.multiple_of(64 * core, 64), 64)
    swaps = []
    for n, (ref, sem) in enumerate(((fr, frecv), (tr, trecv))):
        total_wait(ref.at[:, half, :], sem)
        swaps.append(pltpu.make_async_remote_copy(
            ref.at[:, half, :], ref.at[:, half, :], wsend.at[n], wrecv.at[n],
            device_id=sibling, device_id_type=MESH,
        ))
        swaps[n].start()

    swaps[0].wait()
    for d in range(ND):
        out[:, pl.ds(pl.multiple_of(128 * lax.rem(ba + d, 8), 128), 128)] = fr[d]
    swaps[1].wait()
    for d in range(1, 4):
        out[:, pl.ds(pl.multiple_of(128 * lax.rem(ba + 8 - d, 8), 128), 128)] = tr[d - 1].T

    total_wait(sbuf.at[:, pl.ds(0, 254)], send)
    total_wait(m2buf.at[pl.ds(0, 2), pl.ds(0, 7)], m2send)
    for stage in range(3):
        for k in range(3):
            total_wait(got_from[stage][k], gsend)
    total_wait(fr.at[:, pl.ds(0, 56), :], osend)

    @pl.when(jnp.logical_not(inside))
    def _():
        total_wait(fr.at[:, pl.ds(0, 8), :], osend)

    total_wait(tr.at[:, pl.ds(0, 64), :], osend)


def shards(field, mode_one, mode_two):
    dma = pltpu.SemaphoreType.DMA
    hbm = pl.BlockSpec(memory_space=pltpu.HBM)
    return pl.pallas_call(
        kernel,
        out_shape=jax.ShapeDtypeStruct((128, 1024), F32),
        in_specs=[hbm, hbm, hbm],
        out_specs=pl.BlockSpec(memory_space=pltpu.VMEM),
        scratch_shapes=[
            pltpu.VMEM((4, 1024, JT, 128), BF),
            pltpu.VMEM((JT, 1024, 128), BF),
            pltpu.VMEM((JT, 256, 128), BF),
            pltpu.VMEM((4, 256, JT, 128), BF),
            pltpu.VMEM((4, 2, 8, 256, 128), BF),
            pltpu.VMEM((1024, 256), BF),
            pltpu.VMEM((256, 1024), BF),
            pltpu.VMEM((4, JT, 256), BF),
            pltpu.VMEM((4, 16, JT, 256), BF),
            pltpu.VMEM((4, 256, 256), BF),
            pltpu.VMEM((2, 4, 256, 256), F32),
            pltpu.VMEM((8, 1024, 128), BF),
            pltpu.VMEM((ND, 8, 128), F32),
            pltpu.VMEM((ND, 128, 128), F32),
            pltpu.VMEM((3, 128, 128), F32),
            pltpu.VMEM((256, 256), BF),
            dma((4, 4)), dma((2,)),
            dma, dma((5,)), dma, dma, dma((2,)), dma((2,)), dma((2,)),
            dma((2,)), dma((2,)),
            dma, dma((3, 3)), dma, dma, dma, dma((2,)), dma((2,)),
            *[
                pltpu.VMEM(shape + (len(columns), 8, 128), F32)
                for shape in ((4, 4, 4), (3, 4, 4), (4, 4), (3, 4), (4,), (3,))
                for columns in CLASSES
            ],
        ],
        compiler_params=pltpu.CompilerParams(
            collective_id=0, has_side_effects=True, vmem_limit_bytes=53 * 1024 * 1024
        ),
        cost_estimate=pl.CostEstimate(flops=13_000_000_000, bytes_accessed=18_000_000, transcendentals=0),
    )(field, mode_one, mode_two.reshape(4, JT, 256))


def solution(mesh):
    in_specs = (P(None, "aa", "ba"), P(), P("aa", None))
    return jax.shard_map(shards, mesh=mesh, in_specs=in_specs, out_specs=P("ba", None), check_vma=False)
```

```python
import functools

import jax
import jax.numpy as jnp
from jax import lax
from jax.experimental import pallas as pl
from jax.experimental.pallas import tpu as pltpu
from jax.sharding import PartitionSpec as P

BF, F32 = jnp.bfloat16, jnp.float32
MESH = pl.DeviceIdType.MESH
JT = 16
CLASSES = (((0, 1), (2, 3), (4,)), ((2, 3), (0,), (1,)))
START = ((0, 1, 2), (2, 0, 1))
ROOM = (2, 2, 1)


def where_am_i():
    aa, ba = lax.axis_index("aa"), lax.axis_index("ba")
    core, z = lax.rem(aa, 2), lax.rem(lax.div(aa, 2), 4)
    x = 2 * lax.div(aa, 8) + lax.rem(ba, 2)
    y = lax.div(ba, 2)
    return aa, ba, x, y, z, core


def place(x, y, z, core):
    aa = 8 * lax.div(x, 2) + 2 * z + core
    ba = 2 * y + lax.rem(x, 2)
    return aa, ba


def masks(step):
    one = step ^ (step >> 2)
    mx, my, mz, mc = (one ^ (step >> 4)) & 3, one & 3, step & 3, (step ^ (step >> 6)) & 1
    return ((mx >> 1) << 3) | (mz << 1) | mc, (my << 1) | (mx & 1)


def total_wait(ref, sem):
    pltpu.make_async_copy(ref, ref, sem).wait()


def kernel(
    field, m1_hbm, m2_hbm, out,
    fbuf, wide, obuf, sbuf, rbuf, m1, m1t, m2, m2buf, m2t, cacc, cc, left, acc, blocks,
    fsem, wsem, send, recv, m2send, m2recv, m2sem, m2ysend, m2yrecv, csend, crecv, gsend, grecv, osend, brecv, wsend, wrecv, *parts,
):
    gs, r1, s1, r2, s2, r3 = (parts[3 * n : 3 * n + 3] for n in range(6))
    aa, ba, x, y, z, core = where_am_i()
    tiles = fbuf.shape[0]
    me = 8 * aa + ba
    sibling = {"aa": aa + 1 - 2 * core, "ba": ba}
    place_in_k = 8 * core + 4 * lax.div(x, 2) + z

    def load(tile, part):
        rows = pl.ds(256 * part, 256)
        return pltpu.make_async_copy(
            field.at[rows, pl.ds(JT * tile, JT), :], fbuf.at[tile, rows], fsem.at[tile, part]
        )

    barrier = pltpu.get_barrier_semaphore()

    def greet(aa_mask, ba_mask):
        pl.semaphore_signal(
            barrier, inc=1, device_id={"aa": aa ^ aa_mask, "ba": ba ^ ba_mask}, device_id_type=MESH
        )

    for ba_mask in range(1, 8):
        greet(0, ba_mask)

    @pl.loop(1, 16)
    def _(aa_mask):
        for ba_mask in range(8):
            greet(aa_mask, ba_mask)

    load_m1 = pltpu.make_async_copy(m1_hbm, m1, wsem.at[0])
    load_m2 = pltpu.make_async_copy(m2_hbm, m2, wsem.at[1])
    load_m1.start()
    for part in range(4):
        load(0, part).start()
    load_m2.start()

    for tile in range(1, tiles):
        for part in range(4):
            load(tile, part).start()

    load_m1.wait()
    m1t[...] = m1[...].T

    def send_rows(tile, first, count, sem):
        rows = pl.ds(pl.multiple_of(JT * place_in_k, JT), JT)

        def block(to):
            mine = sbuf.at[tile, pl.ds(2 * to + first, count)]
            return mine, rbuf.at[tile, pl.ds(first, count), ba, rows, :]

        def start(step):
            aa_mask, ba_mask = masks(step)
            to = me ^ ((aa_mask << 3) | ba_mask)
            mine, there = block(to)
            pltpu.make_async_remote_copy(
                mine, there, send, sem, device_id={"aa": to >> 3, "ba": to & 7}, device_id_type=MESH
            ).start()

        for step in range(1, 8):
            start(step)
        pl.loop(1, 16)(lambda turn: [start(8 * turn + step) for step in range(8)] and None)

        mine, there = block(me)
        pltpu.make_async_copy(mine, there, sem).start()

    parity = lax.rem(y, 2)

    def trade_m2(n):
        gathered = m2buf.at[parity + 2 * n, pl.ds(8 * core, 8)]
        to_aa, to_ba = place(x, y ^ (1 + 2 * n), z, core)
        return pltpu.make_async_remote_copy(
            gathered, gathered, m2ysend.at[n], m2yrecv.at[n],
            device_id={"aa": to_aa, "ba": to_ba}, device_id_type=MESH,
        )

    @pl.loop(0, tiles)
    def _(tile):
        @pl.loop(0, 4)
        def _(part):
            load(tile, part).wait()

            @pl.loop(0, 32, unroll=4)
            def _(group):
                at = 256 * part + 8 * group
                wide[pl.ds(pl.multiple_of(JT * at, 128), 128), :] = (
                    fbuf[tile, pl.ds(at, 8)].reshape(128, 128).astype(F32)
                )

        @pl.loop(0, JT // 2)
        def _(pair):
            both = jnp.concatenate(
                [wide[pl.ds(2 * pair + n, 1024, stride=JT), :] for n in range(2)], axis=1
            ).astype(BF)
            got = jnp.dot(m1t[...], both, preferred_element_type=F32)
            for n in range(2):
                obuf[pl.ds(pl.multiple_of(512 * pair + 256 * n, 256), 256), :] = got[:, 128 * n : 128 * n + 128]

        @pl.loop(0, 256, unroll=8)
        def _(r):
            sbuf[tile, r] = obuf[pl.ds(r, JT, stride=256), :].astype(BF)

        @pl.when(tile == 0)
        def _():
            pl.semaphore_wait(barrier, 127)

        @pl.when(tile < 3)
        def _():
            send_rows(tile, 0, 2, recv.at[tile])

        @pl.when(tile == 3)
        def _():
            for half in range(2):
                send_rows(tile, half, 1, recv.at[3 + half])

        @pl.when(tile == 0)
        def _():
            load_m2.wait()
            for mask in range(1, 8):
                to_aa, to_ba = place(x ^ (2 * (mask // 4)), y, z ^ (mask % 4), core)
                for n in range(2):
                    pltpu.make_async_remote_copy(
                        m2.at[parity + 2 * n], m2buf.at[parity + 2 * n, place_in_k], m2send, m2recv,
                        device_id={"aa": to_aa, "ba": to_ba}, device_id_type=MESH,
                    ).start()
            for n in range(2):
                pltpu.make_async_copy(
                    m2.at[parity + 2 * n], m2buf.at[parity + 2 * n, place_in_k], m2recv
                ).start()

        @pl.when(tile == 2)
        def _():
            total_wait(m2buf.at[pl.ds(0, 2), pl.ds(0, 8)], m2recv)
            for n in range(2):
                trade_m2(n).start()

    for n in range(2):
        trade_m2(n).wait()
    half_of_m2 = m2buf.at[:, pl.ds(8 * core, 8)]
    pass_m2 = pltpu.make_async_remote_copy(
        half_of_m2, half_of_m2, m2sem.at[0], m2sem.at[1], device_id=sibling, device_id_type=MESH
    )
    pass_m2.start()
    pass_m2.wait()
    for tile in range(4):
        m2t[tile] = m2buf[tile].reshape(256, 256).T

    def share(half, pair):
        blocks = pl.ds(2 * pair, 2)
        return pltpu.make_async_remote_copy(
            cc.at[blocks, pl.ds(256 * half, 256), :], cc.at[blocks, pl.ds(512 + 256 * half, 256), :],
            csend.at[half, pair], crecv.at[half, pair], device_id=sibling, device_id_type=MESH,
        )

    for tile in range(4):
        if tile < 3:
            total_wait(rbuf.at[tile], recv.at[tile])
        for half in range(2):
            if tile == 3:
                total_wait(rbuf.at[tile, half], recv.at[3 + half])

            @pl.loop(0, 4, unroll=2)
            def _(pair):
                both = jnp.concatenate([rbuf[tile, half, 2 * pair], rbuf[tile, half, 2 * pair + 1]], axis=1)
                got = jnp.dot(m2t[tile], both, preferred_element_type=F32)
                if tile > 0:
                    got += cacc[half, pair]
                if tile < 3:
                    cacc[half, pair] = got
                else:
                    cc[2 * pair, pl.ds(256 * half, 256), :] = got[:, :128].astype(BF)
                    cc[2 * pair + 1, pl.ds(256 * half, 256), :] = got[:, 128:].astype(BF)
                    share(half, pair).start()

    where = (x, y, z)
    sums, got_from = (gs, s1, s2), (r1, r2, r3)
    own_k, their_k = pl.ds(0, 512), pl.ds(512, 512)
    rows = [(low_y, low_x) for low_y in range(2) for low_x in range(2)]

    def row_of(low_y, low_x):
        return 4 * core + 2 * low_y + low_x

    def on_core(which):
        return lambda body: pl.when(core == which)(lambda: body(which))

    def term(rows_of_k, left, block_row, columns):
        right = jnp.concatenate([cc[lax.rem(block_row + d, 8), rows_of_k, :] for d in columns], axis=1)
        return jnp.dot(left, right, preferred_element_type=F32)

    def pieces(which, got, low_y, low_x, k):
        for octet in range(16):
            owner = (2 * (octet >> 3) + low_x, 2 * (octet & 1) + low_y, (octet >> 1) & 3)
            index = tuple(owner[(START[which][k] + stage) % 3] for stage in range(3))
            for n in range(len(CLASSES[which][k])):
                yield gs[k], index + (n,), got[8 * octet : 8 * octet + 8, 128 * n : 128 * n + 128]

    def filled(which, ref, k):
        before = (slice(None),) * (len(ref.shape) - 3)
        return ref.at[before + (pl.ds(0, len(CLASSES[which][k])),)]

    def own_part(which):
        columns = sum(sorted(CLASSES[which]), ())
        for low_y, low_x in rows:
            block_row = row_of(low_y, low_x)
            got = term(own_k, cc[block_row, own_k, :].T, block_row, columns)
            for k, mine in enumerate(CLASSES[which]):
                part = got[:, 128 * mine[0] : 128 * mine[-1] + 128]
                for ref, index, value in pieces(which, part, low_y, low_x, k):
                    ref[index] = value

    def scatter(which, k, stage):
        axis = (START[which][k] + stage) % 3
        for mask in range(1, 4):
            there = [x, y, z]
            there[axis] = there[axis] ^ mask
            to_aa, to_ba = place(*there, core)
            pltpu.make_async_remote_copy(
                filled(which, sums[stage][k], k).at[where[axis] ^ mask],
                filled(which, got_from[stage][k], k).at[mask - 1], gsend, grecv.at[k, stage],
                device_id={"aa": to_aa, "ba": to_ba}, device_id_type=MESH,
            ).start()

    def gathered(which, k, stage):
        total_wait(filled(which, got_from[stage][k], k), grecv.at[k, stage])
        got = filled(which, got_from[stage][k], k)
        own = filled(which, sums[stage][k], k)[where[(START[which][k] + stage) % 3]]
        return own + got[0] + got[1] + got[2]

    def sum_up(which):
        for k, columns in enumerate(CLASSES[which]):
            for low_y, low_x in rows:
                got = term(their_k, left[2 * low_y + low_x], row_of(low_y, low_x), columns)
                for ref, index, value in pieces(which, got, low_y, low_x, k):
                    ref[index] += value
            scatter(which, k, 0)
        for stage in range(2):
            for k in range(3):
                filled(which, sums[stage + 1][k], k)[...] = gathered(which, k, stage)
                scatter(which, k, stage + 1)
        for k, columns in enumerate(CLASSES[which]):
            acc[pl.ds(columns[0], len(columns))] = gathered(which, k, 2) * (1.0 / 65536.0)

    mine = 4 * core + 2 * lax.rem(y, 2) + lax.rem(x, 2)
    taker = lax.div(x, 2)
    own = pl.ds(pl.multiple_of(8 * (8 * taker + 2 * z + lax.div(y, 2)), 8), 8)
    inside = jnp.logical_and(mine == ba, taker == core)
    across = jnp.logical_and(mine + 4 == ba, taker == core)

    def spread(which):
        count = 5 - which

        @pl.loop(0, 8)
        def _(step):
            to_aa = (aa ^ (2 * step) ^ core) | taker
            self = jnp.logical_and(inside, step == 0)
            source, target = acc.at[pl.ds(0, count)], blocks.at[pl.ds(0, count), own, :]

            @pl.when(self)
            def _():
                pltpu.make_async_copy(source, target, brecv).start()

            @pl.when(jnp.logical_not(self))
            def _():
                pltpu.make_async_remote_copy(
                    source, target, osend, brecv, device_id={"aa": to_aa, "ba": mine}, device_id_type=MESH
                ).start()

            for d in range(1, 4):
                pltpu.make_async_remote_copy(
                    acc.at[d], blocks.at[4 + d, own, :], osend, brecv,
                    device_id={"aa": to_aa, "ba": lax.rem(mine + d, 8)}, device_id_type=MESH,
                ).start()

            if which == 0:
                self = jnp.logical_and(across, step == 0)

                @pl.when(self)
                def _():
                    pltpu.make_async_copy(acc.at[4], blocks.at[4, own, :], brecv).start()

                @pl.when(jnp.logical_not(self))
                def _():
                    pltpu.make_async_remote_copy(
                        acc.at[4], blocks.at[4, own, :], osend, brecv,
                        device_id={"aa": to_aa, "ba": mine + 4}, device_id_type=MESH,
                    ).start()

    for which in range(2):
        on_core(which)(own_part)
    for half in range(2):
        for pair in range(4):
            share(half, pair).wait()
    for low_y, low_x in rows:
        left[2 * low_y + low_x] = cc[row_of(low_y, low_x), their_k, :].T
    for which in range(2):
        on_core(which)(sum_up)
    for which in range(2):
        on_core(which)(spread)

    half = blocks.at[:, pl.ds(pl.multiple_of(64 * core, 64), 64), :]
    total_wait(half, brecv)
    swap = pltpu.make_async_remote_copy(
        half, half, wsend, wrecv, device_id=sibling, device_id_type=MESH
    )
    swap.start()
    swap.wait()

    def put(d, value):
        out[:, pl.ds(pl.multiple_of(128 * lax.rem(ba + d, 8), 128), 128)] = value

    for d in range(4):
        put(d, blocks[d])
    for d in range(1, 4):
        put(8 - d, blocks[4 + d].T)

    @pl.when(ba < 4)
    def _():
        put(4, blocks[4])

    @pl.when(ba >= 4)
    def _():
        put(4, blocks[4].T)

    total_wait(sbuf.at[:, pl.ds(0, 254)], send)
    total_wait(m2buf.at[pl.ds(0, 2), pl.ds(0, 7)], m2send)

    def sent(which):
        for stage in range(3):
            for k in range(3):
                total_wait(filled(which, got_from[stage][k], k), gsend)
        count = 5 - which
        total_wait(blocks.at[pl.ds(0, 3), pl.ds(0, 64), :], osend)
        total_wait(blocks.at[pl.ds(0, count), pl.ds(0, 56), :], osend)

        @pl.when(jnp.logical_not(inside))
        def _():
            total_wait(blocks.at[pl.ds(0, count), pl.ds(0, 8), :], osend)

        if which == 0:
            total_wait(blocks.at[pl.ds(0, 1), pl.ds(0, 56), :], osend)

            @pl.when(jnp.logical_not(across))
            def _():
                total_wait(blocks.at[pl.ds(0, 1), pl.ds(0, 8), :], osend)

    for which in range(2):
        on_core(which)(sent)


def shards(field, mode_one, mode_two):
    dma = pltpu.SemaphoreType.DMA
    hbm = pl.BlockSpec(memory_space=pltpu.HBM)
    return pl.pallas_call(
        kernel,
        out_shape=jax.ShapeDtypeStruct((128, 1024), F32),
        in_specs=[hbm, hbm, hbm],
        out_specs=pl.BlockSpec(memory_space=pltpu.VMEM),
        scratch_shapes=[
            pltpu.VMEM((4, 1024, JT, 128), BF),
            pltpu.VMEM((1024 * JT, 128), F32),
            pltpu.VMEM((JT * 256, 128), F32),
            pltpu.VMEM((4, 256, JT, 128), BF),
            pltpu.VMEM((4, 2, 8, 256, 128), BF),
            pltpu.VMEM((1024, 256), BF),
            pltpu.VMEM((256, 1024), BF),
            pltpu.VMEM((4, JT, 256), BF),
            pltpu.VMEM((4, 16, JT, 256), BF),
            pltpu.VMEM((4, 256, 256), BF),
            pltpu.VMEM((2, 4, 256, 256), F32),
            pltpu.VMEM((8, 1024, 128), BF),
            pltpu.VMEM((4, 128, 512), BF),
            pltpu.VMEM((5, 8, 128), F32),
            pltpu.VMEM((8, 128, 128), F32),
            dma((4, 4)), dma((2,)),
            dma, dma((5,)), dma, dma, dma((2,)), dma((2,)), dma((2,)),
            dma((2, 4)), dma((2, 4)),
            dma, dma((3, 3)), dma, dma, dma, dma,
            *[
                pltpu.VMEM(shape + (room, 8, 128), F32)
                for shape in ((4, 4, 4), (3, 4, 4), (4, 4), (3, 4), (4,), (3,))
                for room in ROOM
            ],
        ],
        compiler_params=pltpu.CompilerParams(
            collective_id=0, has_side_effects=True, vmem_limit_bytes=53 * 1024 * 1024
        ),
        cost_estimate=pl.CostEstimate(flops=13_000_000_000, bytes_accessed=18_000_000, transcendentals=0),
    )(field, mode_one, mode_two.reshape(4, JT, 256))


def solution(mesh):
    in_specs = (P(None, "aa", "ba"), P(), P("aa", None))
    return jax.shard_map(shards, mesh=mesh, in_specs=in_specs, out_specs=P("ba", None), check_vma=False)
```

```python
import functools

import jax
import jax.numpy as jnp
from jax import lax
from jax.experimental import pallas as pl
from jax.experimental.pallas import tpu as pltpu
from jax.sharding import PartitionSpec as P

BF, F32 = jnp.bfloat16, jnp.float32
MESH = pl.DeviceIdType.MESH
JT = 16
CLASSES = (((0, 1), (2, 3), (4,)), ((2, 3), (0,), (1,)))
START = ((0, 1, 2), (2, 0, 1))
ROOM = (2, 2, 1)


def where_am_i():
    aa, ba = lax.axis_index("aa"), lax.axis_index("ba")
    core, z = lax.rem(aa, 2), lax.rem(lax.div(aa, 2), 4)
    x = 2 * lax.div(aa, 8) + lax.rem(ba, 2)
    y = lax.div(ba, 2)
    return aa, ba, x, y, z, core


def place(x, y, z, core):
    aa = 8 * lax.div(x, 2) + 2 * z + core
    ba = 2 * y + lax.rem(x, 2)
    return aa, ba


def masks(step):
    one = step ^ (step >> 2)
    mx, my, mz, mc = (one ^ (step >> 4)) & 3, one & 3, step & 3, (step ^ (step >> 6)) & 1
    return ((mx >> 1) << 3) | (mz << 1) | mc, (my << 1) | (mx & 1)


def total_wait(ref, sem):
    pltpu.make_async_copy(ref, ref, sem).wait()


def kernel(
    field, m1_hbm, m2_hbm, out,
    fbuf, wide, obuf, sbuf, rbuf, m1, m1t, m2, m2buf, m2t, cacc, cc, left, acc, blocks,
    fsem, wsem, send, recv, m2send, m2recv, m2sem, m2ysend, m2yrecv, csend, crecv, gsend, grecv, osend, brecv, wsend, wrecv, *parts,
):
    gs, r1, s1, r2, s2, r3 = (parts[3 * n : 3 * n + 3] for n in range(6))
    aa, ba, x, y, z, core = where_am_i()
    tiles = fbuf.shape[0]
    me = 8 * aa + ba
    sibling = {"aa": aa + 1 - 2 * core, "ba": ba}
    place_in_k = 8 * core + 4 * lax.div(x, 2) + z

    def load(tile, part):
        rows = pl.ds(256 * part, 256)
        return pltpu.make_async_copy(
            field.at[rows, pl.ds(JT * tile, JT), :], fbuf.at[tile, rows], fsem.at[tile, part]
        )

    barrier = pltpu.get_barrier_semaphore()

    def greet(aa_mask, ba_mask):
        pl.semaphore_signal(
            barrier, inc=1, device_id={"aa": aa ^ aa_mask, "ba": ba ^ ba_mask}, device_id_type=MESH
        )

    for ba_mask in range(1, 8):
        greet(0, ba_mask)

    @pl.loop(1, 16)
    def _(aa_mask):
        for ba_mask in range(8):
            greet(aa_mask, ba_mask)

    load_m1 = pltpu.make_async_copy(m1_hbm, m1, wsem.at[0])
    load_m2 = pltpu.make_async_copy(m2_hbm, m2, wsem.at[1])
    load_m1.start()
    for part in range(4):
        load(0, part).start()
    load_m2.start()

    for tile in range(1, tiles):
        for part in range(4):
            load(tile, part).start()

    load_m1.wait()
    m1t[...] = m1[...].T

    def send_rows(tile, first, count, sem):
        rows = pl.ds(pl.multiple_of(JT * place_in_k, JT), JT)

        def block(to):
            mine = sbuf.at[tile, pl.ds(2 * to + first, count)]
            return mine, rbuf.at[tile, pl.ds(first, count), ba, rows, :]

        def start(step):
            aa_mask, ba_mask = masks(step)
            to = me ^ ((aa_mask << 3) | ba_mask)
            mine, there = block(to)
            pltpu.make_async_remote_copy(
                mine, there, send, sem, device_id={"aa": to >> 3, "ba": to & 7}, device_id_type=MESH
            ).start()

        for step in range(1, 8):
            start(step)
        pl.loop(1, 16)(lambda turn: [start(8 * turn + step) for step in range(8)] and None)

        mine, there = block(me)
        pltpu.make_async_copy(mine, there, sem).start()

    parity = lax.rem(y, 2)

    def trade_m2(n):
        gathered = m2buf.at[parity + 2 * n, pl.ds(8 * core, 8)]
        to_aa, to_ba = place(x, y ^ (1 + 2 * n), z, core)
        return pltpu.make_async_remote_copy(
            gathered, gathered, m2ysend.at[n], m2yrecv.at[n],
            device_id={"aa": to_aa, "ba": to_ba}, device_id_type=MESH,
        )

    @pl.loop(0, tiles)
    def _(tile):
        @pl.loop(0, 4)
        def _(part):
            load(tile, part).wait()

            @pl.loop(0, 32, unroll=4)
            def _(group):
                at = 256 * part + 8 * group
                wide[pl.ds(pl.multiple_of(JT * at, 128), 128), :] = (
                    fbuf[tile, pl.ds(at, 8)].reshape(128, 128).astype(F32)
                )

        @pl.loop(0, JT // 2)
        def _(pair):
            both = jnp.concatenate(
                [wide[pl.ds(2 * pair + n, 1024, stride=JT), :] for n in range(2)], axis=1
            ).astype(BF)
            got = jnp.dot(m1t[...], both, preferred_element_type=F32)
            for n in range(2):
                obuf[pl.ds(pl.multiple_of(512 * pair + 256 * n, 256), 256), :] = got[:, 128 * n : 128 * n + 128]

        @pl.loop(0, 256, unroll=8)
        def _(r):
            sbuf[tile, r] = obuf[pl.ds(r, JT, stride=256), :].astype(BF)

        @pl.when(tile == 0)
        def _():
            pl.semaphore_wait(barrier, 127)

        @pl.when(tile < 3)
        def _():
            send_rows(tile, 0, 2, recv.at[tile])

        @pl.when(tile == 3)
        def _():
            for half in range(2):
                send_rows(tile, half, 1, recv.at[3 + half])

        @pl.when(tile == 0)
        def _():
            load_m2.wait()
            for mask in range(1, 8):
                to_aa, to_ba = place(x ^ (2 * (mask // 4)), y, z ^ (mask % 4), core)
                for n in range(2):
                    pltpu.make_async_remote_copy(
                        m2.at[parity + 2 * n], m2buf.at[parity + 2 * n, place_in_k], m2send, m2recv,
                        device_id={"aa": to_aa, "ba": to_ba}, device_id_type=MESH,
                    ).start()
            for n in range(2):
                pltpu.make_async_copy(
                    m2.at[parity + 2 * n], m2buf.at[parity + 2 * n, place_in_k], m2recv
                ).start()

        @pl.when(tile == 2)
        def _():
            total_wait(m2buf.at[pl.ds(0, 2), pl.ds(0, 8)], m2recv)
            for n in range(2):
                trade_m2(n).start()

    for n in range(2):
        trade_m2(n).wait()
    half_of_m2 = m2buf.at[:, pl.ds(8 * core, 8)]
    pass_m2 = pltpu.make_async_remote_copy(
        half_of_m2, half_of_m2, m2sem.at[0], m2sem.at[1], device_id=sibling, device_id_type=MESH
    )
    pass_m2.start()
    pass_m2.wait()
    for tile in range(4):
        m2t[tile] = m2buf[tile].reshape(256, 256).T

    def share(half, pair):
        blocks = pl.ds(2 * pair, 2)
        return pltpu.make_async_remote_copy(
            cc.at[blocks, pl.ds(256 * half, 256), :], cc.at[blocks, pl.ds(512 + 256 * half, 256), :],
            csend.at[half, pair], crecv.at[half, pair], device_id=sibling, device_id_type=MESH,
        )

    for tile in range(4):
        if tile < 3:
            total_wait(rbuf.at[tile], recv.at[tile])
        for half in range(2):
            if tile == 3:
                total_wait(rbuf.at[tile, half], recv.at[3 + half])

            @pl.loop(0, 4, unroll=2)
            def _(pair):
                both = jnp.concatenate([rbuf[tile, half, 2 * pair], rbuf[tile, half, 2 * pair + 1]], axis=1)
                got = jnp.dot(m2t[tile], both, preferred_element_type=F32)
                if tile > 0:
                    got += cacc[half, pair]
                if tile < 3:
                    cacc[half, pair] = got
                else:
                    cc[2 * pair, pl.ds(256 * half, 256), :] = got[:, :128].astype(BF)
                    cc[2 * pair + 1, pl.ds(256 * half, 256), :] = got[:, 128:].astype(BF)
                    share(half, pair).start()

    where = (x, y, z)
    sums, got_from = (gs, s1, s2), (r1, r2, r3)
    early_k, late_k = pl.ds(0, 768), pl.ds(768, 256)
    rows = [(low_y, low_x) for low_y in range(2) for low_x in range(2)]

    def row_of(low_y, low_x):
        return 4 * core + 2 * low_y + low_x

    def on_core(which):
        return lambda body: pl.when(core == which)(lambda: body(which))

    def term(rows_of_k, left, block_row, columns):
        right = jnp.concatenate([cc[lax.rem(block_row + d, 8), rows_of_k, :] for d in columns], axis=1)
        return jnp.dot(left, right, preferred_element_type=F32)

    def pieces(which, got, low_y, low_x, k):
        for octet in range(16):
            owner = (2 * (octet >> 3) + low_x, 2 * (octet & 1) + low_y, (octet >> 1) & 3)
            index = tuple(owner[(START[which][k] + stage) % 3] for stage in range(3))
            for n in range(len(CLASSES[which][k])):
                yield gs[k], index + (n,), got[8 * octet : 8 * octet + 8, 128 * n : 128 * n + 128]

    def filled(which, ref, k):
        before = (slice(None),) * (len(ref.shape) - 3)
        return ref.at[before + (pl.ds(0, len(CLASSES[which][k])),)]

    def own_part(which):
        columns = sum(sorted(CLASSES[which]), ())
        for low_y, low_x in rows:
            block_row = row_of(low_y, low_x)
            got = term(early_k, cc[block_row, early_k, :].T, block_row, columns)
            for k, mine in enumerate(CLASSES[which]):
                part = got[:, 128 * mine[0] : 128 * mine[-1] + 128]
                for ref, index, value in pieces(which, part, low_y, low_x, k):
                    ref[index] = value

    def scatter(which, k, stage):
        axis = (START[which][k] + stage) % 3
        for mask in range(1, 4):
            there = [x, y, z]
            there[axis] = there[axis] ^ mask
            to_aa, to_ba = place(*there, core)
            pltpu.make_async_remote_copy(
                filled(which, sums[stage][k], k).at[where[axis] ^ mask],
                filled(which, got_from[stage][k], k).at[mask - 1], gsend, grecv.at[k, stage],
                device_id={"aa": to_aa, "ba": to_ba}, device_id_type=MESH,
            ).start()

    def gathered(which, k, stage):
        total_wait(filled(which, got_from[stage][k], k), grecv.at[k, stage])
        got = filled(which, got_from[stage][k], k)
        own = filled(which, sums[stage][k], k)[where[(START[which][k] + stage) % 3]]
        return own + got[0] + got[1] + got[2]

    def sum_up(which):
        for k, columns in enumerate(CLASSES[which]):
            for low_y, low_x in rows:
                got = term(late_k, left[2 * low_y + low_x], row_of(low_y, low_x), columns)
                for ref, index, value in pieces(which, got, low_y, low_x, k):
                    ref[index] += value
            scatter(which, k, 0)
        for stage in range(2):
            for k in range(3):
                filled(which, sums[stage + 1][k], k)[...] = gathered(which, k, stage)
                scatter(which, k, stage + 1)
        for k, columns in enumerate(CLASSES[which]):
            acc[pl.ds(columns[0], len(columns))] = gathered(which, k, 2) * (1.0 / 65536.0)

    mine = 4 * core + 2 * lax.rem(y, 2) + lax.rem(x, 2)
    taker = lax.div(x, 2)
    own = pl.ds(pl.multiple_of(8 * (8 * taker + 2 * z + lax.div(y, 2)), 8), 8)
    inside = jnp.logical_and(mine == ba, taker == core)
    across = jnp.logical_and(mine + 4 == ba, taker == core)

    def spread(which):
        count = 5 - which

        @pl.loop(0, 8)
        def _(step):
            to_aa = (aa ^ (2 * step) ^ core) | taker
            self = jnp.logical_and(inside, step == 0)
            source, target = acc.at[pl.ds(0, count)], blocks.at[pl.ds(0, count), own, :]

            @pl.when(self)
            def _():
                pltpu.make_async_copy(source, target, brecv).start()

            @pl.when(jnp.logical_not(self))
            def _():
                pltpu.make_async_remote_copy(
                    source, target, osend, brecv, device_id={"aa": to_aa, "ba": mine}, device_id_type=MESH
                ).start()

            for d in range(1, 4):
                pltpu.make_async_remote_copy(
                    acc.at[d], blocks.at[4 + d, own, :], osend, brecv,
                    device_id={"aa": to_aa, "ba": lax.rem(mine + d, 8)}, device_id_type=MESH,
                ).start()

            if which == 0:
                self = jnp.logical_and(across, step == 0)

                @pl.when(self)
                def _():
                    pltpu.make_async_copy(acc.at[4], blocks.at[4, own, :], brecv).start()

                @pl.when(jnp.logical_not(self))
                def _():
                    pltpu.make_async_remote_copy(
                        acc.at[4], blocks.at[4, own, :], osend, brecv,
                        device_id={"aa": to_aa, "ba": mine + 4}, device_id_type=MESH,
                    ).start()

    for pair in range(4):
        share(0, pair).wait()
    for which in range(2):
        on_core(which)(own_part)
    for pair in range(4):
        share(1, pair).wait()
    for low_y, low_x in rows:
        left[2 * low_y + low_x] = cc[row_of(low_y, low_x), late_k, :].T
    for which in range(2):
        on_core(which)(sum_up)
    for which in range(2):
        on_core(which)(spread)

    half = blocks.at[:, pl.ds(pl.multiple_of(64 * core, 64), 64), :]
    total_wait(half, brecv)
    swap = pltpu.make_async_remote_copy(
        half, half, wsend, wrecv, device_id=sibling, device_id_type=MESH
    )
    swap.start()
    swap.wait()

    def put(d, value):
        out[:, pl.ds(pl.multiple_of(128 * lax.rem(ba + d, 8), 128), 128)] = value

    for d in range(4):
        put(d, blocks[d])
    for d in range(1, 4):
        put(8 - d, blocks[4 + d].T)

    @pl.when(ba < 4)
    def _():
        put(4, blocks[4])

    @pl.when(ba >= 4)
    def _():
        put(4, blocks[4].T)

    total_wait(sbuf.at[:, pl.ds(0, 254)], send)
    total_wait(m2buf.at[pl.ds(0, 2), pl.ds(0, 7)], m2send)

    def sent(which):
        for stage in range(3):
            for k in range(3):
                total_wait(filled(which, got_from[stage][k], k), gsend)
        count = 5 - which
        total_wait(blocks.at[pl.ds(0, 3), pl.ds(0, 64), :], osend)
        total_wait(blocks.at[pl.ds(0, count), pl.ds(0, 56), :], osend)

        @pl.when(jnp.logical_not(inside))
        def _():
            total_wait(blocks.at[pl.ds(0, count), pl.ds(0, 8), :], osend)

        if which == 0:
            total_wait(blocks.at[pl.ds(0, 1), pl.ds(0, 56), :], osend)

            @pl.when(jnp.logical_not(across))
            def _():
                total_wait(blocks.at[pl.ds(0, 1), pl.ds(0, 8), :], osend)

    for which in range(2):
        on_core(which)(sent)


def shards(field, mode_one, mode_two):
    dma = pltpu.SemaphoreType.DMA
    hbm = pl.BlockSpec(memory_space=pltpu.HBM)
    return pl.pallas_call(
        kernel,
        out_shape=jax.ShapeDtypeStruct((128, 1024), F32),
        in_specs=[hbm, hbm, hbm],
        out_specs=pl.BlockSpec(memory_space=pltpu.VMEM),
        scratch_shapes=[
            pltpu.VMEM((4, 1024, JT, 128), BF),
            pltpu.VMEM((1024 * JT, 128), F32),
            pltpu.VMEM((JT * 256, 128), F32),
            pltpu.VMEM((4, 256, JT, 128), BF),
            pltpu.VMEM((4, 2, 8, 256, 128), BF),
            pltpu.VMEM((1024, 256), BF),
            pltpu.VMEM((256, 1024), BF),
            pltpu.VMEM((4, JT, 256), BF),
            pltpu.VMEM((4, 16, JT, 256), BF),
            pltpu.VMEM((4, 256, 256), BF),
            pltpu.VMEM((2, 4, 256, 256), F32),
            pltpu.VMEM((8, 1024, 128), BF),
            pltpu.VMEM((4, 128, 256), BF),
            pltpu.VMEM((5, 8, 128), F32),
            pltpu.VMEM((8, 128, 128), F32),
            dma((4, 4)), dma((2,)),
            dma, dma((5,)), dma, dma, dma((2,)), dma((2,)), dma((2,)),
            dma((2, 4)), dma((2, 4)),
            dma, dma((3, 3)), dma, dma, dma, dma,
            *[
                pltpu.VMEM(shape + (room, 8, 128), F32)
                for shape in ((4, 4, 4), (3, 4, 4), (4, 4), (3, 4), (4,), (3,))
                for room in ROOM
            ],
        ],
        compiler_params=pltpu.CompilerParams(
            collective_id=0, has_side_effects=True, vmem_limit_bytes=53 * 1024 * 1024
        ),
        cost_estimate=pl.CostEstimate(flops=13_000_000_000, bytes_accessed=18_000_000, transcendentals=0),
    )(field, mode_one, mode_two.reshape(4, JT, 256))


def solution(mesh):
    in_specs = (P(None, "aa", "ba"), P(), P("aa", None))
    return jax.shard_map(shards, mesh=mesh, in_specs=in_specs, out_specs=P("ba", None), check_vma=False)
```
